256 devices in a mesh: dp: 4 (over x), head: 2 (over y_hi), ctx: 32 (over z, y_lo, core).
Axes of the slice: x: 4, y: 4 (y_hi: 2, y_lo: 2; y = y_hi * 2 + y_lo), z: 8, core: 2. Of those that a mesh axis runs over, the one named last changes fastest.
Arguments:
- q_latent: bfloat16 [4, 64, 1536], P('dp'), may hold values from -6 to 6
- hidden: bfloat16 [4, 64, 7168], P('dp'), may hold values from -96 to 96
- main_queries: bfloat16 [4, 64, 128, 576], P('dp', 'ctx', 'head'), may hold values from -36 to 36
- main_keys: bfloat16 [4, 32768, 576], P('dp', 'ctx'), may hold values from -6 to 6
- index_keys: bfloat16 [4, 32768, 128], P('dp', 'ctx'), may hold values from -96 to 96
- positions: int32 [4, 64], P('dp'), may hold values from 16384 to 32767, as said below
- w_query: bfloat16 [1536, 8192], P('ctx', 'head'), may hold values from -0.15625 to 0.15625
- w_weights: bfloat16 [7168, 64], P('ctx', 'head'), may hold values from -0.0625 to 0.0625
Outputs:
- grad_query: float32 [1536, 8192], P('ctx', 'head')
- grad_weights: float32 [7168, 64], P('ctx', 'head')
- cross_entropy: float32 [4, 64], P('dp')
The draws below stay inside these ranges and needn't reach their ends.
Inputs may be any that keep to these rules, and one draw needn't show every extreme that they name: `positions`: in each sequence some query sits at the last key and some at the lowest position.
All inputs are finite; a program needn't handle non-finite values.
Results may differ from the reference program's by a relative error of at most 0.0075.
The reference program's roundings to bfloat16 on the way (of `index_query`, `score_grad`, `query_grad` and `weight_grad`) count: a program that leaves them out, or rounds other values in their place, can miss the bound.
Values may be sent and summed in bfloat16 or wider, within the bound.
A program may use at most 128 MiB of HBM per device.

```python
import jax
import jax.numpy as jnp
from jax import lax

D = 7168
DQ = 1536
HI = 64
DI = 128
HM = 128
DL = 576
Q = 64
CONTEXT = 32768
SEQS = 4


def draw_main_keys(key, part):
    key = jax.random.fold_in(key, 11)
    values = jnp.clip(jax.random.normal(key, (SEQS, CONTEXT, DL), jnp.float32), -6.0, 6.0)
    return values.astype(jnp.bfloat16)


def draw_main_queries(key, part):
    key = jax.random.fold_in(key, 12)
    values = 4.0 * jnp.clip(jax.random.normal(key, (SEQS, Q, HM, DL), jnp.float32), -9.0, 9.0)
    return values.astype(jnp.bfloat16)


def draw_index_keys(key, part):
    key = jax.random.fold_in(key, 13)
    value_key = jax.random.fold_in(key, 2)
    values = jnp.clip(jax.random.normal(value_key, (SEQS, CONTEXT, DI), jnp.float32), -6.0, 6.0)
    return values.astype(jnp.bfloat16)


def draw_hidden(key, part):
    key = jax.random.fold_in(key, 14)
    value_key = jax.random.fold_in(key, 0)
    values = jnp.clip(jax.random.normal(value_key, (SEQS, Q, D), jnp.float32), -6.0, 6.0)
    return values.astype(jnp.bfloat16)


def draw_positions(key, part):
    key = jax.random.fold_in(key, 15)
    offset_key, row_key = jax.random.split(key)
    offsets = jax.random.randint(offset_key, (SEQS, Q), 0, CONTEXT // 2, jnp.int32)
    row_keys = jax.random.split(row_key, SEQS)
    picked = jax.vmap(lambda one: jax.random.permutation(one, Q)[:2])(row_keys)
    columns = jnp.arange(Q, dtype=jnp.int32)[None, :]
    offsets = jnp.where(columns == picked[:, 0:1], 0, offsets)
    offsets = jnp.where(columns == picked[:, 1:2], CONTEXT // 2 - 1, offsets)
    return (CONTEXT - 1 - offsets).astype(jnp.int32)


def block_scale(rng, shape, cuts, least, top_value):
    def one(axis_at, shards_of):
        steps = jax.random.uniform(jax.random.fold_in(jax.random.fold_in(rng, 6), axis_at), (shards_of,), jnp.float32, least / len(cuts), top_value / len(cuts))
        return jnp.repeat(jnp.exp(steps), shape[axis_at] // shards_of).reshape((-1,) + (1,) * (len(shape) - axis_at - 1))

    level = one(*cuts[0])
    for cut in cuts[1:]:
        level = level * one(*cut)
    return level


def scatter_about(key, dims, width, most, cuts=(), held_as=jnp.bfloat16):
    result = width * jax.random.normal(key, dims, jnp.float32)
    if cuts:
        result = result * block_scale(key, dims, cuts, -0.22, 0.18)
    return jnp.clip(result, -most, most).astype(held_as)


def setup_inputs(seed: int = 0) -> dict:
    seeds = jax.random.split(jax.random.key(seed), 9)
    return {
        "q_latent": scatter_about(seeds[0], (SEQS, Q, DQ), 1.0, 6.0, ((0, 4),)),
        "hidden": draw_hidden(jax.random.fold_in(seeds[8], 71), 0),
        "main_queries": draw_main_queries(jax.random.fold_in(seeds[8], 71), 0),
        "main_keys": draw_main_keys(jax.random.fold_in(seeds[8], 71), 0),
        "index_keys": draw_index_keys(jax.random.fold_in(seeds[8], 71), 0),
        "positions": draw_positions(jax.random.fold_in(seeds[8], 71), 0),
        "w_query": scatter_about(seeds[6], (DQ, HI * DI), DQ ** -0.5, 0.15625, ((0, 32), (1, 2))),
        "w_weights": scatter_about(seeds[7], (D, HI), D ** -0.5, 0.0625, ((0, 32), (1, 2))),
    }


score_scale = 192.0 ** -0.5
masked_floor = -1e30


def main_target(queries, key_rows, visible):
    key_float = key_rows.astype(jnp.float32)
    blocks = queries.reshape(Q, HM // 8, 8, DL).transpose(1, 0, 2, 3)

    def per_block(block):
        scores = jnp.einsum('qhd,sd->qhs', block.astype(jnp.float32), key_float) * score_scale
        scores = jnp.where(visible[:, None, :], scores, masked_floor)
        row_max = jnp.max(scores, axis=2, keepdims=True)
        shifted = jnp.where(visible[:, None, :], jnp.exp(scores - row_max), 0.0)
        return jnp.sum(shifted / jnp.sum(shifted, axis=2, keepdims=True), axis=1)

    return jnp.sum(lax.map(per_block, blocks), axis=0) / HM


def reference(q_latent, hidden, main_queries, main_keys, index_keys, positions, w_query, w_weights):
    index_scale = (HI * DI) ** -0.5
    grad_query = jnp.zeros((DQ, HI * DI), jnp.float32)
    grad_weights = jnp.zeros((D, HI), jnp.float32)
    losses = []
    for sequence in range(SEQS):
        latent = q_latent[sequence]
        activations = hidden[sequence]
        index_query = jnp.dot(latent, w_query, preferred_element_type=jnp.float32).astype(jnp.bfloat16)
        head_weights = jnp.dot(activations, w_weights, preferred_element_type=jnp.float32)
        visible = jnp.arange(CONTEXT, dtype=jnp.int32)[None, :] <= positions[sequence][:, None]
        key_float = index_keys[sequence].astype(jnp.float32)
        query_blocks = index_query.reshape(Q, HI // 8, 8, DI).transpose(1, 0, 2, 3)
        weight_blocks = head_weights.reshape(Q, HI // 8, 8).transpose(1, 0, 2)

        def add_logits(running, inputs):
            block, weights = inputs
            affinity = jnp.einsum('qjd,sd->qjs', block.astype(jnp.float32), key_float)
            return running + jnp.sum(weights[:, :, None] * jnp.maximum(affinity, 0.0), axis=1) * index_scale, None

        logits, _ = lax.scan(add_logits, jnp.zeros((Q, CONTEXT), jnp.float32), (query_blocks, weight_blocks))
        target = main_target(main_queries[sequence], main_keys[sequence], visible)
        row_max = jnp.max(jnp.where(visible, logits, masked_floor), axis=1, keepdims=True)
        shifted = jnp.where(visible, jnp.exp(logits - row_max), 0.0)
        row_sum = jnp.sum(shifted, axis=1, keepdims=True)
        index_probs = shifted / row_sum
        log_probs = logits - (row_max + jnp.log(row_sum))
        losses.append(-jnp.sum(jnp.where(visible, target * log_probs, 0.0), axis=1))
        delta = jnp.where(visible, index_probs - target, 0.0)

        def per_block(inputs):
            block, weights = inputs
            affinity = jnp.einsum('qjd,sd->qjs', block.astype(jnp.float32), key_float)
            score_grad = jnp.where(affinity > 0, delta[:, None, :] * weights[:, :, None] * index_scale, 0.0).astype(jnp.bfloat16)
            query_grad = jnp.einsum('qjs,sd->qjd', score_grad.astype(jnp.float32), key_float)
            weight_grad = jnp.sum(delta[:, None, :] * jnp.maximum(affinity, 0.0), axis=2) * index_scale
            return query_grad, weight_grad

        query_grad, weight_grad = lax.map(per_block, (query_blocks, weight_blocks))
        query_grad = query_grad.transpose(1, 0, 2, 3).reshape(Q, HI * DI).astype(jnp.bfloat16)
        weight_grad = weight_grad.transpose(1, 0, 2).reshape(Q, HI).astype(jnp.bfloat16)
        grad_query = grad_query + jnp.dot(latent.T, query_grad, preferred_element_type=jnp.float32)
        grad_weights = grad_weights + jnp.dot(activations.T, weight_grad, preferred_element_type=jnp.float32)
    return grad_query, grad_weights, jnp.stack(losses)
```

```python
import jax
import jax.numpy as jnp
from jax import lax
from jax.experimental import pallas as pl
from jax.experimental.pallas import tpu as pltpu
from jax.sharding import PartitionSpec as P

HI = 64
DI = 128
HM = 128
DL = 576
MESH = pl.DeviceIdType.MESH
BF = jnp.bfloat16
F32 = jnp.float32

LOG2E = 1.4426950408889634
LN2 = 0.6931471805599453
C2 = 192.0 ** (-0.5) * LOG2E
ISCALE = (HI * DI) ** (-0.5)
FLOOR = -1e30
LOW = -1e29

NT = (((1,), (1,)), ((), ()))
NN = (((1,), (0,)), ((), ()))


def dot(a, b, dims=NN):
    return lax.dot_general(a, b, dims, preferred_element_type=F32)


def log2(x):
    return jnp.log(x) * LOG2E


def remote(src, dst, ss, rs, dev):
    return pltpu.make_async_remote_copy(
        src_ref=src, dst_ref=dst, send_sem=ss, recv_sem=rs, device_id=dev, device_id_type=MESH
    )


def loop(lo, hi, body):
    def turn(i, carry):
        body(i)
        return carry

    lax.fori_loop(lo, hi, turn, 0)


def kernel(
    pos_s, pos_v, lat8, lat_t, hid, hid_t, mq, mk, ik, wq, ww,
    out_q, out_w, out_l,
    WB, IQL, IQY, IQG, HWL, HWY, HWS, HWG, HB, MQ, K2, IK2, E, MA, LA, MB, LB,
    ST, STG, AFF, LM, T, SG, RSB, RSR, WGP, WGR, DISP, QGA, WGS, WGA, LTX, HTX, OUTP,
    s_w, r_w, s_wx, r_wx, s_iqy, r_iqy, s_iqg, r_iqg, s_hwy, r_hwy, s_hwg, r_hwg,
    s_mp, r_mp, s_ra, r_ra, s_la, r_la, s_rb, r_rb, s_lb, r_lb, s_ca, r_ca, s_cb, r_cb,
    s_k, r_k, s_st, r_st, s_rs, r_rs, s_wg, r_wg, s_dq, r_dq, s_dw, r_dw,
    s_lx, r_lx, s_hx, r_hx, s_o, r_o, s_ox, r_ox,
):
    b = lax.axis_index("dp")
    yh = lax.axis_index("head")
    c = lax.axis_index("ctx")
    z = c // 4
    yl = (c // 2) % 2
    core = c % 2
    y = yh * 2 + yl
    u = yl * 2 + core
    g = z * 2 + core
    by = b * 4 + y

    def g_dev(gg):
        return {"dp": b, "head": yh, "ctx": (gg // 2) * 4 + yl * 2 + gg % 2}

    def y_dev(yy):
        return {"dp": b, "head": yy // 2, "ctx": z * 4 + (yy % 2) * 2 + core}

    def x_dev(bb):
        return {"dp": bb, "head": yh, "ctx": c}

    def by_dev(n):
        yy = n % 4
        return {"dp": n // 4, "head": yy // 2, "ctx": z * 4 + (yy % 2) * 2 + core}

    def a_dev(zz, uu):
        return {"dp": b, "head": yh, "ctx": zz * 4 + uu}

    def zm(v):
        return lax.rem(v + 16, 8)

    bar = pltpu.get_barrier_semaphore()

    def hello(dev):
        pl.semaphore_signal(bar, inc=1, device_id=dev, device_id_type=MESH)

    loop(1, 16, lambda d: hello(g_dev(lax.rem(g + d, 16))))
    loop(1, 16, lambda d: hello(by_dev(lax.rem(by + d, 16))))

    def not_self(t, uu):
        return jnp.logical_or(b > 0, jnp.logical_or(t > 0, uu != u))

    def hello_a(i):
        t, uu = i // 4, i % 4

        @pl.when(not_self(t, uu))
        def _():
            hello(a_dev(zm(z - b - 4 * t), uu))
            hello(a_dev(zm(z + b + 4 * t), uu))

    loop(0, 8, hello_a)
    pl.semaphore_wait(bar, jnp.where(b == 0, 44, 46))

    def w_copy(t, uu, slot):
        zd = zm(z - b - 4 * t)
        cols = pl.ds(pl.multiple_of((zd * 4 + uu) * 128, 128), 128)
        return remote(
            wq.at[:, cols], WB.at[b, t, u], s_w.at[t * 4 + uu], r_w.at[t * 4 + slot], a_dev(zd, uu)
        )

    def wx_copy(bb, slot):
        return remote(WB.at[b], WB.at[slot], s_wx.at[bb], r_wx.at[slot], x_dev(bb))

    def iqy_copy(yy, slot):
        return remote(IQL.at[yy], IQY.at[slot], s_iqy.at[yy], r_iqy.at[slot], y_dev(yy))

    def iqg_copy(gg, slot):
        return remote(IQY, IQG.at[slot], s_iqg.at[gg], r_iqg.at[slot], g_dev(gg))

    def hwy_copy(yy, slot):
        return remote(HWL.at[yy], HWY.at[slot], s_hwy.at[yy], r_hwy.at[slot], y_dev(yy))

    def hwg_copy(gg, slot):
        return remote(HWS, HWG.at[slot], s_hwg.at[gg], r_hwg.at[slot], g_dev(gg))

    def st_copy(gg, slot):
        return remote(ST, STG.at[slot], s_st.at[gg], r_st.at[slot], g_dev(gg))

    def rs_copy(gg, slot):
        return remote(RSB.at[gg], RSR.at[slot], s_rs.at[gg], r_rs.at[slot], g_dev(gg))

    def wg_copy(gg, slot):
        return remote(WGP, WGR.at[slot], s_wg.at[gg], r_wg.at[slot], g_dev(gg))

    def dq_copy(n, slot):
        return remote(DISP.at[n % 4], QGA.at[slot], s_dq.at[n], r_dq.at[slot], by_dev(n))

    def dw_copy(n, slot):
        return remote(WGS, WGA.at[slot], s_dw.at[n], r_dw.at[slot], by_dev(n))

    def lx_copy(bb, t, slot):
        return remote(
            lat_t.at[zm(z - bb - 4 * t)], LTX.at[slot, t],
            s_lx.at[bb * 2 + t], r_lx.at[slot * 2 + t], x_dev(bb),
        )

    def hx_copy(bb, slot):
        return remote(hid_t, HTX.at[slot], s_hx.at[bb], r_hx.at[slot], x_dev(bb))

    def o_copy(t, uu, slot):
        zd = zm(z - b - 4 * t)
        cols = pl.ds(pl.multiple_of(c * 128, 128), 128)
        return remote(
            OUTP.at[t, uu], out_q.at[:, cols], s_o.at[t * 4 + uu], r_o.at[t * 4 + slot],
            a_dev(zd, uu),
        )

    def ox_copy(bb, t, slot):
        cols = pl.ds(pl.multiple_of(zm(z + b + 4 * t) * 512, 512), 512)
        return remote(
            out_q.at[:, cols], out_q.at[:, cols],
            s_ox.at[bb * 2 + t], r_ox.at[slot * 2 + t], x_dev(bb),
        )

    def others(n, me, start):
        loop(1, n, lambda d: start(lax.rem(me + d, n)))

    right = {"dp": b, "head": yh, "ctx": zm(z + 1) * 4 + u}
    left = {"dp": b, "head": yh, "ctx": zm(z - 1) * 4 + u}
    twin = {"dp": b, "head": yh, "ctx": z * 4 + yl * 2 + (1 - core)}

    def piece(zz, half):
        return MQ.at[zz * 2 + core, half]

    def ring(kind, k):
        half = yh if kind[1] == "a" else 1 - yh
        zz = zm(z - k) if kind[0] == "r" else zm(z + k)
        ss, rs = {"ra": (s_ra, r_ra), "la": (s_la, r_la), "rb": (s_rb, r_rb), "lb": (s_lb, r_lb)}[kind]
        return remote(
            piece(zz, half), piece(zz, half), ss.at[k], rs.at[k], right if kind[0] == "r" else left
        )

    def to_twin(zz, which):
        half = yh if which == "a" else 1 - yh
        ss, rs = (s_ca, r_ca) if which == "a" else (s_cb, r_cb)
        return remote(piece(zz, half), piece(zz, half), ss.at[zz], rs.at[zz], twin)

    partner = {"dp": b, "head": 1 - yh, "ctx": c}
    mp_copy = remote(mq.at[1 - yh], MQ.at[g, yh], s_mp.at[0], r_mp.at[0], partner)
    up = y_dev(lax.rem(y + 1, 4))
    down = y_dev(lax.rem(y + 3, 4))
    ik_copies = [
        remote(ik.at[0:512], IK2.at[0:512], s_k.at[0], r_k.at[0], up),
        remote(ik.at[512:1024], IK2.at[512:1024], s_k.at[1], r_k.at[1], down),
    ]
    mk_copies = [
        remote(mk.at[0:512], K2.at[0:512], s_k.at[2], r_k.at[2], up),
        remote(mk.at[512:1024], K2.at[512:1024], s_k.at[3], r_k.at[3], down),
    ]

    mp_copy.start()

    def w_start(i):
        t, uu = i // 4, i % 4

        @pl.when(not_self(t, uu))
        def _():
            w_copy(t, uu, u).start()

    loop(0, 8, w_start)
    MQ[g, yh] = mq[yh]
    ring("ra", 0).start()
    ring("la", 0).start()
    to_twin(z, "a").start()
    HWL[...] = dot(hid[...], ww[...]).reshape(4, 16, 128)
    others(4, y, lambda yy: hwy_copy(yy, y).start())
    HWY[y] = HWL[y]
    for one in ik_copies:
        one.start()
    for one in mk_copies:
        one.start()

    @pl.when(b == 0)
    def _():
        WB[0, 0, u] = wq[:, pl.ds(pl.multiple_of(c * 128, 128), 128)]

    for ref in (MA, LA, MB, LB):
        ref[...] = jnp.zeros_like(ref)

    def w_wait(i):
        t, uu = i // 4, i % 4

        @pl.when(not_self(t, uu))
        def _():
            w_copy(t, uu, uu).wait_recv()

    loop(0, 8, w_wait)
    others(4, b, lambda bb: wx_copy(bb, b).start())

    mp_copy.wait_recv()
    ring("rb", 0).start()
    ring("lb", 0).start()
    to_twin(z, "b").start()

    lane = lax.broadcasted_iota(jnp.int32, (128, 128), 1)
    key_row = lax.broadcasted_iota(jnp.int32, (1, 1024), 1)
    c_far = z * 4 + (1 - yl) * 2 + core

    def scores(zz, keys, base, part, m_acc, l_acc):
        q = MQ[pl.ds(zz * 2, 2)].reshape(256, DL)
        s = dot(q, keys[...], NT)
        for i in range(2):
            slot = zz * 2 + i
            vis = key_row + base <= pos_s[slot]
            si = jnp.where(vis, s[i * 128:(i + 1) * 128], FLOOR)
            m = jnp.maximum(jnp.max(si, axis=1, keepdims=True), LOW)
            e = jnp.exp2((si - m) * C2)
            E[part, slot] = e
            here = lane == slot
            m_acc[...] = jnp.where(here, m, m_acc[...])
            l_acc[...] = jnp.where(here, jnp.sum(e, axis=1, keepdims=True), l_acc[...])

    def near(zz):
        to_twin(zz, "a").wait_recv()
        to_twin(zz, "b").wait_recv()
        scores(zz, mk, c * 1024, 0, MA, LA)

    def step(k):
        if k < 4:
            ring("ra", k).wait_recv()
            if k < 3:
                ring("ra", k + 1).start()
            to_twin(zm(z - 1 - k), "a").start()
        if k < 3:
            ring("la", k).wait_recv()
            if k < 2:
                ring("la", k + 1).start()
            to_twin(zm(z + 1 + k), "a").start()
            ring("rb", k).wait_recv()
            if k < 2:
                ring("rb", k + 1).start()
            to_twin(zm(z - 1 - k), "b").start()
        ring("lb", k).wait_recv()
        if k < 3:
            ring("lb", k + 1).start()
        to_twin(zm(z + 1 + k), "b").start()

    step(0)
    near(z)
    others(4, b, lambda bb: wx_copy(bb, bb).wait_recv())
    iq = jnp.zeros((64, 128), F32)
    for bb in range(4):
        for t in range(2):
            iq = iq + dot(lat8[zm(z + bb + 4 * t)], WB[bb, t].reshape(192, 128))
    IQL[...] = iq.astype(BF).reshape(4, 16, 128)
    others(4, y, lambda yy: iqy_copy(yy, y).start())
    IQY[y] = IQL[y]
    others(4, y, lambda yy: hwy_copy(yy, yy).wait_recv())
    HWS[...] = HWY[0] + HWY[1] + HWY[2] + HWY[3]
    others(16, g, lambda gg: hwg_copy(gg, g).start())
    HWG[g] = HWS[...]
    step(1)
    others(4, y, lambda yy: iqy_copy(yy, yy).wait_recv())
    others(16, g, lambda gg: iqg_copy(gg, g).start())
    IQG[g] = IQY[...]
    loop(0, 2, lambda i: near(zm(z - 1 + 2 * i)))
    step(2)
    loop(0, 2, lambda i: near(zm(z - 2 + 4 * i)))
    step(3)
    others(4, b, lambda bb: [lx_copy(bb, t, b).start() for t in range(2)])
    others(4, b, lambda bb: hx_copy(bb, b).start())
    for t in range(2):
        LTX[b, t] = lat_t[zm(z - b - 4 * t)]
    HTX[b] = hid_t[...]
    loop(0, 2, lambda i: near(zm(z - 3 + 6 * i)))
    near(zm(z + 4))

    others(16, g, lambda gg: hwg_copy(gg, gg).wait_recv())
    hw = HWG[0]
    for gg in range(1, 16):
        hw = hw + HWG[gg]
    for gg in range(16):
        for ys in range(4):
            j = (ys // 2) * 32 + (gg // 2) * 4 + (ys % 2) * 2 + gg % 2
            HB[gg * 4 + ys] = jnp.broadcast_to(hw[:, j:j + 1] * ISCALE, (16, 128))
    others(16, g, lambda gg: iqg_copy(gg, gg).wait_recv())
    for one in ik_copies:
        one.wait_recv()
    lane256 = lax.broadcasted_iota(jnp.int32, (16, 256), 1)
    posq = pos_v[...]
    posq = jnp.concatenate([posq, posq], axis=1)

    def index_tile(keys, i, tile, base):
        kt = keys[pl.ds(pl.multiple_of(i * 256, 256), 256), :]
        aff = dot(IQG[...].reshape(1024, 128), kt, NT)
        AFF[tile] = aff
        total = jnp.zeros((16, 256), F32)
        for p in range(64):
            hb = HB[p]
            total = total + jnp.maximum(aff[p * 16:(p + 1) * 16], 0.0) * jnp.concatenate([hb, hb], axis=1)
        vis = lane256 + (base + i * 256) <= posq
        LM[tile] = jnp.where(vis, total * LOG2E, FLOOR)

    loop(0, 4, lambda i: index_tile(ik, i, i, c * 1024))
    loop(0, 4, lambda i: index_tile(IK2, i, i + 4, c_far * 1024))
    lm = LM[...]
    im = jnp.maximum(jnp.max(jnp.max(lm, axis=0), axis=1, keepdims=True), LOW)
    il = jnp.sum(jnp.sum(jnp.exp2(lm - im[None]), axis=0), axis=1, keepdims=True)
    ST[16:32] = jnp.broadcast_to(im + log2(jnp.maximum(il, 1e-37)), (16, 128))

    for one in mk_copies:
        one.wait_recv()
    loop(0, 8, lambda zz: scores(zz, K2, c_far * 1024, 1, MB, LB))
    ma, mb = MA[...], MB[...]
    mx = jnp.maximum(ma, mb)
    ls = LA[...] * jnp.exp2((ma - mx) * C2) + LB[...] * jnp.exp2((mb - mx) * C2)
    ST[0:16] = (mx * C2 + log2(jnp.maximum(ls, 1e-37))).T[0:16]
    others(16, g, lambda gg: st_copy(gg, g).start())
    STG[g] = ST[...]
    others(16, g, lambda gg: st_copy(gg, gg).wait_recv())
    stats = STG[...]
    top = jnp.max(stats, axis=0)
    lse = top + log2(jnp.sum(jnp.exp2(stats - top[None]), axis=0))
    lse_t = jnp.concatenate([lse[0:16], jnp.zeros((112, 128), F32)], axis=0).T
    MA[...] = jnp.exp2(ma * C2 - lse_t) * (1.0 / HM)
    MB[...] = jnp.exp2(mb * C2 - lse_t) * (1.0 / HM)

    def target(slot):
        for part, ref in ((0, MA), (1, MB)):
            w = jnp.sum(jnp.where(lane == slot, ref[...], 0.0), axis=1, keepdims=True)
            row = jnp.sum(E[part, slot] * w, axis=0, keepdims=True)
            for t in range(4):
                T[part * 4 + t, pl.ds(slot, 1), :] = row[:, t * 256:(t + 1) * 256]

    loop(0, 16, target)
    li = lse[16:32]
    li = jnp.concatenate([li, li], axis=1)
    loss = jnp.zeros((16, 1), F32)
    for t in range(8):
        shifted = LM[t] - li
        tt = T[t]
        loss = loss - jnp.sum(tt * shifted, axis=1, keepdims=True) * LN2
        T[t] = jnp.exp2(shifted) - tt

    lane16 = lax.broadcasted_iota(jnp.int32, (16, 128), 1)
    WGP[...] = jnp.where(lane16 == 64, loss, 0.0)

    def back(i):
        for h in range(2):
            zz = zm(z + 4 - 2 * i - h)
            rows = pl.ds(pl.multiple_of(zz * 128, 128), 128)
            hb = HB[pl.ds(zz * 8, 8)]
            hb = jnp.concatenate([hb, hb], axis=2)
            acc = jnp.zeros((8, 16, 128), F32)
            for t in range(8):
                aff = AFF[t, rows, :].reshape(8, 16, 256)
                delta = T[t][None]
                sg = jnp.where(aff > 0.0, delta * hb, 0.0)
                SG[t, h * 128:(h + 1) * 128, :] = sg.reshape(128, 256).astype(BF)
                prod = delta * jnp.maximum(aff, 0.0)
                acc = acc + prod[:, :, 0:128] + prod[:, :, 128:256]
            got = jnp.sum(acc, axis=2, keepdims=True) * ISCALE
            wg = WGP[...]
            for n in range(8):
                cs, ys = n // 4, n % 4
                j = (ys // 2) * 32 + zz * 4 + (ys % 2) * 2 + cs
                wg = jnp.where(lane16 == j, got[n], wg)
            WGP[...] = wg
        total = jnp.zeros((256, 128), F32)
        for t in range(8):
            kt = (ik if t < 4 else IK2)[(t % 4) * 256:(t % 4 + 1) * 256, :]
            total = total + dot(SG[t], kt)
        for h in range(2):
            zz = zm(z + 4 - 2 * i - h)
            RSB[pl.ds(zz * 2, 2)] = total[h * 128:(h + 1) * 128].reshape(2, 4, 16, 128)
            for cs in range(2):
                gg = zz * 2 + cs

                @pl.when(gg != g)
                def _():
                    rs_copy(gg, g).start()

    loop(0, 4, back)
    others(16, g, lambda gg: wg_copy(gg, g).start())
    WGR[g] = WGP[...]
    RSR[g] = RSB[g]
    others(16, g, lambda gg: rs_copy(gg, gg).wait_recv())
    qg = RSR[0]
    for gg in range(1, 16):
        qg = qg + RSR[gg]
    DISP[...] = qg.astype(BF)
    others(16, by, lambda n: dq_copy(n, by).start())
    QGA[by] = DISP[y]
    others(16, g, lambda gg: wg_copy(gg, gg).wait_recv())
    wg = WGR[0]
    for gg in range(1, 16):
        wg = wg + WGR[gg]
    WGS[...] = wg
    others(16, by, lambda n: dw_copy(n, by).start())
    WGA[by] = WGS[...]

    others(4, b, lambda bb: [lx_copy(bb, t, bb).wait_recv() for t in range(2)])
    others(16, by, lambda n: dq_copy(n, n).wait_recv())
    for t in range(2):
        o = jnp.zeros((192, 128), F32)
        for bb in range(4):
            o = o + dot(LTX[bb, t], QGA[bb * 4:(bb + 1) * 4].reshape(64, 128))
        OUTP[t] = o.reshape(4, 48, 128)
        for uu in range(4):

            @pl.when(not_self(t, uu))
            def _():
                o_copy(t, uu, u).start()

    @pl.when(b == 0)
    def _():
        out_q[:, pl.ds(pl.multiple_of(c * 128, 128), 128)] = OUTP[0, u]

    others(4, b, lambda bb: hx_copy(bb, bb).wait_recv())
    others(16, by, lambda n: dw_copy(n, n).wait_recv())
    gw = jnp.zeros((224, 128), F32)
    for bb in range(4):
        gw = gw + dot(HTX[bb], WGA[bb * 4:(bb + 1) * 4].reshape(64, 128).astype(BF))
    out_w[...] = jnp.where(yh == 0, gw[:, 0:32], gw[:, 32:64])
    out_l[...] = WGA[pl.ds(b * 4, 4)].reshape(64, 128)

    for t in range(2):
        for uu in range(4):

            @pl.when(not_self(t, uu))
            def _():
                cols = pl.ds(pl.multiple_of((zm(z + b + 4 * t) * 4 + uu) * 128, 128), 128)
                remote(
                    OUTP.at[t, uu], out_q.at[:, cols], s_o.at[t * 4 + uu], r_o.at[t * 4 + uu],
                    a_dev(zm(z + b + 4 * t), uu),
                ).wait_recv()

        others(4, b, lambda bb: ox_copy(bb, t, b).start())
    for t in range(2):

        def arrive(bb):
            cols = pl.ds(pl.multiple_of(zm(z + bb + 4 * t) * 512, 512), 512)
            remote(
                out_q.at[:, cols], out_q.at[:, cols],
                s_ox.at[bb * 2 + t], r_ox.at[bb * 2 + t], x_dev(bb),
            ).wait_recv()

        others(4, b, arrive)

    mp_copy.wait_send()
    for one in ik_copies + mk_copies:
        one.wait_send()
    for kind, n in (("ra", 4), ("la", 3), ("rb", 3), ("lb", 4)):
        for k in range(n):
            ring(kind, k).wait_send()

    def twins(zz):
        to_twin(zz, "a").wait_send()
        to_twin(zz, "b").wait_send()

    loop(0, 8, twins)

    def a_sends(i):
        t, uu = i // 4, i % 4

        @pl.when(not_self(t, uu))
        def _():
            w_copy(t, uu, u).wait_send()
            o_copy(t, uu, u).wait_send()

    loop(0, 8, a_sends)

    def x_sends(bb):
        wx_copy(bb, b).wait_send()
        hx_copy(bb, b).wait_send()
        for t in range(2):
            lx_copy(bb, t, b).wait_send()
            ox_copy(bb, t, b).wait_send()

    others(4, b, x_sends)

    def y_sends(yy):
        iqy_copy(yy, y).wait_send()
        hwy_copy(yy, y).wait_send()

    others(4, y, y_sends)

    def g_sends(gg):
        iqg_copy(gg, g).wait_send()
        hwg_copy(gg, g).wait_send()
        st_copy(gg, g).wait_send()
        rs_copy(gg, g).wait_send()
        wg_copy(gg, g).wait_send()

    others(16, g, g_sends)

    def by_sends(n):
        dq_copy(n, by).wait_send()
        dw_copy(n, by).wait_send()

    others(16, by, by_sends)


def per_device(
    q_latent, hidden, main_queries, main_keys, index_keys, positions, w_query, w_weights
):
    c = lax.axis_index("ctx")
    yh = lax.axis_index("head")
    y = yh * 2 + (c // 2) % 2
    rows_hidden = w_weights.shape[0]

    def by_group(x):
        x = x.reshape(8, 2, 2, 2, -1).transpose(3, 1, 0, 2, 4)
        return x.reshape(64, -1)

    latent = by_group(q_latent[0])
    lat8 = latent.reshape(64, 8, 192).transpose(1, 0, 2)
    lat_t = latent.T.reshape(8, 192, 64)
    hid = by_group(lax.dynamic_slice_in_dim(hidden[0], c * rows_hidden, rows_hidden, 1))
    hid_t = hid.T
    pos = lax.dynamic_slice_in_dim(by_group(positions[0][:, None])[:, 0], y * 16, 16, 0)
    pos_v = jnp.broadcast_to(pos[:, None], (16, 128))
    ww = jnp.concatenate([w_weights, jnp.zeros((rows_hidden, 96), BF)], axis=1)
    ww = jnp.where(yh == 0, ww, jnp.roll(ww, 32, axis=1))

    vm = pl.BlockSpec(memory_space=pltpu.VMEM)
    dma = pltpu.SemaphoreType.DMA
    sems = []
    for n in (8, 4, 4, 16, 4, 16, 1, 4, 3, 3, 4, 8, 8, 4, 16, 16, 16, 16, 16, 8, 4, 8, 8):
        sems += [dma((n,)), dma((n,))]
    out_q, out_w, out_l = pl.pallas_call(
        kernel,
        out_shape=(
            jax.ShapeDtypeStruct((48, 4096), F32),
            jax.ShapeDtypeStruct((224, 32), F32),
            jax.ShapeDtypeStruct((64, 128), F32),
        ),
        in_specs=[pl.BlockSpec(memory_space=pltpu.SMEM)] + [vm] * 10,
        out_specs=(vm, vm, vm),
        scratch_shapes=[
            pltpu.VMEM((4, 2, 4, 48, 128), BF),
            pltpu.VMEM((4, 16, 128), BF),
            pltpu.VMEM((4, 16, 128), BF),
            pltpu.VMEM((16, 4, 16, 128), BF),
            pltpu.VMEM((4, 16, 128), F32),
            pltpu.VMEM((4, 16, 128), F32),
            pltpu.VMEM((16, 128), F32),
            pltpu.VMEM((16, 16, 128), F32),
            pltpu.VMEM((64, 16, 128), F32),
            pltpu.VMEM((16, 2, 64, DL), BF),
            pltpu.VMEM((1024, DL), BF),
            pltpu.VMEM((1024, DI), BF),
            pltpu.VMEM((2, 16, 128, 1024), F32),
            pltpu.VMEM((128, 128), F32),
            pltpu.VMEM((128, 128), F32),
            pltpu.VMEM((128, 128), F32),
            pltpu.VMEM((128, 128), F32),
            pltpu.VMEM((32, 128), F32),
            pltpu.VMEM((16, 32, 128), F32),
            pltpu.VMEM((8, 1024, 256), F32),
            pltpu.VMEM((8, 16, 256), F32),
            pltpu.VMEM((8, 16, 256), F32),
            pltpu.VMEM((8, 256, 256), BF),
            pltpu.VMEM((16, 4, 16, 128), F32),
            pltpu.VMEM((16, 4, 16, 128), F32),
            pltpu.VMEM((16, 128), F32),
            pltpu.VMEM((16, 16, 128), F32),
            pltpu.VMEM((4, 16, 128), BF),
            pltpu.VMEM((16, 16, 128), BF),
            pltpu.VMEM((16, 128), F32),
            pltpu.VMEM((16, 16, 128), F32),
            pltpu.VMEM((4, 2, 192, 64), BF),
            pltpu.VMEM((4, 224, 64), BF),
            pltpu.VMEM((2, 4, 48, 128), F32),
        ]
        + sems,
        compiler_params=pltpu.CompilerParams(
            collective_id=0, has_side_effects=True, vmem_limit_bytes=56 * 1024 * 1024
        ),
        name="indexer_step",
    )(pos, pos_v, lat8, lat_t, hid, hid_t, main_queries[0], main_keys[0], index_keys[0], w_query, ww)
    loss = out_l[:, 64].reshape(2, 2, 8, 2).transpose(2, 1, 3, 0).reshape(1, 64)
    return out_q, out_w, loss


def solution(mesh):
    return jax.shard_map(
        per_device,
        mesh=mesh,
        in_specs=(
            P("dp", None, None),
            P("dp", None, None),
            P("dp", "ctx", "head", None),
            P("dp", "ctx", None),
            P("dp", "ctx", None),
            P("dp", None),
            P("ctx", "head"),
            P("ctx", "head"),
        ),
        out_specs=(P("ctx", "head"), P("ctx", "head"), P("dp", None)),
        check_vma=False,
    )
```

```python
import jax
import jax.numpy as jnp
from jax import lax
from jax.experimental import pallas as pl
from jax.experimental.pallas import tpu as pltpu
from jax.sharding import PartitionSpec as P

HI = 64
DI = 128
HM = 128
DL = 576
MESH = pl.DeviceIdType.MESH
BF = jnp.bfloat16
F32 = jnp.float32

LOG2E = 1.4426950408889634
LN2 = 0.6931471805599453
C2 = 192.0 ** (-0.5) * LOG2E
ISCALE = (HI * DI) ** (-0.5)
FLOOR = -1e30
LOW = -1e29

NT = (((1,), (1,)), ((), ()))
NN = (((1,), (0,)), ((), ()))
TN = (((0,), (0,)), ((), ()))


def dot(a, b, dims=NN):
    return lax.dot_general(a, b, dims, preferred_element_type=F32)


def log2(x):
    return jnp.log(x) * LOG2E


def remote(src, dst, ss, rs, dev):
    return pltpu.make_async_remote_copy(
        src_ref=src, dst_ref=dst, send_sem=ss, recv_sem=rs, device_id=dev, device_id_type=MESH
    )


def loop(lo, hi, body):
    def turn(i, carry):
        body(i)
        return carry

    lax.fori_loop(lo, hi, turn, 0)


def kernel(
    pos_s, lat_h, hid_h, mq_h, mk_h, ik_h, wq_h, ww_h,
    out_q, out_w, out_l,
    LATN, HIDW, MQL, K1, IK1, WQ, WWT, WWF, LAT8, HID, LTF, HTX, WB, PJ, IQP, IQY, IQG,
    HWL, HWY, HWS, HWG, HB, MQ, K2, IK2, E, MA, LA, MS, ST, STG, SI, SIG, AFF, LM, T, SG,
    RSB, RSR, WGP, WGR, DISP, QGA, WGS, WGA, OUTP, GWT,
    s_in,
    s_w, r_w, s_pj, r_pj, s_iqg, r_iqg, s_hwy, r_hwy, s_hwg, r_hwg,
    s_mp, r_mp, s_ra, r_ra, s_la, r_la, s_rb, r_rb, s_lb, r_lb, s_ca, r_ca, s_cb, r_cb,
    s_ik, r_ik, s_k, r_k, s_st, r_st, s_si, r_si, s_rs, r_rs, s_wg, r_wg, s_dq, r_dq, s_dw, r_dw,
    s_lx, r_lx, s_hx, r_hx, s_o, r_o, s_ox, r_ox,
):
    b = lax.axis_index("dp")
    yh = lax.axis_index("head")
    c = lax.axis_index("ctx")
    z = c // 4
    yl = (c // 2) % 2
    core = c % 2
    y = yh * 2 + yl
    u = yl * 2 + core
    g = z * 2 + core
    by = b * 4 + y
    hid_rows = ww_h.shape[1]

    hid_tile = jnp.minimum((c * hid_rows) // 128, 53)
    hid_rest = c * hid_rows - hid_tile * 128
    loads = [
        pltpu.make_async_copy(lat_h, LATN, s_in.at[0]),
        pltpu.make_async_copy(
            hid_h.at[:, pl.ds(pl.multiple_of(hid_tile * 128, 128), 384)], HIDW, s_in.at[1]
        ),
        pltpu.make_async_copy(ww_h, WWT, s_in.at[2]),
        pltpu.make_async_copy(wq_h, WQ, s_in.at[3]),
        pltpu.make_async_copy(mq_h, MQL, s_in.at[4]),
        pltpu.make_async_copy(mk_h, K1, s_in.at[5]),
        pltpu.make_async_copy(ik_h, IK1, s_in.at[6]),
    ]
    for one in loads:
        one.start()

    def g_dev(gg):
        return {"dp": b, "head": yh, "ctx": (gg // 2) * 4 + yl * 2 + gg % 2}

    def y_dev(yy):
        return {"dp": b, "head": yy // 2, "ctx": z * 4 + (yy % 2) * 2 + core}

    def x_dev(bb):
        return {"dp": bb, "head": yh, "ctx": c}

    def by_dev(n):
        yy = n % 4
        return {"dp": n // 4, "head": yy // 2, "ctx": z * 4 + (yy % 2) * 2 + core}

    def a_dev(zz, uu):
        return {"dp": b, "head": yh, "ctx": zz * 4 + uu}

    def zm(v):
        return lax.rem(v + 16, 8)

    def others(n, me, start):
        loop(1, n, lambda d: start(lax.rem(me + d, n)))

    bar = pltpu.get_barrier_semaphore()

    def hello(dev):
        pl.semaphore_signal(bar, inc=1, device_id=dev, device_id_type=MESH)

    others(16, g, lambda gg: hello(g_dev(gg)))
    others(16, by, lambda n: hello(by_dev(n)))

    def not_self(t, uu):
        return jnp.logical_or(b > 0, jnp.logical_or(t > 0, uu != u))

    def hello_a(i):
        t, uu = i // 4, i % 4

        @pl.when(not_self(t, uu))
        def _():
            hello(a_dev(zm(z - b - 4 * t), uu))
            hello(a_dev(zm(z + b + 4 * t), uu))

    loop(0, 8, hello_a)

    row64 = lax.broadcasted_iota(jnp.int32, (64, 64), 0)
    col64 = lax.broadcasted_iota(jnp.int32, (64, 64), 1)

    def natural(r):
        return ((r >> 1) & 7) * 8 + ((r >> 4) & 1) * 4 + (r & 1) * 2 + (r >> 5)

    perm = jnp.where(natural(row64) == col64, 1.0, 0.0).astype(BF)
    WWF[...] = jnp.zeros_like(WWF)
    loads[0].wait()
    lat = dot(perm, LATN[...]).astype(BF)
    for p in range(8):
        LAT8[p] = lat[:, p * 192:(p + 1) * 192]
    loads[1].wait()
    loads[2].wait()
    WWF[pl.ds(pl.multiple_of(yh * 32, 32), 32), :] = WWT[...]
    sel_row = lax.broadcasted_iota(jnp.int32, (384, hid_rows), 0)
    sel_col = lax.broadcasted_iota(jnp.int32, (384, hid_rows), 1)
    sel = jnp.where(sel_row == sel_col + hid_rest, 1.0, 0.0).astype(BF)
    HID[...] = dot(perm, dot(HIDW[...], sel).astype(BF)).astype(BF)
    HWL[...] = dot(HID[...], WWF[...], NT).reshape(4, 16, 128)
    for one in loads[3:]:
        one.wait()
    pl.semaphore_wait(bar, jnp.where(b == 0, 44, 46))

    def w_copy(t, uu, slot):
        zd = zm(z - b - 4 * t)
        cols = pl.ds(pl.multiple_of((zd * 4 + uu) * 128, 128), 128)
        return remote(
            WQ.at[:, cols], WB.at[t, u], s_w.at[t * 4 + uu], r_w.at[t * 4 + slot], a_dev(zd, uu)
        )

    def pj_copy(n, slot):
        return remote(PJ.at[n], IQP.at[slot], s_pj.at[n], r_pj.at[slot], by_dev(n))

    def iqg_copy(gg, slot):
        return remote(IQY, IQG.at[slot], s_iqg.at[gg], r_iqg.at[slot], g_dev(gg))

    def hwy_copy(yy, slot):
        return remote(HWL.at[yy], HWY.at[slot], s_hwy.at[yy], r_hwy.at[slot], y_dev(yy))

    def hwg_copy(gg, slot):
        return remote(HWS, HWG.at[slot], s_hwg.at[gg], r_hwg.at[slot], g_dev(gg))

    def st_copy(gg, slot):
        return remote(ST, STG.at[slot], s_st.at[gg], r_st.at[slot], g_dev(gg))

    def si_copy(gg, slot):
        return remote(SI, SIG.at[slot], s_si.at[gg], r_si.at[slot], g_dev(gg))

    def rs_copy(gg, slot):
        return remote(RSB.at[gg], RSR.at[slot], s_rs.at[gg], r_rs.at[slot], g_dev(gg))

    def wg_copy(gg, slot):
        return remote(WGP, WGR.at[slot], s_wg.at[gg], r_wg.at[slot], g_dev(gg))

    def dq_copy(n, slot):
        return remote(DISP.at[n % 4], QGA.at[slot], s_dq.at[n], r_dq.at[slot], by_dev(n))

    def dw_copy(n, slot):
        return remote(WGS, WGA.at[slot], s_dw.at[n], r_dw.at[slot], by_dev(n))

    def lx_copy(bb, t, slot):
        return remote(
            LAT8.at[zm(z + bb + 4 * t)], LTF.at[t, slot],
            s_lx.at[bb * 2 + t], r_lx.at[slot * 2 + t], x_dev(bb),
        )

    def hx_copy(bb, slot):
        return remote(HID, HTX.at[slot], s_hx.at[bb], r_hx.at[slot], x_dev(bb))

    def out_cols(zz, uu, n):
        return pl.ds(pl.multiple_of((zz * 4 + uu) * 128, 128), n * 128)

    def o_copy(t, uu):
        return remote(
            OUTP.at[t, uu], out_q.at[:, out_cols(z, u, 1)], s_o.at[t * 4 + uu], r_o.at[t * 4 + u],
            a_dev(zm(z + b + 4 * t), uu),
        )

    def o_arrival(t, uu):
        zz = zm(z - b - 4 * t)
        return remote(
            OUTP.at[t, uu], out_q.at[:, out_cols(zz, uu, 1)], s_o.at[t * 4 + uu],
            r_o.at[t * 4 + uu], a_dev(zz, uu),
        )

    def ox_copy(bb, t):
        cols = out_cols(zm(z - b - 4 * t), 0, 4)
        return remote(
            out_q.at[:, cols], out_q.at[:, cols], s_ox.at[bb * 2 + t], r_ox.at[b * 2 + t], x_dev(bb)
        )

    def ox_arrival(bb, t):
        cols = out_cols(zm(z - bb - 4 * t), 0, 4)
        return remote(
            out_q.at[:, cols], out_q.at[:, cols], s_ox.at[bb * 2 + t], r_ox.at[bb * 2 + t], x_dev(bb)
        )

    right = {"dp": b, "head": yh, "ctx": zm(z + 1) * 4 + u}
    left = {"dp": b, "head": yh, "ctx": zm(z - 1) * 4 + u}
    twin = {"dp": b, "head": yh, "ctx": z * 4 + yl * 2 + (1 - core)}

    def piece(zz, half):
        return MQ.at[zz * 2 + core, half]

    def ring(kind, k):
        half = yh if kind[1] == "a" else 1 - yh
        zz = zm(z - k) if kind[0] == "r" else zm(z + k)
        ss, rs = {"ra": (s_ra, r_ra), "la": (s_la, r_la), "rb": (s_rb, r_rb), "lb": (s_lb, r_lb)}[kind]
        return remote(
            piece(zz, half), piece(zz, half), ss.at[k], rs.at[k], right if kind[0] == "r" else left
        )

    def to_twin(zz, which):
        half = yh if which == "a" else 1 - yh
        ss, rs = (s_ca, r_ca) if which == "a" else (s_cb, r_cb)
        return remote(piece(zz, half), piece(zz, half), ss.at[zz], rs.at[zz], twin)

    partner = {"dp": b, "head": 1 - yh, "ctx": c}
    mp_copy = remote(MQL.at[1 - yh], MQ.at[g, yh], s_mp.at[0], r_mp.at[0], partner)
    up = y_dev(lax.rem(y + 1, 4))
    down = y_dev(lax.rem(y + 3, 4))

    def ik_copy(h):
        return remote(
            IK1.at[h * 4:(h + 1) * 4], IK2.at[:, h], s_ik.at[h], r_ik.at[h], down if h else up
        )

    def k_copy(h, i):
        return remote(
            K1.at[:, pl.ds(pl.multiple_of(h * 512 + i * 128, 128), 128)],
            K2.at[i, :, h * 128:(h + 1) * 128],
            s_k.at[h * 4 + i], r_k.at[h * 4 + i], down if h else up,
        )

    def w_start(i):
        t, uu = i // 4, i % 4

        @pl.when(not_self(t, uu))
        def _():
            w_copy(t, uu, u).start()

    loop(0, 8, w_start)
    mp_copy.start()
    others(4, b, lambda bb: [lx_copy(bb, t, b).start() for t in range(2)])
    MQ[g, yh] = MQL[yh]
    ring("ra", 0).start()
    ring("la", 0).start()
    to_twin(z, "a").start()
    others(4, y, lambda yy: hwy_copy(yy, y).start())

    def k_start(i):
        k_copy(0, i).start()
        k_copy(1, i).start()

    loop(0, 4, k_start)
    for h in range(2):
        ik_copy(h).start()
    HWY[y] = HWL[y]

    @pl.when(b == 0)
    def _():
        WB[0, u] = WQ[:, pl.ds(pl.multiple_of(c * 128, 128), 128)]

    for t in range(2):
        LTF[t, b] = LAT8[zm(z + b + 4 * t)]
    HTX[b] = HID[...]
    MA[...] = jnp.zeros_like(MA)
    LA[...] = jnp.zeros_like(LA)

    mp_copy.wait_recv()
    ring("rb", 0).start()
    ring("lb", 0).start()
    to_twin(z, "b").start()

    lane = lax.broadcasted_iota(jnp.int32, (128, 128), 1)
    near_row = lax.broadcasted_iota(jnp.int32, (1, 1024), 1) + c * 1024
    col256 = lax.broadcasted_iota(jnp.int32, (1, 256), 1)
    far_row = (z * 4 + (1 - yl) * 2 + core) * 1024 + (col256 >> 7) * 512 + (col256 & 127)

    def position(slot):
        return pos_s[0, (slot // 2) * 8 + (slot % 2) * 2 + 4 * yl + yh]

    def scores(zz, keys, key_row, part, cols):
        q = MQ[pl.ds(zz * 2, 2)].reshape(256, DL)
        s = dot(q, keys)
        for i in range(2):
            slot = zz * 2 + i
            vis = key_row <= position(slot)
            si = jnp.where(vis, s[i * 128:(i + 1) * 128], FLOOR)
            m = jnp.maximum(jnp.max(si, axis=1, keepdims=True), LOW)
            e = jnp.exp2((si - m) * C2)
            E[slot, :, cols] = e
            here = lane == part * 16 + slot
            MA[...] = jnp.where(here, m, MA[...])
            LA[...] = jnp.where(here, jnp.sum(e, axis=1, keepdims=True), LA[...])

    def near(zz):
        to_twin(zz, "a").wait_recv()
        to_twin(zz, "b").wait_recv()
        scores(zz, K1[...], near_row, 0, pl.ds(0, 1024))

    def step(k):
        ring("ra", k).wait_recv()
        if k < 3:
            ring("ra", k + 1).start()
        to_twin(zm(z - 1 - k), "a").start()
        if k < 3:
            ring("la", k).wait_recv()
            if k < 2:
                ring("la", k + 1).start()
            to_twin(zm(z + 1 + k), "a").start()
            ring("rb", k).wait_recv()
            if k < 2:
                ring("rb", k + 1).start()
            to_twin(zm(z - 1 - k), "b").start()
        ring("lb", k).wait_recv()
        if k < 3:
            ring("lb", k + 1).start()
        to_twin(zm(z + 1 + k), "b").start()

    step(0)
    near(z)

    def w_wait(i):
        t, uu = i // 4, i % 4

        @pl.when(not_self(t, uu))
        def _():
            w_copy(t, uu, uu).wait_recv()

    loop(0, 8, w_wait)
    others(4, b, lambda bb: [lx_copy(bb, t, bb).wait_recv() for t in range(2)])
    PJ[...] = (
        dot(LTF[0].reshape(256, 192), WB[0].reshape(192, 128))
        + dot(LTF[1].reshape(256, 192), WB[1].reshape(192, 128))
    ).reshape(16, 16, 128)
    others(16, by, lambda n: pj_copy(n, by).start())
    IQP[by] = PJ[by]
    others(4, y, lambda yy: hwy_copy(yy, yy).wait_recv())
    HWS[...] = HWY[0] + HWY[1] + HWY[2] + HWY[3]
    others(16, g, lambda gg: hwg_copy(gg, g).start())
    HWG[g] = HWS[...]
    others(4, b, lambda bb: hx_copy(bb, b).start())
    step(1)
    others(16, by, lambda n: pj_copy(n, n).wait_recv())
    for ys in range(4):
        IQY[ys] = (IQP[ys] + IQP[4 + ys] + IQP[8 + ys] + IQP[12 + ys]).astype(BF)
    others(16, g, lambda gg: iqg_copy(gg, g).start())
    IQG[g] = IQY[...]
    loop(0, 2, lambda i: near(zm(z - 1 + 2 * i)))
    step(2)
    loop(0, 2, lambda i: near(zm(z - 2 + 4 * i)))
    step(3)
    loop(0, 2, lambda i: near(zm(z - 3 + 6 * i)))
    near(zm(z + 4))

    def far(i):
        k_copy(0, i).wait_recv()
        k_copy(1, i).wait_recv()
        cols = pl.ds(pl.multiple_of(1024 + i * 256, 256), 256)
        loop(0, 8, lambda zz: scores(zz, K2[i], far_row + i * 128, 1 + i, cols))

    loop(0, 4, far)
    MS[...] = MA[...].T
    sums = LA[...].T
    tops = [MS[16 * p:16 * (p + 1)] for p in range(5)]
    mx = tops[0]
    for p in range(1, 5):
        mx = jnp.maximum(mx, tops[p])
    total = jnp.zeros((16, 128), F32)
    for p in range(5):
        total = total + sums[16 * p:16 * (p + 1)] * jnp.exp2((tops[p] - mx) * C2)
    ST[...] = mx * C2 + log2(jnp.maximum(total, 1e-37))
    others(16, g, lambda gg: st_copy(gg, g).start())
    STG[g] = ST[...]

    others(16, g, lambda gg: hwg_copy(gg, gg).wait_recv())
    hw = HWG[0]
    for gg in range(1, 16):
        hw = hw + HWG[gg]
    hw = hw * ISCALE
    for gg in range(16):
        for ys in range(4):
            j = (ys // 2) * 32 + (gg // 2) * 4 + (ys % 2) * 2 + gg % 2
            HB[gg * 4 + ys] = jnp.broadcast_to(hw[:, j:j + 1], (16, 128))
    sub256 = lax.broadcasted_iota(jnp.int32, (16, 256), 0)
    posq = jnp.zeros((16, 256), jnp.int32)
    for slot in range(16):
        posq = jnp.where(sub256 == slot, position(slot), posq)
    others(16, g, lambda gg: iqg_copy(gg, gg).wait_recv())
    for h in range(2):
        ik_copy(h).wait_recv()

    def index_tile(kt, tile, key_row):
        aff = dot(IQG[...].reshape(1024, 128), kt.reshape(256, 128), NT)
        AFF[tile] = aff
        total = jnp.zeros((16, 256), F32)
        for p in range(64):
            hb = HB[p]
            total = total + jnp.maximum(aff[p * 16:(p + 1) * 16], 0.0) * jnp.concatenate([hb, hb], axis=1)
        LM[tile] = jnp.where(key_row <= posq, total * LOG2E, FLOOR)

    loop(0, 4, lambda i: index_tile(IK1[pl.ds(i * 2, 2)], i, col256 + (c * 1024 + i * 256)))
    loop(0, 4, lambda i: index_tile(IK2[i], i + 4, far_row + i * 128))
    lm = LM[...]
    im = jnp.maximum(jnp.max(jnp.max(lm, axis=0), axis=1, keepdims=True), LOW)
    il = jnp.sum(jnp.sum(jnp.exp2(lm - im[None]), axis=0), axis=1, keepdims=True)
    lane16 = lax.broadcasted_iota(jnp.int32, (16, 128), 1)
    diag = lane16 == lax.broadcasted_iota(jnp.int32, (16, 128), 0)
    il = im + log2(jnp.maximum(il, 1e-37))
    SI[...] = jnp.broadcast_to(jnp.sum(jnp.where(diag, il, 0.0), axis=0, keepdims=True), (8, 128))
    others(16, g, lambda gg: si_copy(gg, g).start())
    SIG[g] = SI[...]

    others(16, g, lambda gg: st_copy(gg, gg).wait_recv())
    stats = STG[...]
    top = jnp.max(stats, axis=0)
    lse = top + log2(jnp.sum(jnp.exp2(stats - top[None]), axis=0))
    weights = [jnp.exp2(MS[16 * p:16 * (p + 1)] * C2 - lse) * (1.0 / HM) for p in range(5)]
    MA[...] = jnp.concatenate(weights + [jnp.zeros((48, 128), F32)], axis=0).T

    def target(slot):
        for p in range(5):
            w = jnp.sum(jnp.where(lane == p * 16 + slot, MA[...], 0.0), axis=1, keepdims=True)
            lo, hi = (0, 1024) if p == 0 else (768 + 256 * p, 1024 + 256 * p)
            row = jnp.sum(E[slot, :, lo:hi] * w, axis=0, keepdims=True)
            for t in range(lo // 256, hi // 256):
                T[t, pl.ds(slot, 1), :] = row[:, t * 256 - lo:t * 256 - lo + 256]

    loop(0, 16, target)
    others(16, g, lambda gg: si_copy(gg, gg).wait_recv())
    istats = SIG[...]
    itop = jnp.max(istats, axis=0)
    li = (itop + log2(jnp.sum(jnp.exp2(istats - itop[None]), axis=0)))[0:1]
    li = jnp.sum(jnp.where(diag, li, 0.0), axis=1, keepdims=True)
    loss = jnp.zeros((16, 1), F32)
    for t in range(8):
        shifted = LM[t] - li
        tt = T[t]
        loss = loss - jnp.sum(tt * shifted, axis=1, keepdims=True) * LN2
        T[t] = jnp.exp2(shifted) - tt

    WGP[...] = jnp.where(lane16 == 64, loss, 0.0)

    def back(i):
        for h in range(2):
            zz = zm(z + 4 - 2 * i - h)
            rows = pl.ds(pl.multiple_of(zz * 128, 128), 128)
            hb = HB[pl.ds(zz * 8, 8)]
            hb = jnp.concatenate([hb, hb], axis=2)
            acc = jnp.zeros((8, 16, 128), F32)
            for t in range(8):
                aff = AFF[t, rows, :].reshape(8, 16, 256)
                delta = T[t][None]
                sg = jnp.where(aff > 0.0, delta * hb, 0.0)
                SG[t, h * 128:(h + 1) * 128, :] = sg.reshape(128, 256).astype(BF)
                prod = delta * jnp.maximum(aff, 0.0)
                acc = acc + prod[:, :, 0:128] + prod[:, :, 128:256]
            got = jnp.sum(acc, axis=2, keepdims=True) * ISCALE
            wg = WGP[...]
            for n in range(8):
                cs, ys = n // 4, n % 4
                j = (ys // 2) * 32 + zz * 4 + (ys % 2) * 2 + cs
                wg = jnp.where(lane16 == j, got[n], wg)
            WGP[...] = wg
        total = jnp.zeros((256, 128), F32)
        for t in range(8):
            kt = IK1[2 * t:2 * t + 2] if t < 4 else IK2[t - 4]
            total = total + dot(SG[t], kt.reshape(256, 128))
        for h in range(2):
            zz = zm(z + 4 - 2 * i - h)
            part = total[h * 128:(h + 1) * 128].reshape(2, 4, 16, 128)
            RSB[pl.ds(zz * 2, 2)] = part.astype(BF)
            for cs in range(2):
                gg = zz * 2 + cs

                @pl.when(gg != g)
                def _():
                    rs_copy(gg, g).start()

    loop(0, 4, back)
    others(16, g, lambda gg: wg_copy(gg, g).start())
    WGR[g] = WGP[...]
    RSR[g] = RSB[g]

    mp_copy.wait_send()
    for h in range(2):
        ik_copy(h).wait_send()

    def k_sent(i):
        k_copy(0, i).wait_send()
        k_copy(1, i).wait_send()

    loop(0, 4, k_sent)
    for kind, n in (("ra", 4), ("la", 3), ("rb", 3), ("lb", 4)):
        for k in range(n):
            ring(kind, k).wait_send()

    def twins(zz):
        to_twin(zz, "a").wait_send()
        to_twin(zz, "b").wait_send()

    loop(0, 8, twins)

    def w_sent(i):
        t, uu = i // 4, i % 4

        @pl.when(not_self(t, uu))
        def _():
            w_copy(t, uu, u).wait_send()

    loop(0, 8, w_sent)

    def x_sent(bb):
        hx_copy(bb, b).wait_send()
        for t in range(2):
            lx_copy(bb, t, b).wait_send()

    others(4, b, x_sent)
    others(4, y, lambda yy: hwy_copy(yy, y).wait_send())

    def g_sent(gg):
        iqg_copy(gg, g).wait_send()
        hwg_copy(gg, g).wait_send()
        st_copy(gg, g).wait_send()
        si_copy(gg, g).wait_send()

    others(16, g, g_sent)
    others(16, by, lambda n: pj_copy(n, by).wait_send())

    others(16, g, lambda gg: rs_copy(gg, gg).wait_recv())
    qg = RSR[0].astype(F32)
    for gg in range(1, 16):
        qg = qg + RSR[gg].astype(F32)
    DISP[...] = qg.astype(BF)
    others(16, by, lambda n: dq_copy(n, by).start())
    QGA[by] = DISP[y]
    others(16, g, lambda gg: wg_copy(gg, gg).wait_recv())
    wg = WGR[0]
    for gg in range(1, 16):
        wg = wg + WGR[gg]
    WGS[...] = wg
    others(16, by, lambda n: dw_copy(n, by).start())
    WGA[by] = WGS[...]

    others(16, by, lambda n: dq_copy(n, n).wait_recv())
    for t in range(2):
        OUTP[t] = dot(LTF[t].reshape(256, 192), QGA[...].reshape(256, 128), TN).reshape(4, 48, 128)
        for uu in range(4):

            @pl.when(not_self(t, uu))
            def _():
                o_copy(t, uu).start()

    @pl.when(b == 0)
    def _():
        out_q[:, out_cols(z, u, 1)] = OUTP[0, u]

    others(4, b, lambda bb: hx_copy(bb, bb).wait_recv())
    others(16, by, lambda n: dw_copy(n, n).wait_recv())
    wg_all = WGA[...].reshape(256, 128)
    GWT[...] = dot(wg_all.astype(BF), HTX[...].reshape(256, hid_rows), TN)
    out_w[...] = GWT[pl.ds(pl.multiple_of(yh * 32, 32), 32), :]
    own = WGA[pl.ds(b * 4, 4)].reshape(64, 128)
    row = lax.broadcasted_iota(jnp.int32, (64, 128), 0)
    col = lax.broadcasted_iota(jnp.int32, (64, 128), 1)
    losses = jnp.where(natural(row) == col, own[:, 64:65], 0.0)
    out_l[...] = jnp.sum(losses, axis=0, keepdims=True)[:, 0:64]

    for t in range(2):
        for uu in range(4):

            @pl.when(not_self(t, uu))
            def _():
                o_arrival(t, uu).wait_recv()

        others(4, b, lambda bb: ox_copy(bb, t).start())

    def g_left(gg):
        rs_copy(gg, g).wait_send()
        wg_copy(gg, g).wait_send()

    others(16, g, g_left)

    def by_left(n):
        dq_copy(n, by).wait_send()
        dw_copy(n, by).wait_send()

    others(16, by, by_left)
    for t in range(2):
        for uu in range(4):

            @pl.when(not_self(t, uu))
            def _():
                o_copy(t, uu).wait_send()

    for t in range(2):
        others(4, b, lambda bb: ox_arrival(bb, t).wait_recv())
    for t in range(2):
        others(4, b, lambda bb: ox_copy(bb, t).wait_send())


def per_device(
    q_latent, hidden, main_queries, main_keys, index_keys, positions, w_query, w_weights
):
    hid_rows = w_weights.shape[0]
    vm = pl.BlockSpec(memory_space=pltpu.VMEM)
    hbm = pl.BlockSpec(memory_space=pl.ANY)
    dma = pltpu.SemaphoreType.DMA
    sems = [dma((7,))]
    for n in (8, 16, 16, 4, 16, 1, 4, 3, 3, 4, 8, 8, 2, 8, 16, 16, 16, 16, 16, 16, 8, 4, 8, 8):
        sems += [dma((n,)), dma((n,))]
    out_q, out_w, out_l = pl.pallas_call(
        kernel,
        out_shape=(
            jax.ShapeDtypeStruct((48, 4096), F32),
            jax.ShapeDtypeStruct((32, hid_rows), F32),
            jax.ShapeDtypeStruct((1, 64), F32),
        ),
        in_specs=[pl.BlockSpec(memory_space=pltpu.SMEM)] + [hbm] * 7,
        out_specs=(vm, vm, vm),
        scratch_shapes=[
            pltpu.VMEM((64, 1536), BF),
            pltpu.VMEM((64, 384), BF),
            pltpu.VMEM((2, 64, DL), BF),
            pltpu.VMEM((DL, 1024), BF),
            pltpu.VMEM((8, 128, DI), BF),
            pltpu.VMEM((48, 4096), BF),
            pltpu.VMEM((32, hid_rows), BF),
            pltpu.VMEM((128, hid_rows), BF),
            pltpu.VMEM((8, 64, 192), BF),
            pltpu.VMEM((64, hid_rows), BF),
            pltpu.VMEM((2, 4, 64, 192), BF),
            pltpu.VMEM((4, 64, hid_rows), BF),
            pltpu.VMEM((2, 4, 48, 128), BF),
            pltpu.VMEM((16, 16, 128), F32),
            pltpu.VMEM((16, 16, 128), F32),
            pltpu.VMEM((4, 16, 128), BF),
            pltpu.VMEM((16, 4, 16, 128), BF),
            pltpu.VMEM((4, 16, 128), F32),
            pltpu.VMEM((4, 16, 128), F32),
            pltpu.VMEM((16, 128), F32),
            pltpu.VMEM((16, 16, 128), F32),
            pltpu.VMEM((64, 16, 128), F32),
            pltpu.VMEM((16, 2, 64, DL), BF),
            pltpu.VMEM((4, DL, 256), BF),
            pltpu.VMEM((4, 2, 128, DI), BF),
            pltpu.VMEM((16, 128, 2048), F32),
            pltpu.VMEM((128, 128), F32),
            pltpu.VMEM((128, 128), F32),
            pltpu.VMEM((128, 128), F32),
            pltpu.VMEM((16, 128), F32),
            pltpu.VMEM((16, 16, 128), F32),
            pltpu.VMEM((8, 128), F32),
            pltpu.VMEM((16, 8, 128), F32),
            pltpu.VMEM((8, 1024, 256), F32),
            pltpu.VMEM((8, 16, 256), F32),
            pltpu.VMEM((8, 16, 256), F32),
            pltpu.VMEM((8, 256, 256), BF),
            pltpu.VMEM((16, 4, 16, 128), BF),
            pltpu.VMEM((16, 4, 16, 128), BF),
            pltpu.VMEM((16, 128), F32),
            pltpu.VMEM((16, 16, 128), F32),
            pltpu.VMEM((4, 16, 128), BF),
            pltpu.VMEM((16, 16, 128), BF),
            pltpu.VMEM((16, 128), F32),
            pltpu.VMEM((16, 16, 128), F32),
            pltpu.VMEM((2, 4, 48, 128), F32),
            pltpu.VMEM((128, hid_rows), F32),
        ]
        + sems,
        compiler_params=pltpu.CompilerParams(
            collective_id=0, has_side_effects=True, vmem_limit_bytes=56 * 1024 * 1024
        ),
        name="indexer_step",
    )(
        positions, q_latent[0], hidden[0], main_queries[0], main_keys[0].T,
        index_keys[0].reshape(8, 128, DI), w_query, w_weights.T,
    )
    return out_q, out_w.T, out_l


def solution(mesh):
    return jax.shard_map(
        per_device,
        mesh=mesh,
        in_specs=(
            P("dp", None, None),
            P("dp", None, None),
            P("dp", "ctx", "head", None),
            P("dp", "ctx", None),
            P("dp", "ctx", None),
            P("dp", None),
            P("ctx", "head"),
            P("ctx", "head"),
        ),
        out_specs=(P("ctx", "head"), P("ctx", "head"), P("dp", None)),
        check_vma=False,
    )
```

```python
import jax
import jax.numpy as jnp
from jax import lax
from jax.experimental import pallas as pl
from jax.experimental.pallas import tpu as pltpu
from jax.sharding import PartitionSpec as P

HI = 64
DI = 128
HM = 128
DL = 576
MESH = pl.DeviceIdType.MESH
BF = jnp.bfloat16
F32 = jnp.float32

LOG2E = 1.4426950408889634
LN2 = 0.6931471805599453
C2 = 192.0 ** (-0.5) * LOG2E
ISCALE = (HI * DI) ** (-0.5)
FLOOR = -1e30
LOW = -1e29

NT = (((1,), (1,)), ((), ()))
NN = (((1,), (0,)), ((), ()))
TN = (((0,), (0,)), ((), ()))


def dot(a, b, dims=NN):
    return lax.dot_general(a, b, dims, preferred_element_type=F32)


def log2(x):
    return jnp.log(x) * LOG2E


def remote(src, dst, ss, rs, dev):
    return pltpu.make_async_remote_copy(
        src_ref=src, dst_ref=dst, send_sem=ss, recv_sem=rs, device_id=dev, device_id_type=MESH
    )


def loop(lo, hi, body):
    def turn(i, carry):
        body(i)
        return carry

    lax.fori_loop(lo, hi, turn, 0)


def kernel(
    pos_s, lat_h, hid_h, mq_h, mk_h, ik_h, wq_h, ww_h,
    out_q, out_w, out_l,
    LATN, HIDW, MQL, K1, IK1, WQ, WWT, WWF, LAT8, HID, LTF, HTX, WB, PJ, IQP, IQY, IQG,
    HWL, HWY, HWS, HWG, HWC, HWT, HB, MQ, K2, IK2, E, MA, LA, MS, ST, STG, SI, SIG, AFF, LM, T, SG,
    RSB, RSR, WGP, WGR, DISP, QGA, WGS, WGA, OUTP, GWT,
    s_in,
    s_w, r_w, s_pj, r_pj, s_iqg, r_iqg, s_hwy, r_hwy, s_hwg, r_hwg,
    s_iqt, r_iqt, s_hwt, r_hwt, s_mp, r_mp, s_qa, r_qa, s_qb, r_qb, s_ca, r_ca, s_cb, r_cb,
    s_ik, r_ik, s_k, r_k, s_st, r_st, s_si, r_si, s_rs, r_rs, s_wg, r_wg, s_dq, r_dq, s_dw, r_dw,
    s_lx, r_lx, s_hx, r_hx, s_o, r_o, s_ox, r_ox,
):
    b = lax.axis_index("dp")
    yh = lax.axis_index("head")
    c = lax.axis_index("ctx")
    z = c // 4
    yl = (c // 2) % 2
    core = c % 2
    y = yh * 2 + yl
    u = yl * 2 + core
    g = z * 2 + core
    by = b * 4 + y
    hid_rows = ww_h.shape[1]

    hid_tile = jnp.minimum((c * hid_rows) // 128, 53)
    hid_rest = c * hid_rows - hid_tile * 128
    loads = [
        pltpu.make_async_copy(lat_h, LATN, s_in.at[0]),
        pltpu.make_async_copy(
            hid_h.at[:, pl.ds(pl.multiple_of(hid_tile * 128, 128), 384)], HIDW, s_in.at[1]
        ),
        pltpu.make_async_copy(ww_h, WWT, s_in.at[2]),
        pltpu.make_async_copy(wq_h, WQ, s_in.at[3]),
        pltpu.make_async_copy(mq_h, MQL, s_in.at[4]),
        pltpu.make_async_copy(mk_h, K1, s_in.at[5]),
        pltpu.make_async_copy(ik_h, IK1, s_in.at[6]),
    ]
    for one in loads:
        one.start()

    def g_dev(gg):
        return {"dp": b, "head": yh, "ctx": (gg // 2) * 4 + yl * 2 + gg % 2}

    def y_dev(yy):
        return {"dp": b, "head": yy // 2, "ctx": z * 4 + (yy % 2) * 2 + core}

    def x_dev(bb):
        return {"dp": bb, "head": yh, "ctx": c}

    def by_dev(n):
        yy = n % 4
        return {"dp": n // 4, "head": yy // 2, "ctx": z * 4 + (yy % 2) * 2 + core}

    def a_dev(zz, uu):
        return {"dp": b, "head": yh, "ctx": zz * 4 + uu}

    def zm(v):
        return lax.rem(v + 16, 8)

    def others(n, me, start):
        loop(1, n, lambda d: start(lax.rem(me + d, n)))

    bar = pltpu.get_barrier_semaphore()

    def hello(dev):
        pl.semaphore_signal(bar, inc=1, device_id=dev, device_id_type=MESH)

    others(16, g, lambda gg: hello(g_dev(gg)))
    others(16, by, lambda n: hello(by_dev(n)))

    def not_self(t, uu):
        return jnp.logical_or(b > 0, jnp.logical_or(t > 0, uu != u))

    def hello_a(i):
        t, uu = i // 4, i % 4

        @pl.when(not_self(t, uu))
        def _():
            hello(a_dev(zm(z - b - 4 * t), uu))
            hello(a_dev(zm(z + b + 4 * t), uu))

    loop(0, 8, hello_a)

    row64 = lax.broadcasted_iota(jnp.int32, (64, 64), 0)
    col64 = lax.broadcasted_iota(jnp.int32, (64, 64), 1)

    def natural(r):
        return ((r >> 1) & 7) * 8 + ((r >> 4) & 1) * 4 + (r & 1) * 2 + (r >> 5)

    perm = jnp.where(natural(row64) == col64, 1.0, 0.0).astype(BF)
    WWF[...] = jnp.zeros_like(WWF)
    loads[0].wait()
    lat = dot(perm, LATN[...]).astype(BF)
    for p in range(8):
        LAT8[p] = lat[:, p * 192:(p + 1) * 192]
    loads[1].wait()
    loads[2].wait()
    WWF[pl.ds(pl.multiple_of(yh * 32, 32), 32), :] = WWT[...]
    sel_row = lax.broadcasted_iota(jnp.int32, (384, hid_rows), 0)
    sel_col = lax.broadcasted_iota(jnp.int32, (384, hid_rows), 1)
    sel = jnp.where(sel_row == sel_col + hid_rest, 1.0, 0.0).astype(BF)
    HID[...] = dot(perm, dot(HIDW[...], sel).astype(BF)).astype(BF)
    HWL[...] = dot(HID[...], WWF[...], NT).reshape(4, 16, 128)
    for one in loads[3:]:
        one.wait()
    pl.semaphore_wait(bar, jnp.where(b == 0, 44, 46))

    def w_copy(t, uu, slot):
        zd = zm(z - b - 4 * t)
        cols = pl.ds(pl.multiple_of((zd * 4 + uu) * 128, 128), 128)
        return remote(
            WQ.at[:, cols], WB.at[t, u], s_w.at[t * 4 + uu], r_w.at[t * 4 + slot], a_dev(zd, uu)
        )

    def pj_copy(n, slot):
        return remote(PJ.at[n], IQP.at[slot], s_pj.at[n], r_pj.at[slot], by_dev(n))

    def iqz_copy(zz, slot):
        return remote(IQY, IQG.at[core, slot], s_iqg.at[zz], r_iqg.at[slot], a_dev(zz, u))

    def hwz_copy(zz, slot):
        return remote(HWS, HWG.at[slot], s_hwg.at[zz], r_hwg.at[slot], a_dev(zz, u))

    def hwy_copy(yy, slot):
        return remote(HWL.at[yy], HWY.at[slot], s_hwy.at[yy], r_hwy.at[slot], y_dev(yy))

    def st_copy(gg, slot):
        return remote(ST, STG.at[slot], s_st.at[gg], r_st.at[slot], g_dev(gg))

    def si_copy(gg, slot):
        return remote(SI, SIG.at[slot], s_si.at[gg], r_si.at[slot], g_dev(gg))

    def rs_copy(gg, slot):
        return remote(RSB.at[gg], RSR.at[slot], s_rs.at[gg], r_rs.at[slot], g_dev(gg))

    def wg_copy(gg, slot):
        return remote(WGP, WGR.at[slot], s_wg.at[gg], r_wg.at[slot], g_dev(gg))

    def dq_copy(n, slot):
        return remote(DISP.at[n % 4], QGA.at[slot], s_dq.at[n], r_dq.at[slot], by_dev(n))

    def dw_copy(n, slot):
        return remote(WGS, WGA.at[slot], s_dw.at[n], r_dw.at[slot], by_dev(n))

    def lx_copy(bb, t, slot):
        return remote(
            LAT8.at[zm(z + bb + 4 * t)], LTF.at[t, slot],
            s_lx.at[bb * 2 + t], r_lx.at[slot * 2 + t], x_dev(bb),
        )

    def hx_copy(bb, slot):
        return remote(HID, HTX.at[slot], s_hx.at[bb], r_hx.at[slot], x_dev(bb))

    def out_cols(zz, uu, n):
        return pl.ds(pl.multiple_of((zz * 4 + uu) * 128, 128), n * 128)

    def o_copy(t, uu):
        return remote(
            OUTP.at[t, uu], out_q.at[:, out_cols(z, u, 1)], s_o.at[t * 4 + uu], r_o.at[t * 4 + u],
            a_dev(zm(z + b + 4 * t), uu),
        )

    def o_arrival(t, uu):
        zz = zm(z - b - 4 * t)
        return remote(
            OUTP.at[t, uu], out_q.at[:, out_cols(zz, uu, 1)], s_o.at[t * 4 + uu],
            r_o.at[t * 4 + uu], a_dev(zz, uu),
        )

    def ox_copy(bb, t):
        cols = out_cols(zm(z - b - 4 * t), 0, 4)
        return remote(
            out_q.at[:, cols], out_q.at[:, cols], s_ox.at[bb * 2 + t], r_ox.at[b * 2 + t], x_dev(bb)
        )

    def ox_arrival(bb, t):
        cols = out_cols(zm(z - bb - 4 * t), 0, 4)
        return remote(
            out_q.at[:, cols], out_q.at[:, cols], s_ox.at[bb * 2 + t], r_ox.at[bb * 2 + t], x_dev(bb)
        )

    twin = {"dp": b, "head": yh, "ctx": z * 4 + yl * 2 + (1 - core)}
    iqt_copy = remote(IQG.at[core], IQG.at[core], s_iqt.at[0], r_iqt.at[0], twin)
    hwt_copy = remote(HWC, HWT, s_hwt.at[0], r_hwt.at[0], twin)
    hops = {
        "a": ((0, 2), (0, -2), (0, 1), (0, -1), (-2, 1), (2, -1), (-2, 2)),
        "b": ((0, 2), (0, -2), (0, 1), (0, -1), (-2, 1), (2, -1), (2, -2)),
    }

    def piece(zz, kind):
        return MQ.at[zz * 2 + core, yh if kind == "a" else 1 - yh]

    def hop(kind, n):
        of, far_by = hops[kind][n]
        ss, rs = (s_qa, r_qa) if kind == "a" else (s_qb, r_qb)
        zz = zm(z + of)
        return remote(
            piece(zz, kind), piece(zz, kind), ss.at[n], rs.at[zz], a_dev(zm(z + far_by), u)
        )

    def arrival(kind, of):
        ss, rs = (s_qa, r_qa) if kind == "a" else (s_qb, r_qb)
        zz = zm(z + of)
        remote(piece(zz, kind), piece(zz, kind), ss.at[0], rs.at[zz], a_dev(zm(z + of), u)).wait_recv()
        to_twin(zz, kind).start()

    def to_twin(zz, kind):
        ss, rs = (s_ca, r_ca) if kind == "a" else (s_cb, r_cb)
        return remote(piece(zz, kind), piece(zz, kind), ss.at[zz], rs.at[zz], twin)

    partner = {"dp": b, "head": 1 - yh, "ctx": c}
    mp_copy = remote(MQL.at[1 - yh], MQ.at[g, yh], s_mp.at[0], r_mp.at[0], partner)
    up = y_dev(lax.rem(y + 1, 4))
    down = y_dev(lax.rem(y + 3, 4))

    def ik_copy(h):
        return remote(
            IK1.at[h * 4:(h + 1) * 4], IK2.at[:, h], s_ik.at[h], r_ik.at[h], down if h else up
        )

    def k_copy(h, i):
        return remote(
            K1.at[:, pl.ds(pl.multiple_of(h * 512 + i * 128, 128), 128)],
            K2.at[i, :, h * 128:(h + 1) * 128],
            s_k.at[h * 4 + i], r_k.at[h * 4 + i], down if h else up,
        )

    def w_start(i):
        t, uu = i // 4, i % 4

        @pl.when(not_self(t, uu))
        def _():
            w_copy(t, uu, u).start()

    loop(0, 8, w_start)
    mp_copy.start()
    others(4, b, lambda bb: [lx_copy(bb, t, b).start() for t in range(2)])
    MQ[g, yh] = MQL[yh]
    for n in range(4):
        hop("a", n).start()
    to_twin(z, "a").start()
    others(4, y, lambda yy: hwy_copy(yy, y).start())

    def k_start(i):
        k_copy(0, i).start()
        k_copy(1, i).start()

    k_start(0)
    k_start(1)
    HWY[y] = HWL[y]

    @pl.when(b == 0)
    def _():
        WB[0, u] = WQ[:, pl.ds(pl.multiple_of(c * 128, 128), 128)]

    for t in range(2):
        LTF[t, b] = LAT8[zm(z + b + 4 * t)]
    HTX[b] = HID[...]
    MA[...] = jnp.zeros_like(MA)
    LA[...] = jnp.zeros_like(LA)

    mp_copy.wait_recv()
    for n in range(4):
        hop("b", n).start()
    to_twin(z, "b").start()

    lane = lax.broadcasted_iota(jnp.int32, (128, 128), 1)
    near_row = lax.broadcasted_iota(jnp.int32, (1, 1024), 1) + c * 1024
    col256 = lax.broadcasted_iota(jnp.int32, (1, 256), 1)
    far_row = (z * 4 + (1 - yl) * 2 + core) * 1024 + (col256 >> 7) * 512 + (col256 & 127)

    def position(slot):
        return pos_s[0, (slot // 2) * 8 + (slot % 2) * 2 + 4 * yl + yh]

    def scores(zz, keys, key_row, part, cols):
        q = MQ[pl.ds(zz * 2, 2)].reshape(256, DL)
        s = dot(q, keys)
        for i in range(2):
            slot = zz * 2 + i
            vis = key_row <= position(slot)
            si = jnp.where(vis, s[i * 128:(i + 1) * 128], FLOOR)
            m = jnp.maximum(jnp.max(si, axis=1, keepdims=True), LOW)
            e = jnp.exp2((si - m) * C2)
            E[slot, :, cols] = e
            here = lane == part * 16 + slot
            MA[...] = jnp.where(here, m, MA[...])
            LA[...] = jnp.where(here, jnp.sum(e, axis=1, keepdims=True), LA[...])

    def near(zz):
        to_twin(zz, "a").wait_recv()
        to_twin(zz, "b").wait_recv()
        scores(zz, K1[...], near_row, 0, pl.ds(0, 1024))

    def w_wait(i):
        t, uu = i // 4, i % 4

        @pl.when(not_self(t, uu))
        def _():
            w_copy(t, uu, uu).wait_recv()

    loop(0, 8, w_wait)
    others(4, b, lambda bb: [lx_copy(bb, t, bb).wait_recv() for t in range(2)])
    PJ[...] = (
        dot(LTF[0].reshape(256, 192), WB[0].reshape(192, 128))
        + dot(LTF[1].reshape(256, 192), WB[1].reshape(192, 128))
    ).reshape(16, 16, 128)
    others(16, by, lambda n: pj_copy(n, by).start())
    k_start(2)
    k_start(3)
    for h in range(2):
        ik_copy(h).start()
    IQP[by] = PJ[by]

    for of, n in ((-2, 4), (2, 5)):
        arrival("a", of)
        hop("a", n).start()
        if of == -2:
            hop("a", 6).start()
    arrival("a", -1)
    arrival("a", 1)
    others(4, y, lambda yy: hwy_copy(yy, yy).wait_recv())
    HWS[...] = HWY[0] + HWY[1] + HWY[2] + HWY[3]
    others(8, z, lambda zz: hwz_copy(zz, z).start())
    HWG[z] = HWS[...]
    others(4, b, lambda bb: hx_copy(bb, b).start())
    near(z)
    for of, n in ((-2, 4), (2, 5)):
        arrival("b", of)
        hop("b", n).start()
        if of == 2:
            hop("b", 6).start()
    arrival("b", -1)
    arrival("b", 1)
    others(16, by, lambda n: pj_copy(n, n).wait_recv())
    for ys in range(4):
        IQY[ys] = (IQP[ys] + IQP[4 + ys] + IQP[8 + ys] + IQP[12 + ys]).astype(BF)
    others(8, z, lambda zz: iqz_copy(zz, z).start())
    IQG[core, z] = IQY[...]

    def plane(k):
        return zm(z + jnp.where(lax.rem(k, 2) == 1, (k + 1) // 2, -(k // 2)))

    loop(1, 5, lambda k: near(plane(k)))

    def far(i, lo, hi):
        cols = pl.ds(pl.multiple_of(1024 + i * 256, 256), 256)
        loop(lo, hi, lambda k: scores(plane(k), K2[i], far_row + i * 128, 1 + i, cols))

    def k_wait(i):
        k_copy(0, i).wait_recv()
        k_copy(1, i).wait_recv()

    def far_early(i):
        k_wait(i)
        far(i, 0, 5)

    loop(0, 2, far_early)
    for kind in ("a", "b"):
        for of in (-3, 3, 4):
            arrival(kind, of)
    others(8, z, lambda zz: hwz_copy(zz, zz).wait_recv())
    hw = HWG[0]
    for zz in range(1, 8):
        hw = hw + HWG[zz]
    HWC[...] = hw
    hwt_copy.start()
    others(8, z, lambda zz: iqz_copy(zz, zz).wait_recv())
    iqt_copy.start()
    loop(5, 8, lambda k: near(plane(k)))
    loop(0, 2, lambda i: far(i, 5, 8))

    def far_late(i):
        k_wait(i)
        far(i, 0, 8)

    loop(2, 4, far_late)
    MS[...] = MA[...].T
    sums = LA[...].T
    tops = [MS[16 * p:16 * (p + 1)] for p in range(5)]
    mx = tops[0]
    for p in range(1, 5):
        mx = jnp.maximum(mx, tops[p])
    total = jnp.zeros((16, 128), F32)
    for p in range(5):
        total = total + sums[16 * p:16 * (p + 1)] * jnp.exp2((tops[p] - mx) * C2)
    ST[...] = mx * C2 + log2(jnp.maximum(total, 1e-37))
    others(16, g, lambda gg: st_copy(gg, g).start())
    STG[g] = ST[...]

    hwt_copy.wait_recv()
    hw = (HWC[...] + HWT[...]) * ISCALE
    for p in range(64):
        cs, zs, ys = p // 32, (p // 4) % 8, p % 4
        j = (ys // 2) * 32 + zs * 4 + (ys % 2) * 2 + cs
        HB[p] = jnp.broadcast_to(hw[:, j:j + 1], (16, 128))
    sub256 = lax.broadcasted_iota(jnp.int32, (16, 256), 0)
    posq = jnp.zeros((16, 256), jnp.int32)
    for slot in range(16):
        posq = jnp.where(sub256 == slot, position(slot), posq)
    iqt_copy.wait_recv()
    for h in range(2):
        ik_copy(h).wait_recv()

    def index_tile(kt, tile, key_row):
        aff = dot(IQG[...].reshape(1024, 128), kt.reshape(256, 128), NT)
        AFF[tile] = aff.reshape(2, 512, 256)
        total = jnp.zeros((16, 256), F32)
        for p in range(64):
            hb = HB[p]
            total = total + jnp.maximum(aff[p * 16:(p + 1) * 16], 0.0) * jnp.concatenate([hb, hb], axis=1)
        LM[tile] = jnp.where(key_row <= posq, total * LOG2E, FLOOR)

    loop(0, 4, lambda i: index_tile(IK1[pl.ds(i * 2, 2)], i, col256 + (c * 1024 + i * 256)))
    loop(0, 4, lambda i: index_tile(IK2[i], i + 4, far_row + i * 128))
    lm = LM[...]
    im = jnp.maximum(jnp.max(jnp.max(lm, axis=0), axis=1, keepdims=True), LOW)
    il = jnp.sum(jnp.sum(jnp.exp2(lm - im[None]), axis=0), axis=1, keepdims=True)
    lane16 = lax.broadcasted_iota(jnp.int32, (16, 128), 1)
    diag = lane16 == lax.broadcasted_iota(jnp.int32, (16, 128), 0)
    il = im + log2(jnp.maximum(il, 1e-37))
    SI[...] = jnp.broadcast_to(jnp.sum(jnp.where(diag, il, 0.0), axis=0, keepdims=True), (8, 128))
    others(16, g, lambda gg: si_copy(gg, g).start())
    SIG[g] = SI[...]

    others(16, g, lambda gg: st_copy(gg, gg).wait_recv())
    stats = STG[...]
    top = jnp.max(stats, axis=0)
    lse = top + log2(jnp.sum(jnp.exp2(stats - top[None]), axis=0))
    weights = [jnp.exp2(MS[16 * p:16 * (p + 1)] * C2 - lse) * (1.0 / HM) for p in range(5)]
    MA[...] = jnp.concatenate(weights + [jnp.zeros((48, 128), F32)], axis=0).T

    def target(slot):
        for p in range(5):
            w = jnp.sum(jnp.where(lane == p * 16 + slot, MA[...], 0.0), axis=1, keepdims=True)
            lo, hi = (0, 1024) if p == 0 else (768 + 256 * p, 1024 + 256 * p)
            row = jnp.sum(E[slot, :, lo:hi] * w, axis=0, keepdims=True)
            for t in range(lo // 256, hi // 256):
                T[t, pl.ds(slot, 1), :] = row[:, t * 256 - lo:t * 256 - lo + 256]

    loop(0, 16, target)
    others(16, g, lambda gg: si_copy(gg, gg).wait_recv())
    istats = SIG[...]
    itop = jnp.max(istats, axis=0)
    li = (itop + log2(jnp.sum(jnp.exp2(istats - itop[None]), axis=0)))[0:1]
    li = jnp.sum(jnp.where(diag, li, 0.0), axis=1, keepdims=True)
    loss = jnp.zeros((16, 1), F32)
    for t in range(8):
        shifted = LM[t] - li
        tt = T[t]
        loss = loss - jnp.sum(tt * shifted, axis=1, keepdims=True) * LN2
        T[t] = jnp.exp2(shifted) - tt

    WGP[...] = jnp.where(lane16 == 64, loss, 0.0)

    def back(i):
        for h in range(2):
            zz = zm(z + 4 - 2 * i - h)
            rows = pl.ds(pl.multiple_of(zz * 64, 64), 64)
            accs = []
            for cs in range(2):
                hb = HB[pl.ds(cs * 32 + zz * 4, 4)]
                hb = jnp.concatenate([hb, hb], axis=2)
                acc = jnp.zeros((4, 16, 128), F32)
                for t in range(8):
                    aff = AFF[t, cs, rows, :].reshape(4, 16, 256)
                    delta = T[t][None]
                    sg = jnp.where(aff > 0.0, delta * hb, 0.0)
                    top_row = h * 128 + cs * 64
                    SG[t, top_row:top_row + 64, :] = sg.reshape(64, 256).astype(BF)
                    prod = delta * jnp.maximum(aff, 0.0)
                    acc = acc + prod[:, :, 0:128] + prod[:, :, 128:256]
                accs.append(acc)
            acc = jnp.concatenate(accs, axis=0)
            got = jnp.sum(acc, axis=2, keepdims=True) * ISCALE
            wg = WGP[...]
            for n in range(8):
                cs, ys = n // 4, n % 4
                j = (ys // 2) * 32 + zz * 4 + (ys % 2) * 2 + cs
                wg = jnp.where(lane16 == j, got[n], wg)
            WGP[...] = wg
        total = jnp.zeros((256, 128), F32)
        for t in range(8):
            kt = IK1[2 * t:2 * t + 2] if t < 4 else IK2[t - 4]
            total = total + dot(SG[t], kt.reshape(256, 128))
        for h in range(2):
            zz = zm(z + 4 - 2 * i - h)
            part = total[h * 128:(h + 1) * 128].reshape(2, 4, 16, 128)
            RSB[pl.ds(zz * 2, 2)] = part.astype(BF)
            for cs in range(2):
                gg = zz * 2 + cs

                @pl.when(gg != g)
                def _():
                    rs_copy(gg, g).start()

    loop(0, 4, back)
    others(16, g, lambda gg: wg_copy(gg, g).start())
    WGR[g] = WGP[...]
    RSR[g] = RSB[g]

    mp_copy.wait_send()
    for h in range(2):
        ik_copy(h).wait_send()

    def k_sent(i):
        k_copy(0, i).wait_send()
        k_copy(1, i).wait_send()

    loop(0, 4, k_sent)
    for n in range(7):
        hop("a", n).wait_send()
        hop("b", n).wait_send()
    iqt_copy.wait_send()
    hwt_copy.wait_send()

    def twins(zz):
        to_twin(zz, "a").wait_send()
        to_twin(zz, "b").wait_send()

    loop(0, 8, twins)

    def w_sent(i):
        t, uu = i // 4, i % 4

        @pl.when(not_self(t, uu))
        def _():
            w_copy(t, uu, u).wait_send()

    loop(0, 8, w_sent)

    def x_sent(bb):
        hx_copy(bb, b).wait_send()
        for t in range(2):
            lx_copy(bb, t, b).wait_send()

    others(4, b, x_sent)
    others(4, y, lambda yy: hwy_copy(yy, y).wait_send())

    def g_sent(gg):
        st_copy(gg, g).wait_send()
        si_copy(gg, g).wait_send()

    others(16, g, g_sent)

    def z_sent(zz):
        iqz_copy(zz, z).wait_send()
        hwz_copy(zz, z).wait_send()

    others(8, z, z_sent)
    others(16, by, lambda n: pj_copy(n, by).wait_send())

    others(16, g, lambda gg: rs_copy(gg, gg).wait_recv())
    qg = RSR[0].astype(F32)
    for gg in range(1, 16):
        qg = qg + RSR[gg].astype(F32)
    DISP[...] = qg.astype(BF)
    others(16, by, lambda n: dq_copy(n, by).start())
    QGA[by] = DISP[y]
    others(16, g, lambda gg: wg_copy(gg, gg).wait_recv())
    wg = WGR[0]
    for gg in range(1, 16):
        wg = wg + WGR[gg]
    WGS[...] = wg
    others(16, by, lambda n: dw_copy(n, by).start())
    WGA[by] = WGS[...]

    others(16, by, lambda n: dq_copy(n, n).wait_recv())
    for t in range(2):
        o = dot(LTF[t].reshape(256, 192), QGA[...].reshape(256, 128), TN)
        OUTP[t] = o.astype(BF).reshape(4, 48, 128)
        for uu in range(4):

            @pl.when(not_self(t, uu))
            def _():
                o_copy(t, uu).start()

    @pl.when(b == 0)
    def _():
        out_q[:, out_cols(z, u, 1)] = OUTP[0, u]

    others(4, b, lambda bb: hx_copy(bb, bb).wait_recv())
    others(16, by, lambda n: dw_copy(n, n).wait_recv())
    wg_all = WGA[...].reshape(256, 128)
    GWT[...] = dot(wg_all.astype(BF), HTX[...].reshape(256, hid_rows), TN)
    out_w[...] = GWT[pl.ds(pl.multiple_of(yh * 32, 32), 32), :]
    own = WGA[pl.ds(b * 4, 4)].reshape(64, 128)
    row = lax.broadcasted_iota(jnp.int32, (64, 128), 0)
    col = lax.broadcasted_iota(jnp.int32, (64, 128), 1)
    losses = jnp.where(natural(row) == col, own[:, 64:65], 0.0)
    out_l[...] = jnp.sum(losses, axis=0, keepdims=True)[:, 0:64]

    for t in range(2):
        for uu in range(4):

            @pl.when(not_self(t, uu))
            def _():
                o_arrival(t, uu).wait_recv()

        others(4, b, lambda bb: ox_copy(bb, t).start())

    def g_left(gg):
        rs_copy(gg, g).wait_send()
        wg_copy(gg, g).wait_send()

    others(16, g, g_left)

    def by_left(n):
        dq_copy(n, by).wait_send()
        dw_copy(n, by).wait_send()

    others(16, by, by_left)
    for t in range(2):
        for uu in range(4):

            @pl.when(not_self(t, uu))
            def _():
                o_copy(t, uu).wait_send()

    for t in range(2):
        others(4, b, lambda bb: ox_arrival(bb, t).wait_recv())
    for t in range(2):
        others(4, b, lambda bb: ox_copy(bb, t).wait_send())


def per_device(
    q_latent, hidden, main_queries, main_keys, index_keys, positions, w_query, w_weights
):
    hid_rows = w_weights.shape[0]
    vm = pl.BlockSpec(memory_space=pltpu.VMEM)
    hbm = pl.BlockSpec(memory_space=pl.ANY)
    dma = pltpu.SemaphoreType.DMA
    sems = [dma((7,))]
    for n in (8, 16, 8, 4, 8, 1, 1, 1, 8, 8, 8, 8, 2, 8, 16, 16, 16, 16, 16, 16, 8, 4, 8, 8):
        sems += [dma((n,)), dma((n,))]
    out_q, out_w, out_l = pl.pallas_call(
        kernel,
        out_shape=(
            jax.ShapeDtypeStruct((48, 4096), BF),
            jax.ShapeDtypeStruct((32, hid_rows), F32),
            jax.ShapeDtypeStruct((1, 64), F32),
        ),
        in_specs=[pl.BlockSpec(memory_space=pltpu.SMEM)] + [hbm] * 7,
        out_specs=(vm, vm, vm),
        scratch_shapes=[
            pltpu.VMEM((64, 1536), BF),
            pltpu.VMEM((64, 384), BF),
            pltpu.VMEM((2, 64, DL), BF),
            pltpu.VMEM((DL, 1024), BF),
            pltpu.VMEM((8, 128, DI), BF),
            pltpu.VMEM((48, 4096), BF),
            pltpu.VMEM((32, hid_rows), BF),
            pltpu.VMEM((128, hid_rows), BF),
            pltpu.VMEM((8, 64, 192), BF),
            pltpu.VMEM((64, hid_rows), BF),
            pltpu.VMEM((2, 4, 64, 192), BF),
            pltpu.VMEM((4, 64, hid_rows), BF),
            pltpu.VMEM((2, 4, 48, 128), BF),
            pltpu.VMEM((16, 16, 128), F32),
            pltpu.VMEM((16, 16, 128), F32),
            pltpu.VMEM((4, 16, 128), BF),
            pltpu.VMEM((2, 8, 4, 16, 128), BF),
            pltpu.VMEM((4, 16, 128), F32),
            pltpu.VMEM((4, 16, 128), F32),
            pltpu.VMEM((16, 128), F32),
            pltpu.VMEM((8, 16, 128), F32),
            pltpu.VMEM((16, 128), F32),
            pltpu.VMEM((16, 128), F32),
            pltpu.VMEM((64, 16, 128), F32),
            pltpu.VMEM((16, 2, 64, DL), BF),
            pltpu.VMEM((4, DL, 256), BF),
            pltpu.VMEM((4, 2, 128, DI), BF),
            pltpu.VMEM((16, 128, 2048), F32),
            pltpu.VMEM((128, 128), F32),
            pltpu.VMEM((128, 128), F32),
            pltpu.VMEM((128, 128), F32),
            pltpu.VMEM((16, 128), F32),
            pltpu.VMEM((16, 16, 128), F32),
            pltpu.VMEM((8, 128), F32),
            pltpu.VMEM((16, 8, 128), F32),
            pltpu.VMEM((8, 2, 512, 256), F32),
            pltpu.VMEM((8, 16, 256), F32),
            pltpu.VMEM((8, 16, 256), F32),
            pltpu.VMEM((8, 256, 256), BF),
            pltpu.VMEM((16, 4, 16, 128), BF),
            pltpu.VMEM((16, 4, 16, 128), BF),
            pltpu.VMEM((16, 128), F32),
            pltpu.VMEM((16, 16, 128), F32),
            pltpu.VMEM((4, 16, 128), BF),
            pltpu.VMEM((16, 16, 128), BF),
            pltpu.VMEM((16, 128), F32),
            pltpu.VMEM((16, 16, 128), F32),
            pltpu.VMEM((2, 4, 48, 128), BF),
            pltpu.VMEM((128, hid_rows), F32),
        ]
        + sems,
        compiler_params=pltpu.CompilerParams(
            collective_id=0, has_side_effects=True, vmem_limit_bytes=56 * 1024 * 1024
        ),
        name="indexer_step",
    )(
        positions, q_latent[0], hidden[0], main_queries[0], main_keys[0].T,
        index_keys[0].reshape(8, 128, DI), w_query, w_weights.T,
    )
    return out_q.astype(F32), out_w.T, out_l


def solution(mesh):
    return jax.shard_map(
        per_device,
        mesh=mesh,
        in_specs=(
            P("dp", None, None),
            P("dp", None, None),
            P("dp", "ctx", "head", None),
            P("dp", "ctx", None),
            P("dp", "ctx", None),
            P("dp", None),
            P("ctx", "head"),
            P("ctx", "head"),
        ),
        out_specs=(P("ctx", "head"), P("ctx", "head"), P("dp", None)),
        check_vma=False,
    )
```

```python
import jax
import jax.numpy as jnp
from jax import lax
from jax.experimental import pallas as pl
from jax.experimental.pallas import tpu as pltpu
from jax.sharding import PartitionSpec as P

HI = 64
DI = 128
HM = 128
DL = 576
MESH = pl.DeviceIdType.MESH
BF = jnp.bfloat16
F32 = jnp.float32

LOG2E = 1.4426950408889634
LN2 = 0.6931471805599453
C2 = 192.0 ** (-0.5) * LOG2E
ISCALE = (HI * DI) ** (-0.5)
FLOOR = -1e30
LOW = -1e29

NT = (((1,), (1,)), ((), ()))
NN = (((1,), (0,)), ((), ()))
TN = (((0,), (0,)), ((), ()))


def dot(a, b, dims=NN):
    return lax.dot_general(a, b, dims, preferred_element_type=F32)


def log2(x):
    return jnp.log(x) * LOG2E


def remote(src, dst, ss, rs, dev):
    return pltpu.make_async_remote_copy(
        src_ref=src, dst_ref=dst, send_sem=ss, recv_sem=rs, device_id=dev, device_id_type=MESH
    )


def loop(lo, hi, body):
    def turn(i, carry):
        body(i)
        return carry

    lax.fori_loop(lo, hi, turn, 0)


def kernel(
    pos_s, lat_h, hid_h, mq_h, mk_h, ik_h, wq_h, ww_h,
    out_q, out_w, out_l,
    LATN, HIDW, MQL, K1, IK1, WQ, WWT, WWF, LAT8, HID, LTF, HTX, WB, PJ, IQP, IQY, IQG,
    HWL, HWY, HWS, HWG, HWC, HWT, HB, MQ, K2, IK2, E, MA, LA, MS, ST, STG, SI, SIG, AFF, LM, T, SG,
    RSB, RSR, WGP, WGR, DISP, QGA, WGS, WGA, OUTP, GWT,
    s_in,
    s_w, r_w, s_pj, r_pj, s_iqg, r_iqg, s_hwy, r_hwy, s_hwg, r_hwg,
    s_iqt, r_iqt, s_hwt, r_hwt, s_mp, r_mp, s_qa, r_qa, s_qb, r_qb, s_ca, r_ca, s_cb, r_cb,
    s_ik, r_ik, s_k, r_k, s_st, r_st, s_si, r_si, s_rs, r_rs, s_wg, r_wg, s_dq, r_dq, s_dw, r_dw,
    s_lx, r_lx, s_hx, r_hx, s_o, r_o, s_ox, r_ox,
):
    b = lax.axis_index("dp")
    yh = lax.axis_index("head")
    c = lax.axis_index("ctx")
    z = c // 4
    yl = (c // 2) % 2
    core = c % 2
    y = yh * 2 + yl
    u = yl * 2 + core
    g = z * 2 + core
    by = b * 4 + y
    hid_rows = ww_h.shape[1]

    hid_tile = jnp.minimum((c * hid_rows) // 128, 53)
    hid_rest = c * hid_rows - hid_tile * 128
    loads = [
        pltpu.make_async_copy(lat_h, LATN, s_in.at[0]),
        pltpu.make_async_copy(
            hid_h.at[:, pl.ds(pl.multiple_of(hid_tile * 128, 128), 384)], HIDW, s_in.at[1]
        ),
        pltpu.make_async_copy(ww_h, WWT, s_in.at[2]),
        pltpu.make_async_copy(wq_h, WQ, s_in.at[3]),
        pltpu.make_async_copy(mq_h, MQL, s_in.at[4]),
        pltpu.make_async_copy(mk_h, K1, s_in.at[5]),
        pltpu.make_async_copy(ik_h, IK1, s_in.at[6]),
    ]
    for one in loads:
        one.start()

    def g_dev(gg):
        return {"dp": b, "head": yh, "ctx": (gg // 2) * 4 + yl * 2 + gg % 2}

    def y_dev(yy):
        return {"dp": b, "head": yy // 2, "ctx": z * 4 + (yy % 2) * 2 + core}

    def x_dev(bb):
        return {"dp": bb, "head": yh, "ctx": c}

    def by_dev(n):
        yy = n % 4
        return {"dp": n // 4, "head": yy // 2, "ctx": z * 4 + (yy % 2) * 2 + core}

    def a_dev(zz, uu):
        return {"dp": b, "head": yh, "ctx": zz * 4 + uu}

    def zm(v):
        return lax.rem(v + 16, 8)

    def others(n, me, start):
        loop(1, n, lambda d: start(lax.rem(me + d, n)))

    bar = pltpu.get_barrier_semaphore()

    def hello(dev):
        pl.semaphore_signal(bar, inc=1, device_id=dev, device_id_type=MESH)

    others(16, g, lambda gg: hello(g_dev(gg)))
    others(16, by, lambda n: hello(by_dev(n)))

    def not_self(t, uu):
        return jnp.logical_or(b > 0, jnp.logical_or(t > 0, uu != u))

    def hello_a(i):
        t, uu = i // 4, i % 4

        @pl.when(not_self(t, uu))
        def _():
            hello(a_dev(zm(z - b - 4 * t), uu))
            hello(a_dev(zm(z + b + 4 * t), uu))

    loop(0, 8, hello_a)

    row64 = lax.broadcasted_iota(jnp.int32, (64, 64), 0)
    col64 = lax.broadcasted_iota(jnp.int32, (64, 64), 1)

    def natural(r):
        return ((r >> 1) & 7) * 8 + ((r >> 4) & 1) * 4 + (r & 1) * 2 + (r >> 5)

    perm = jnp.where(natural(row64) == col64, 1.0, 0.0).astype(BF)
    WWF[...] = jnp.zeros_like(WWF)
    loads[0].wait()
    lat = dot(perm, LATN[...]).astype(BF)
    for p in range(8):
        LAT8[p] = lat[:, p * 192:(p + 1) * 192]
    loads[1].wait()
    loads[2].wait()
    WWF[pl.ds(pl.multiple_of(yh * 32, 32), 32), :] = WWT[...]
    sel_row = lax.broadcasted_iota(jnp.int32, (384, hid_rows), 0)
    sel_col = lax.broadcasted_iota(jnp.int32, (384, hid_rows), 1)
    sel = jnp.where(sel_row == sel_col + hid_rest, 1.0, 0.0).astype(BF)
    HID[...] = dot(perm, dot(HIDW[...], sel).astype(BF)).astype(BF)
    HWL[...] = dot(HID[...], WWF[...], NT).reshape(4, 16, 128)
    for one in loads[3:]:
        one.wait()
    pl.semaphore_wait(bar, jnp.where(b == 0, 44, 46))

    def w_copy(t, uu, slot):
        zd = zm(z - b - 4 * t)
        cols = pl.ds(pl.multiple_of((zd * 4 + uu) * 128, 128), 128)
        return remote(
            WQ.at[:, cols], WB.at[t, u], s_w.at[t * 4 + uu], r_w.at[t * 4 + slot], a_dev(zd, uu)
        )

    def pj_copy(n, slot):
        return remote(PJ.at[n], IQP.at[slot], s_pj.at[n], r_pj.at[slot], by_dev(n))

    def iqz_copy(zz, slot):
        return remote(IQY, IQG.at[core, slot], s_iqg.at[zz], r_iqg.at[slot], a_dev(zz, u))

    def hwz_copy(zz, slot):
        return remote(HWS, HWG.at[slot], s_hwg.at[zz], r_hwg.at[slot], a_dev(zz, u))

    def hwy_copy(yy, slot):
        return remote(HWL.at[yy], HWY.at[slot], s_hwy.at[yy], r_hwy.at[slot], y_dev(yy))

    def st_copy(gg, slot):
        return remote(ST, STG.at[slot], s_st.at[gg], r_st.at[slot], g_dev(gg))

    def si_copy(gg, slot):
        return remote(SI, SIG.at[slot], s_si.at[gg], r_si.at[slot], g_dev(gg))

    def rs_copy(gg, slot):
        return remote(RSB.at[gg], RSR.at[slot], s_rs.at[gg], r_rs.at[slot], g_dev(gg))

    def wg_copy(gg, slot):
        return remote(WGP, WGR.at[slot], s_wg.at[gg], r_wg.at[slot], g_dev(gg))

    def dq_copy(n, slot):
        return remote(DISP.at[n % 4], QGA.at[slot], s_dq.at[n], r_dq.at[slot], by_dev(n))

    def dw_copy(n, slot):
        return remote(WGS, WGA.at[slot], s_dw.at[n], r_dw.at[slot], by_dev(n))

    def lx_copy(bb, t, slot):
        return remote(
            LAT8.at[zm(z + bb + 4 * t)], LTF.at[t, slot],
            s_lx.at[bb * 2 + t], r_lx.at[slot * 2 + t], x_dev(bb),
        )

    def hx_copy(bb, slot):
        return remote(HID, HTX.at[slot], s_hx.at[bb], r_hx.at[slot], x_dev(bb))

    def out_cols(zz, uu, n):
        return pl.ds(pl.multiple_of((zz * 4 + uu) * 128, 128), n * 128)

    def o_copy(t, uu):
        return remote(
            OUTP.at[t, uu], out_q.at[:, out_cols(z, u, 1)], s_o.at[t * 4 + uu], r_o.at[t * 4 + u],
            a_dev(zm(z + b + 4 * t), uu),
        )

    def o_arrival(t, uu):
        zz = zm(z - b - 4 * t)
        return remote(
            OUTP.at[t, uu], out_q.at[:, out_cols(zz, uu, 1)], s_o.at[t * 4 + uu],
            r_o.at[t * 4 + uu], a_dev(zz, uu),
        )

    def ox_copy(bb, t):
        cols = out_cols(zm(z - b - 4 * t), 0, 4)
        return remote(
            out_q.at[:, cols], out_q.at[:, cols], s_ox.at[bb * 2 + t], r_ox.at[b * 2 + t], x_dev(bb)
        )

    def ox_arrival(bb, t):
        cols = out_cols(zm(z - bb - 4 * t), 0, 4)
        return remote(
            out_q.at[:, cols], out_q.at[:, cols], s_ox.at[bb * 2 + t], r_ox.at[bb * 2 + t], x_dev(bb)
        )

    twin = {"dp": b, "head": yh, "ctx": z * 4 + yl * 2 + (1 - core)}
    iqt_copy = remote(IQG.at[core], IQG.at[core], s_iqt.at[0], r_iqt.at[0], twin)
    hwt_copy = remote(HWC, HWT, s_hwt.at[0], r_hwt.at[0], twin)
    hops = {
        "a": ((0, 2), (0, -2), (0, 1), (0, -1), (-2, 1), (2, -1), (-2, 2)),
        "b": ((0, 2), (0, -2), (0, 1), (0, -1), (-2, 1), (2, -1), (2, -2)),
    }

    places = {0: 0, 1: 1, -1: 2, 2: 3, -2: 4, 3: 5, -3: 6, 4: 7, -4: 7}

    def piece(of, kind):
        return MQ.at[places[of], core, yh if kind == "a" else 1 - yh]

    def hop(kind, n):
        of, far_by = hops[kind][n]
        ss, rs = (s_qa, r_qa) if kind == "a" else (s_qb, r_qb)
        there = of - far_by
        return remote(
            piece(of, kind), piece(there, kind), ss.at[n], rs.at[places[there]],
            a_dev(zm(z + far_by), u),
        )

    def arrival(kind, of):
        ss, rs = (s_qa, r_qa) if kind == "a" else (s_qb, r_qb)
        here = piece(of, kind)
        remote(here, here, ss.at[0], rs.at[places[of]], a_dev(zm(z + of), u)).wait_recv()
        to_twin(places[of], kind).start()

    def to_twin(k, kind):
        ss, rs = (s_ca, r_ca) if kind == "a" else (s_cb, r_cb)
        here = MQ.at[k, core, yh if kind == "a" else 1 - yh]
        return remote(here, here, ss.at[k], rs.at[k], twin)

    partner = {"dp": b, "head": 1 - yh, "ctx": c}
    mp_copy = remote(MQL.at[1 - yh], MQ.at[0, core, yh], s_mp.at[0], r_mp.at[0], partner)
    up = y_dev(lax.rem(y + 1, 4))
    down = y_dev(lax.rem(y + 3, 4))

    def ik_copy(h):
        return remote(
            IK1.at[h * 4:(h + 1) * 4], IK2.at[:, h], s_ik.at[h], r_ik.at[h], down if h else up
        )

    def k_copy(h, i):
        return remote(
            K1.at[:, pl.ds(pl.multiple_of(h * 512 + i * 128, 128), 128)],
            K2.at[i, :, h * 128:(h + 1) * 128],
            s_k.at[h * 4 + i], r_k.at[h * 4 + i], down if h else up,
        )

    def w_start(i):
        t, uu = i // 4, i % 4

        @pl.when(not_self(t, uu))
        def _():
            w_copy(t, uu, u).start()

    loop(0, 8, w_start)
    mp_copy.start()
    others(4, b, lambda bb: [lx_copy(bb, t, b).start() for t in range(2)])
    MQ[0, core, yh] = MQL[yh]
    for n in range(4):
        hop("a", n).start()
    to_twin(0, "a").start()
    others(4, y, lambda yy: hwy_copy(yy, y).start())

    def k_start(i):
        k_copy(0, i).start()
        k_copy(1, i).start()

    k_start(0)
    k_start(1)
    HWY[y] = HWL[y]

    @pl.when(b == 0)
    def _():
        WB[0, u] = WQ[:, pl.ds(pl.multiple_of(c * 128, 128), 128)]

    for t in range(2):
        LTF[t, b] = LAT8[zm(z + b + 4 * t)]
    HTX[b] = HID[...]
    MA[...] = jnp.zeros_like(MA)
    LA[...] = jnp.zeros_like(LA)

    mp_copy.wait_recv()
    for n in range(4):
        hop("b", n).start()
    to_twin(0, "b").start()

    lane = lax.broadcasted_iota(jnp.int32, (128, 128), 1)
    near_row = lax.broadcasted_iota(jnp.int32, (1, 1024), 1) + c * 1024
    col256 = lax.broadcasted_iota(jnp.int32, (1, 256), 1)
    far_row = (z * 4 + (1 - yl) * 2 + core) * 1024 + (col256 >> 7) * 512 + (col256 & 127)

    def position(slot):
        return pos_s[0, (slot // 2) * 8 + (slot % 2) * 2 + 4 * yl + yh]

    def plane(k):
        return zm(z + jnp.where(lax.rem(k, 2) == 1, (k + 1) // 2, -(k // 2)))

    def scores(k, count, keys, key_row, part, cols):
        q = MQ[pl.ds(k, count)].reshape(count * 256, DL)
        s = dot(q, keys)
        ma, la = MA[...], LA[...]
        for i in range(count * 2):
            slot = plane(k + i // 2) * 2 + i % 2
            vis = key_row <= position(slot)
            si = jnp.where(vis, s[i * 128:(i + 1) * 128], FLOOR)
            m = jnp.maximum(jnp.max(si, axis=1, keepdims=True), LOW)
            e = jnp.exp2((si - m) * C2)
            E[slot, :, cols] = e
            here = lane == part * 16 + slot
            ma = jnp.where(here, m, ma)
            la = jnp.where(here, jnp.sum(e, axis=1, keepdims=True), la)
        MA[...] = ma
        LA[...] = la

    def near(k):
        to_twin(k, "a").wait_recv()
        to_twin(k, "b").wait_recv()
        scores(k, 1, K1[...], near_row, 0, pl.ds(0, 1024))

    def w_wait(i):
        t, uu = i // 4, i % 4

        @pl.when(not_self(t, uu))
        def _():
            w_copy(t, uu, uu).wait_recv()

    loop(0, 8, w_wait)
    others(4, b, lambda bb: [lx_copy(bb, t, bb).wait_recv() for t in range(2)])
    PJ[...] = (
        dot(LTF[0].reshape(256, 192), WB[0].reshape(192, 128))
        + dot(LTF[1].reshape(256, 192), WB[1].reshape(192, 128))
    ).reshape(16, 16, 128)
    others(16, by, lambda n: pj_copy(n, by).start())
    k_start(2)
    k_start(3)
    for h in range(2):
        ik_copy(h).start()
    IQP[by] = PJ[by]

    for of, n in ((-2, 4), (2, 5)):
        arrival("a", of)
        hop("a", n).start()
        if of == -2:
            hop("a", 6).start()
    arrival("a", -1)
    arrival("a", 1)
    others(4, y, lambda yy: hwy_copy(yy, yy).wait_recv())
    HWS[...] = HWY[0] + HWY[1] + HWY[2] + HWY[3]
    others(8, z, lambda zz: hwz_copy(zz, z).start())
    HWG[z] = HWS[...]
    others(4, b, lambda bb: hx_copy(bb, b).start())
    near(0)
    for of, n in ((-2, 4), (2, 5)):
        arrival("b", of)
        hop("b", n).start()
        if of == 2:
            hop("b", 6).start()
    arrival("b", -1)
    arrival("b", 1)
    others(16, by, lambda n: pj_copy(n, n).wait_recv())
    for ys in range(4):
        IQY[ys] = (IQP[ys] + IQP[4 + ys] + IQP[8 + ys] + IQP[12 + ys]).astype(BF)
    others(8, z, lambda zz: iqz_copy(zz, z).start())
    IQG[core, z] = IQY[...]

    loop(1, 5, near)

    def far(i, k, count):
        cols = pl.ds(pl.multiple_of(1024 + i * 256, 256), 256)
        scores(k, count, K2[i], far_row + i * 128, 1 + i, cols)

    def far_early(i):
        k_copy(0, i).wait_recv()
        k_copy(1, i).wait_recv()
        far(i, 0, 5)

    loop(0, 4, far_early)
    for kind in ("a", "b"):
        for of in (-3, 3, 4):
            arrival(kind, of)
    others(8, z, lambda zz: hwz_copy(zz, zz).wait_recv())
    hw = HWG[0]
    for zz in range(1, 8):
        hw = hw + HWG[zz]
    HWC[...] = hw
    hwt_copy.start()
    others(8, z, lambda zz: iqz_copy(zz, zz).wait_recv())
    iqt_copy.start()
    loop(5, 8, near)
    loop(0, 4, lambda i: far(i, 5, 3))
    MS[...] = MA[...].T
    sums = LA[...].T
    tops = [MS[16 * p:16 * (p + 1)] for p in range(5)]
    mx = tops[0]
    for p in range(1, 5):
        mx = jnp.maximum(mx, tops[p])
    total = jnp.zeros((16, 128), F32)
    for p in range(5):
        total = total + sums[16 * p:16 * (p + 1)] * jnp.exp2((tops[p] - mx) * C2)
    ST[...] = mx * C2 + log2(jnp.maximum(total, 1e-37))
    others(16, g, lambda gg: st_copy(gg, g).start())
    STG[g] = ST[...]

    hwt_copy.wait_recv()
    hw = (HWC[...] + HWT[...]) * ISCALE
    for p in range(64):
        cs, zs, ys = p // 32, (p // 4) % 8, p % 4
        j = (ys // 2) * 32 + zs * 4 + (ys % 2) * 2 + cs
        HB[p] = jnp.broadcast_to(hw[:, j:j + 1], (16, 128))
    sub256 = lax.broadcasted_iota(jnp.int32, (16, 256), 0)
    posq = jnp.zeros((16, 256), jnp.int32)
    for slot in range(16):
        posq = jnp.where(sub256 == slot, position(slot), posq)
    iqt_copy.wait_recv()
    for h in range(2):
        ik_copy(h).wait_recv()

    def index_tile(kt, tile, key_row):
        aff = dot(IQG[...].reshape(1024, 128), kt.reshape(256, 128), NT)
        AFF[tile] = aff.reshape(2, 512, 256)
        total = jnp.zeros((16, 256), F32)
        for p in range(64):
            hb = HB[p]
            total = total + jnp.maximum(aff[p * 16:(p + 1) * 16], 0.0) * jnp.concatenate([hb, hb], axis=1)
        LM[tile] = jnp.where(key_row <= posq, total * LOG2E, FLOOR)

    loop(0, 4, lambda i: index_tile(IK1[pl.ds(i * 2, 2)], i, col256 + (c * 1024 + i * 256)))
    loop(0, 4, lambda i: index_tile(IK2[i], i + 4, far_row + i * 128))
    lm = LM[...]
    im = jnp.maximum(jnp.max(jnp.max(lm, axis=0), axis=1, keepdims=True), LOW)
    il = jnp.sum(jnp.sum(jnp.exp2(lm - im[None]), axis=0), axis=1, keepdims=True)
    lane16 = lax.broadcasted_iota(jnp.int32, (16, 128), 1)
    diag = lane16 == lax.broadcasted_iota(jnp.int32, (16, 128), 0)
    il = im + log2(jnp.maximum(il, 1e-37))
    SI[...] = jnp.broadcast_to(jnp.sum(jnp.where(diag, il, 0.0), axis=0, keepdims=True), (8, 128))
    others(16, g, lambda gg: si_copy(gg, g).start())
    SIG[g] = SI[...]

    others(16, g, lambda gg: st_copy(gg, gg).wait_recv())
    stats = STG[...]
    top = jnp.max(stats, axis=0)
    lse = top + log2(jnp.sum(jnp.exp2(stats - top[None]), axis=0))
    weights = [jnp.exp2(MS[16 * p:16 * (p + 1)] * C2 - lse) * (1.0 / HM) for p in range(5)]
    MA[...] = jnp.concatenate(weights + [jnp.zeros((48, 128), F32)], axis=0).T

    def target(slot):
        for p in range(5):
            w = jnp.sum(jnp.where(lane == p * 16 + slot, MA[...], 0.0), axis=1, keepdims=True)
            lo, hi = (0, 1024) if p == 0 else (768 + 256 * p, 1024 + 256 * p)
            row = jnp.sum(E[slot, :, lo:hi] * w, axis=0, keepdims=True)
            for t in range(lo // 256, hi // 256):
                T[t, pl.ds(slot, 1), :] = row[:, t * 256 - lo:t * 256 - lo + 256]

    loop(0, 16, target)
    others(16, g, lambda gg: si_copy(gg, gg).wait_recv())
    istats = SIG[...]
    itop = jnp.max(istats, axis=0)
    li = (itop + log2(jnp.sum(jnp.exp2(istats - itop[None]), axis=0)))[0:1]
    li = jnp.sum(jnp.where(diag, li, 0.0), axis=1, keepdims=True)
    loss = jnp.zeros((16, 1), F32)
    for t in range(8):
        shifted = LM[t] - li
        tt = T[t]
        loss = loss - jnp.sum(tt * shifted, axis=1, keepdims=True) * LN2
        T[t] = jnp.exp2(shifted) - tt

    WGP[...] = jnp.where(lane16 == 64, loss, 0.0)

    def back(i):
        for h in range(2):
            zz = zm(z + 4 - 2 * i - h)
            rows = pl.ds(pl.multiple_of(zz * 64, 64), 64)
            accs = []
            for cs in range(2):
                hb = HB[pl.ds(cs * 32 + zz * 4, 4)]
                hb = jnp.concatenate([hb, hb], axis=2)
                acc = jnp.zeros((4, 16, 128), F32)
                for t in range(8):
                    aff = AFF[t, cs, rows, :].reshape(4, 16, 256)
                    delta = T[t][None]
                    sg = jnp.where(aff > 0.0, delta * hb, 0.0)
                    top_row = h * 128 + cs * 64
                    SG[t, top_row:top_row + 64, :] = sg.reshape(64, 256).astype(BF)
                    prod = delta * jnp.maximum(aff, 0.0)
                    acc = acc + prod[:, :, 0:128] + prod[:, :, 128:256]
                accs.append(acc)
            acc = jnp.concatenate(accs, axis=0)
            got = jnp.sum(acc, axis=2, keepdims=True) * ISCALE
            wg = WGP[...]
            for n in range(8):
                cs, ys = n // 4, n % 4
                j = (ys // 2) * 32 + zz * 4 + (ys % 2) * 2 + cs
                wg = jnp.where(lane16 == j, got[n], wg)
            WGP[...] = wg
        total = jnp.zeros((256, 128), F32)
        for t in range(8):
            kt = IK1[2 * t:2 * t + 2] if t < 4 else IK2[t - 4]
            total = total + dot(SG[t], kt.reshape(256, 128))
        for h in range(2):
            zz = zm(z + 4 - 2 * i - h)
            part = total[h * 128:(h + 1) * 128].reshape(2, 4, 16, 128)
            RSB[pl.ds(zz * 2, 2)] = part.astype(BF)
            for cs in range(2):
                gg = zz * 2 + cs

                @pl.when(gg != g)
                def _():
                    rs_copy(gg, g).start()

    loop(0, 4, back)
    others(16, g, lambda gg: wg_copy(gg, g).start())
    WGR[g] = WGP[...]
    RSR[g] = RSB[g]

    mp_copy.wait_send()
    for h in range(2):
        ik_copy(h).wait_send()

    def k_sent(i):
        k_copy(0, i).wait_send()
        k_copy(1, i).wait_send()

    loop(0, 4, k_sent)
    for n in range(7):
        hop("a", n).wait_send()
        hop("b", n).wait_send()
    iqt_copy.wait_send()
    hwt_copy.wait_send()

    def twins(zz):
        to_twin(zz, "a").wait_send()
        to_twin(zz, "b").wait_send()

    loop(0, 8, twins)

    def w_sent(i):
        t, uu = i // 4, i % 4

        @pl.when(not_self(t, uu))
        def _():
            w_copy(t, uu, u).wait_send()

    loop(0, 8, w_sent)

    def x_sent(bb):
        hx_copy(bb, b).wait_send()
        for t in range(2):
            lx_copy(bb, t, b).wait_send()

    others(4, b, x_sent)
    others(4, y, lambda yy: hwy_copy(yy, y).wait_send())

    def g_sent(gg):
        st_copy(gg, g).wait_send()
        si_copy(gg, g).wait_send()

    others(16, g, g_sent)

    def z_sent(zz):
        iqz_copy(zz, z).wait_send()
        hwz_copy(zz, z).wait_send()

    others(8, z, z_sent)
    others(16, by, lambda n: pj_copy(n, by).wait_send())

    others(16, g, lambda gg: rs_copy(gg, gg).wait_recv())
    qg = RSR[0].astype(F32)
    for gg in range(1, 16):
        qg = qg + RSR[gg].astype(F32)
    DISP[...] = qg.astype(BF)
    others(16, by, lambda n: dq_copy(n, by).start())
    QGA[by] = DISP[y]
    others(16, g, lambda gg: wg_copy(gg, gg).wait_recv())
    wg = WGR[0]
    for gg in range(1, 16):
        wg = wg + WGR[gg]
    WGS[...] = wg
    others(16, by, lambda n: dw_copy(n, by).start())
    WGA[by] = WGS[...]

    others(16, by, lambda n: dq_copy(n, n).wait_recv())
    for t in range(2):
        o = dot(LTF[t].reshape(256, 192), QGA[...].reshape(256, 128), TN)
        OUTP[t] = o.astype(BF).reshape(4, 48, 128)
        for uu in range(4):

            @pl.when(not_self(t, uu))
            def _():
                o_copy(t, uu).start()

    @pl.when(b == 0)
    def _():
        out_q[:, out_cols(z, u, 1)] = OUTP[0, u]

    others(4, b, lambda bb: hx_copy(bb, bb).wait_recv())
    others(16, by, lambda n: dw_copy(n, n).wait_recv())
    wg_all = WGA[...].reshape(256, 128)
    GWT[...] = dot(wg_all.astype(BF), HTX[...].reshape(256, hid_rows), TN)
    out_w[...] = GWT[pl.ds(pl.multiple_of(yh * 32, 32), 32), :]
    own = WGA[pl.ds(b * 4, 4)].reshape(64, 128)
    row = lax.broadcasted_iota(jnp.int32, (64, 128), 0)
    col = lax.broadcasted_iota(jnp.int32, (64, 128), 1)
    losses = jnp.where(natural(row) == col, own[:, 64:65], 0.0)
    out_l[...] = jnp.sum(losses, axis=0, keepdims=True)[:, 0:64]

    for t in range(2):
        for uu in range(4):

            @pl.when(not_self(t, uu))
            def _():
                o_arrival(t, uu).wait_recv()

        others(4, b, lambda bb: ox_copy(bb, t).start())

    def g_left(gg):
        rs_copy(gg, g).wait_send()
        wg_copy(gg, g).wait_send()

    others(16, g, g_left)

    def by_left(n):
        dq_copy(n, by).wait_send()
        dw_copy(n, by).wait_send()

    others(16, by, by_left)
    for t in range(2):
        for uu in range(4):

            @pl.when(not_self(t, uu))
            def _():
                o_copy(t, uu).wait_send()

    for t in range(2):
        others(4, b, lambda bb: ox_arrival(bb, t).wait_recv())
    for t in range(2):
        others(4, b, lambda bb: ox_copy(bb, t).wait_send())


def per_device(
    q_latent, hidden, main_queries, main_keys, index_keys, positions, w_query, w_weights
):
    hid_rows = w_weights.shape[0]
    vm = pl.BlockSpec(memory_space=pltpu.VMEM)
    hbm = pl.BlockSpec(memory_space=pl.ANY)
    dma = pltpu.SemaphoreType.DMA
    sems = [dma((7,))]
    for n in (8, 16, 8, 4, 8, 1, 1, 1, 8, 8, 8, 8, 2, 8, 16, 16, 16, 16, 16, 16, 8, 4, 8, 8):
        sems += [dma((n,)), dma((n,))]
    out_q, out_w, out_l = pl.pallas_call(
        kernel,
        out_shape=(
            jax.ShapeDtypeStruct((48, 4096), BF),
            jax.ShapeDtypeStruct((32, hid_rows), F32),
            jax.ShapeDtypeStruct((1, 64), F32),
        ),
        in_specs=[pl.BlockSpec(memory_space=pltpu.SMEM)] + [hbm] * 7,
        out_specs=(vm, vm, vm),
        scratch_shapes=[
            pltpu.VMEM((64, 1536), BF),
            pltpu.VMEM((64, 384), BF),
            pltpu.VMEM((2, 64, DL), BF),
            pltpu.VMEM((DL, 1024), BF),
            pltpu.VMEM((8, 128, DI), BF),
            pltpu.VMEM((48, 4096), BF),
            pltpu.VMEM((32, hid_rows), BF),
            pltpu.VMEM((128, hid_rows), BF),
            pltpu.VMEM((8, 64, 192), BF),
            pltpu.VMEM((64, hid_rows), BF),
            pltpu.VMEM((2, 4, 64, 192), BF),
            pltpu.VMEM((4, 64, hid_rows), BF),
            pltpu.VMEM((2, 4, 48, 128), BF),
            pltpu.VMEM((16, 16, 128), F32),
            pltpu.VMEM((16, 16, 128), F32),
            pltpu.VMEM((4, 16, 128), BF),
            pltpu.VMEM((2, 8, 4, 16, 128), BF),
            pltpu.VMEM((4, 16, 128), F32),
            pltpu.VMEM((4, 16, 128), F32),
            pltpu.VMEM((16, 128), F32),
            pltpu.VMEM((8, 16, 128), F32),
            pltpu.VMEM((16, 128), F32),
            pltpu.VMEM((16, 128), F32),
            pltpu.VMEM((64, 16, 128), F32),
            pltpu.VMEM((8, 2, 2, 64, DL), BF),
            pltpu.VMEM((4, DL, 256), BF),
            pltpu.VMEM((4, 2, 128, DI), BF),
            pltpu.VMEM((16, 128, 2048), F32),
            pltpu.VMEM((128, 128), F32),
            pltpu.VMEM((128, 128), F32),
            pltpu.VMEM((128, 128), F32),
            pltpu.VMEM((16, 128), F32),
            pltpu.VMEM((16, 16, 128), F32),
            pltpu.VMEM((8, 128), F32),
            pltpu.VMEM((16, 8, 128), F32),
            pltpu.VMEM((8, 2, 512, 256), F32),
            pltpu.VMEM((8, 16, 256), F32),
            pltpu.VMEM((8, 16, 256), F32),
            pltpu.VMEM((8, 256, 256), BF),
            pltpu.VMEM((16, 4, 16, 128), BF),
            pltpu.VMEM((16, 4, 16, 128), BF),
            pltpu.VMEM((16, 128), F32),
            pltpu.VMEM((16, 16, 128), F32),
            pltpu.VMEM((4, 16, 128), BF),
            pltpu.VMEM((16, 16, 128), BF),
            pltpu.VMEM((16, 128), F32),
            pltpu.VMEM((16, 16, 128), F32),
            pltpu.VMEM((2, 4, 48, 128), BF),
            pltpu.VMEM((128, hid_rows), F32),
        ]
        + sems,
        compiler_params=pltpu.CompilerParams(
            collective_id=0, has_side_effects=True, vmem_limit_bytes=56 * 1024 * 1024
        ),
        name="indexer_step",
    )(
        positions, q_latent[0], hidden[0], main_queries[0], main_keys[0].T,
        index_keys[0].reshape(8, 128, DI), w_query, w_weights.T,
    )
    return out_q.astype(F32), out_w.T, out_l


def solution(mesh):
    return jax.shard_map(
        per_device,
        mesh=mesh,
        in_specs=(
            P("dp", None, None),
            P("dp", None, None),
            P("dp", "ctx", "head", None),
            P("dp", "ctx", None),
            P("dp", "ctx", None),
            P("dp", None),
            P("ctx", "head"),
            P("ctx", "head"),
        ),
        out_specs=(P("ctx", "head"), P("ctx", "head"), P("dp", None)),
        check_vma=False,
    )
```

```python
import jax
import jax.numpy as jnp
from jax import lax
from jax.experimental import pallas as pl
from jax.experimental.pallas import tpu as pltpu
from jax.sharding import PartitionSpec as P

HI = 64
DI = 128
HM = 128
DL = 576
MESH = pl.DeviceIdType.MESH
BF = jnp.bfloat16
F32 = jnp.float32

LOG2E = 1.4426950408889634
LN2 = 0.6931471805599453
C2 = 192.0 ** (-0.5) * LOG2E
ISCALE = (HI * DI) ** (-0.5)
FLOOR = -1e30
LOW = -1e29

NT = (((1,), (1,)), ((), ()))
NN = (((1,), (0,)), ((), ()))
TN = (((0,), (0,)), ((), ()))


def dot(a, b, dims=NN):
    return lax.dot_general(a, b, dims, preferred_element_type=F32)


def log2(x):
    return jnp.log(x) * LOG2E


def remote(src, dst, ss, rs, dev):
    return pltpu.make_async_remote_copy(
        src_ref=src, dst_ref=dst, send_sem=ss, recv_sem=rs, device_id=dev, device_id_type=MESH
    )


def loop(lo, hi, body):
    def turn(i, carry):
        body(i)
        return carry

    lax.fori_loop(lo, hi, turn, 0)


def kernel(
    pos_s, lat_h, hid_h, mq_h, mk_h, ik_h, wq_h, ww_h,
    out_q, out_w, out_l,
    LATN, HIDW, MQL, K1, IK1, WQ, WWT, WWF, LAT8, HID, LTF, HTX, WB, PJ, IQP, IQY, IQG,
    HWL, HWY, HWS, HWG, HWC, HWT, HB, MQ, K2, IK2, E, MA, LA, MS, ST, STG, SI, SIG, AFF, LM, T, SG,
    RSB, RSR, WGP, WGR, DISP, QGA, WGS, WGA, OUTP, GWT,
    s_in,
    s_w, r_w, s_pj, r_pj, s_iqg, r_iqg, s_hwy, r_hwy, s_hwg, r_hwg,
    s_iqt, r_iqt, s_hwt, r_hwt, s_mp, r_mp, s_qa, r_qa, s_qb, r_qb, s_ca, r_ca, s_cb, r_cb,
    s_ik, r_ik, s_k, r_k, s_st, r_st, s_si, r_si, s_rs, r_rs, s_wg, r_wg, s_dq, r_dq, s_dw, r_dw,
    s_lx, r_lx, s_hx, r_hx, s_o, r_o, s_ox, r_ox,
):
    b = lax.axis_index("dp")
    yh = lax.axis_index("head")
    c = lax.axis_index("ctx")
    z = c // 4
    yl = (c // 2) % 2
    core = c % 2
    y = yh * 2 + yl
    u = yl * 2 + core
    g = z * 2 + core
    by = b * 4 + y
    hid_rows = ww_h.shape[1]

    hid_tile = jnp.minimum((c * hid_rows) // 128, 53)
    hid_rest = c * hid_rows - hid_tile * 128
    loads = [
        pltpu.make_async_copy(lat_h, LATN, s_in.at[0]),
        pltpu.make_async_copy(
            hid_h.at[:, pl.ds(pl.multiple_of(hid_tile * 128, 128), 384)], HIDW, s_in.at[1]
        ),
        pltpu.make_async_copy(ww_h, WWT, s_in.at[2]),
        pltpu.make_async_copy(wq_h, WQ, s_in.at[3]),
        pltpu.make_async_copy(mq_h, MQL, s_in.at[4]),
        pltpu.make_async_copy(mk_h, K1, s_in.at[5]),
        pltpu.make_async_copy(ik_h, IK1, s_in.at[6]),
    ]
    for one in loads:
        one.start()

    def g_dev(gg):
        return {"dp": b, "head": yh, "ctx": (gg // 2) * 4 + yl * 2 + gg % 2}

    def y_dev(yy):
        return {"dp": b, "head": yy // 2, "ctx": z * 4 + (yy % 2) * 2 + core}

    def x_dev(bb):
        return {"dp": bb, "head": yh, "ctx": c}

    def by_dev(n):
        yy = n % 4
        return {"dp": n // 4, "head": yy // 2, "ctx": z * 4 + (yy % 2) * 2 + core}

    def a_dev(zz, uu):
        return {"dp": b, "head": yh, "ctx": zz * 4 + uu}

    def zm(v):
        return lax.rem(v + 16, 8)

    def others(n, me, start):
        loop(1, n, lambda d: start(lax.rem(me + d, n)))

    bar = pltpu.get_barrier_semaphore()

    def hello(dev):
        pl.semaphore_signal(bar, inc=1, device_id=dev, device_id_type=MESH)

    others(16, g, lambda gg: hello(g_dev(gg)))
    others(16, by, lambda n: hello(by_dev(n)))

    def not_self(t, uu):
        return jnp.logical_or(b > 0, jnp.logical_or(t > 0, uu != u))

    def hello_a(i):
        t, uu = i // 4, i % 4

        @pl.when(not_self(t, uu))
        def _():
            hello(a_dev(zm(z - b - 4 * t), uu))
            hello(a_dev(zm(z + b + 4 * t), uu))

    loop(0, 8, hello_a)

    row64 = lax.broadcasted_iota(jnp.int32, (64, 64), 0)
    col64 = lax.broadcasted_iota(jnp.int32, (64, 64), 1)

    def natural(r):
        return ((r >> 1) & 7) * 8 + ((r >> 4) & 1) * 4 + (r & 1) * 2 + (r >> 5)

    perm = jnp.where(natural(row64) == col64, 1.0, 0.0).astype(BF)
    WWF[...] = jnp.zeros_like(WWF)
    loads[0].wait()
    lat = dot(perm, LATN[...]).astype(BF)
    for p in range(8):
        LAT8[p] = lat[:, p * 192:(p + 1) * 192]
    loads[1].wait()
    loads[2].wait()
    WWF[pl.ds(pl.multiple_of(yh * 32, 32), 32), :] = WWT[...]
    sel_row = lax.broadcasted_iota(jnp.int32, (384, hid_rows), 0)
    sel_col = lax.broadcasted_iota(jnp.int32, (384, hid_rows), 1)
    sel = jnp.where(sel_row == sel_col + hid_rest, 1.0, 0.0).astype(BF)
    HID[...] = dot(perm, dot(HIDW[...], sel).astype(BF)).astype(BF)
    HWL[...] = dot(HID[...], WWF[...], NT).reshape(4, 16, 128)
    for one in loads[3:]:
        one.wait()
    pl.semaphore_wait(bar, jnp.where(b == 0, 44, 46))

    def w_copy(t, uu, slot):
        zd = zm(z - b - 4 * t)
        cols = pl.ds(pl.multiple_of((zd * 4 + uu) * 128, 128), 128)
        return remote(
            WQ.at[:, cols], WB.at[t, u], s_w.at[t * 4 + uu], r_w.at[t * 4 + slot], a_dev(zd, uu)
        )

    def pj_copy(n, slot):
        return remote(PJ.at[n], IQP.at[slot], s_pj.at[n], r_pj.at[slot], by_dev(n))

    def iqz_copy(zz, slot):
        return remote(IQY, IQG.at[core, slot], s_iqg.at[zz], r_iqg.at[slot], a_dev(zz, u))

    def hwz_copy(zz, slot):
        return remote(HWS, HWG.at[slot], s_hwg.at[zz], r_hwg.at[slot], a_dev(zz, u))

    def hwy_copy(yy, slot):
        return remote(HWL.at[yy], HWY.at[slot], s_hwy.at[yy], r_hwy.at[slot], y_dev(yy))

    def st_copy(gg, slot):
        return remote(ST, STG.at[slot], s_st.at[gg], r_st.at[slot], g_dev(gg))

    def si_copy(gg, slot):
        return remote(SI, SIG.at[slot], s_si.at[gg], r_si.at[slot], g_dev(gg))

    def rs_copy(gg, slot):
        return remote(RSB.at[gg], RSR.at[slot], s_rs.at[gg], r_rs.at[slot], g_dev(gg))

    def wg_copy(gg, slot):
        return remote(WGP, WGR.at[slot], s_wg.at[gg], r_wg.at[slot], g_dev(gg))

    def dq_copy(n, slot):
        return remote(DISP.at[n % 4], QGA.at[slot], s_dq.at[n], r_dq.at[slot], by_dev(n))

    def dw_copy(n, slot):
        return remote(WGS, WGA.at[slot], s_dw.at[n], r_dw.at[slot], by_dev(n))

    def lx_copy(bb, t, slot):
        return remote(
            LAT8.at[zm(z + bb + 4 * t)], LTF.at[t, slot],
            s_lx.at[bb * 2 + t], r_lx.at[slot * 2 + t], x_dev(bb),
        )

    def hx_copy(bb, slot):
        return remote(HID, HTX.at[slot], s_hx.at[bb], r_hx.at[slot], x_dev(bb))

    def out_cols(zz, uu, n):
        return pl.ds(pl.multiple_of((zz * 4 + uu) * 128, 128), n * 128)

    def o_copy(t, uu):
        return remote(
            OUTP.at[t, uu], out_q.at[:, out_cols(z, u, 1)], s_o.at[t * 4 + uu], r_o.at[t * 4 + u],
            a_dev(zm(z + b + 4 * t), uu),
        )

    def o_arrival(t, uu):
        zz = zm(z - b - 4 * t)
        return remote(
            OUTP.at[t, uu], out_q.at[:, out_cols(zz, uu, 1)], s_o.at[t * 4 + uu],
            r_o.at[t * 4 + uu], a_dev(zz, uu),
        )

    def ox_copy(bb, t):
        cols = out_cols(zm(z - b - 4 * t), 0, 4)
        return remote(
            out_q.at[:, cols], out_q.at[:, cols], s_ox.at[bb * 2 + t], r_ox.at[b * 2 + t], x_dev(bb)
        )

    def ox_arrival(bb, t):
        cols = out_cols(zm(z - bb - 4 * t), 0, 4)
        return remote(
            out_q.at[:, cols], out_q.at[:, cols], s_ox.at[bb * 2 + t], r_ox.at[bb * 2 + t], x_dev(bb)
        )

    twin = {"dp": b, "head": yh, "ctx": z * 4 + yl * 2 + (1 - core)}
    iqt_copy = remote(IQG.at[core], IQG.at[core], s_iqt.at[0], r_iqt.at[0], twin)
    hwt_copy = remote(HWC, HWT, s_hwt.at[0], r_hwt.at[0], twin)
    hops = {
        "a": ((0, 1), (0, -1), (-1, 1), (1, -1), (-2, 1), (-2, 2), (2, -1)),
        "b": ((0, 2), (0, -2), (0, 1), (0, -1), (-2, 1), (2, -1), (2, -2)),
    }

    places = {0: 0, 1: 1, -1: 2, 2: 3, -2: 4, 3: 5, -3: 6, 4: 7, -4: 7}

    def piece(of, kind):
        return MQ.at[places[of], core, yh if kind == "a" else 1 - yh]

    def hop(kind, n):
        of, far_by = hops[kind][n]
        ss, rs = (s_qa, r_qa) if kind == "a" else (s_qb, r_qb)
        there = of - far_by
        return remote(
            piece(of, kind), piece(there, kind), ss.at[n], rs.at[places[there]],
            a_dev(zm(z + far_by), u),
        )

    def arrival(kind, of):
        ss, rs = (s_qa, r_qa) if kind == "a" else (s_qb, r_qb)
        here = piece(of, kind)
        remote(here, here, ss.at[0], rs.at[places[of]], a_dev(zm(z + of), u)).wait_recv()
        to_twin(places[of], kind).start()

    def to_twin(k, kind):
        ss, rs = (s_ca, r_ca) if kind == "a" else (s_cb, r_cb)
        here = MQ.at[k, core, yh if kind == "a" else 1 - yh]
        return remote(here, here, ss.at[k], rs.at[k], twin)

    partner = {"dp": b, "head": 1 - yh, "ctx": c}
    mp_copy = remote(MQL.at[1 - yh], MQ.at[0, core, yh], s_mp.at[0], r_mp.at[0], partner)
    up = y_dev(lax.rem(y + 1, 4))
    down = y_dev(lax.rem(y + 3, 4))

    def ik_copy(h):
        return remote(
            IK1.at[h * 4:(h + 1) * 4], IK2.at[:, h], s_ik.at[h], r_ik.at[h], down if h else up
        )

    def k_copy(h, i):
        return remote(
            K1.at[:, pl.ds(pl.multiple_of(h * 512 + i * 128, 128), 128)],
            K2.at[i, :, h * 128:(h + 1) * 128],
            s_k.at[h * 4 + i], r_k.at[h * 4 + i], down if h else up,
        )

    def w_start(i):
        t, uu = i // 4, i % 4

        @pl.when(not_self(t, uu))
        def _():
            w_copy(t, uu, u).start()

    loop(0, 8, w_start)
    mp_copy.start()
    others(4, b, lambda bb: [lx_copy(bb, t, b).start() for t in range(2)])
    MQ[0, core, yh] = MQL[yh]
    for n in range(2):
        hop("a", n).start()
    to_twin(0, "a").start()
    others(4, y, lambda yy: hwy_copy(yy, y).start())

    def k_start(i):
        k_copy(0, i).start()
        k_copy(1, i).start()

    k_start(0)
    k_start(1)
    HWY[y] = HWL[y]

    @pl.when(b == 0)
    def _():
        WB[0, u] = WQ[:, pl.ds(pl.multiple_of(c * 128, 128), 128)]

    for t in range(2):
        LTF[t, b] = LAT8[zm(z + b + 4 * t)]
    HTX[b] = HID[...]
    MA[...] = jnp.zeros_like(MA)
    LA[...] = jnp.zeros_like(LA)

    mp_copy.wait_recv()
    for n in range(4):
        hop("b", n).start()
    to_twin(0, "b").start()
    for of, n in ((-1, 2), (1, 3)):
        arrival("a", of)
        hop("a", n).start()

    lane = lax.broadcasted_iota(jnp.int32, (128, 128), 1)
    near_row = lax.broadcasted_iota(jnp.int32, (1, 1024), 1) + c * 1024
    col256 = lax.broadcasted_iota(jnp.int32, (1, 256), 1)
    far_row = (z * 4 + (1 - yl) * 2 + core) * 1024 + (col256 >> 7) * 512 + (col256 & 127)

    def position(slot):
        return pos_s[0, (slot // 2) * 8 + (slot % 2) * 2 + 4 * yl + yh]

    def plane(k):
        return zm(z + jnp.where(lax.rem(k, 2) == 1, (k + 1) // 2, -(k // 2)))

    def scores(k, count, keys, key_row, part, cols):
        q = MQ[pl.ds(k, count)].reshape(count * 256, DL)
        s = dot(q, keys)
        ma, la = MA[...], LA[...]
        for i in range(count * 2):
            slot = plane(k + i // 2) * 2 + i % 2
            vis = key_row <= position(slot)
            si = jnp.where(vis, s[i * 128:(i + 1) * 128], FLOOR)
            m = jnp.maximum(jnp.max(si, axis=1, keepdims=True), LOW)
            e = jnp.exp2((si - m) * C2)
            E[slot, :, cols] = e
            here = lane == part * 16 + slot
            ma = jnp.where(here, m, ma)
            la = jnp.where(here, jnp.sum(e, axis=1, keepdims=True), la)
        MA[...] = ma
        LA[...] = la

    def near(k, count):
        for i in range(k, k + count):
            to_twin(i, "a").wait_recv()
            to_twin(i, "b").wait_recv()
        scores(k, count, K1[...], near_row, 0, pl.ds(0, 1024))

    def w_wait(i):
        t, uu = i // 4, i % 4

        @pl.when(not_self(t, uu))
        def _():
            w_copy(t, uu, uu).wait_recv()

    loop(0, 8, w_wait)
    others(4, b, lambda bb: [lx_copy(bb, t, bb).wait_recv() for t in range(2)])
    PJ[...] = (
        dot(LTF[0].reshape(256, 192), WB[0].reshape(192, 128))
        + dot(LTF[1].reshape(256, 192), WB[1].reshape(192, 128))
    ).reshape(16, 16, 128)
    others(16, by, lambda n: pj_copy(n, by).start())
    k_start(2)
    k_start(3)
    for h in range(2):
        ik_copy(h).start()
    IQP[by] = PJ[by]

    for of, first, last in ((-2, 4, 6), (2, 6, 7)):
        arrival("a", of)
        for n in range(first, last):
            hop("a", n).start()
    others(4, y, lambda yy: hwy_copy(yy, yy).wait_recv())
    hw = HWY[0] + HWY[1] + HWY[2] + HWY[3]
    HWS[...] = jnp.concatenate([hw[0:8, 0:64], hw[8:16, 0:64]], axis=1)
    others(8, z, lambda zz: hwz_copy(zz, z).start())
    HWG[z] = HWS[...]
    others(4, b, lambda bb: hx_copy(bb, b).start())
    near(0, 1)
    for of, n in ((-2, 4), (2, 5)):
        arrival("b", of)
        hop("b", n).start()
        if of == 2:
            hop("b", 6).start()
    arrival("b", -1)
    arrival("b", 1)
    others(16, by, lambda n: pj_copy(n, n).wait_recv())
    for ys in range(4):
        IQY[ys] = (IQP[ys] + IQP[4 + ys] + IQP[8 + ys] + IQP[12 + ys]).astype(BF)
    others(8, z, lambda zz: iqz_copy(zz, z).start())
    IQG[core, z] = IQY[...]

    near(1, 4)

    def far(i, k, count):
        cols = pl.ds(pl.multiple_of(1024 + i * 256, 256), 256)
        scores(k, count, K2[i], far_row + i * 128, 1 + i, cols)

    def far_early(i):
        k_copy(0, i).wait_recv()
        k_copy(1, i).wait_recv()
        far(i, 0, 5)

    loop(0, 4, far_early)
    for kind in ("a", "b"):
        for of in (-3, 3, 4):
            arrival(kind, of)
    others(8, z, lambda zz: hwz_copy(zz, zz).wait_recv())
    hw = HWG[0]
    for zz in range(1, 8):
        hw = hw + HWG[zz]
    HWC[...] = hw
    hwt_copy.start()
    others(8, z, lambda zz: iqz_copy(zz, zz).wait_recv())
    iqt_copy.start()
    near(5, 3)
    loop(0, 4, lambda i: far(i, 5, 3))
    MS[...] = MA[...].T
    sums = LA[...].T
    tops = [MS[16 * p:16 * (p + 1)] for p in range(5)]
    mx = tops[0]
    for p in range(1, 5):
        mx = jnp.maximum(mx, tops[p])
    total = jnp.zeros((16, 128), F32)
    for p in range(5):
        total = total + sums[16 * p:16 * (p + 1)] * jnp.exp2((tops[p] - mx) * C2)
    ST[...] = mx * C2 + log2(jnp.maximum(total, 1e-37))
    others(16, g, lambda gg: st_copy(gg, g).start())
    STG[g] = ST[...]

    hwt_copy.wait_recv()
    hw = (HWC[...] + HWT[...]) * ISCALE
    hw = jnp.concatenate([hw[:, 0:64], hw[:, 64:128]], axis=0)
    for p in range(64):
        cs, zs, ys = p // 32, (p // 4) % 8, p % 4
        j = (ys // 2) * 32 + zs * 4 + (ys % 2) * 2 + cs
        HB[p] = jnp.broadcast_to(hw[:, j:j + 1], (16, 128))
    sub256 = lax.broadcasted_iota(jnp.int32, (16, 256), 0)
    posq = jnp.zeros((16, 256), jnp.int32)
    for slot in range(16):
        posq = jnp.where(sub256 == slot, position(slot), posq)
    iqt_copy.wait_recv()
    for h in range(2):
        ik_copy(h).wait_recv()

    def index_tile(kt, tile, key_row):
        aff = dot(IQG[...].reshape(1024, 128), kt.reshape(256, 128), NT)
        AFF[tile] = aff.reshape(2, 512, 256)
        total = jnp.zeros((16, 256), F32)
        for p in range(64):
            hb = HB[p]
            total = total + jnp.maximum(aff[p * 16:(p + 1) * 16], 0.0) * jnp.concatenate([hb, hb], axis=1)
        LM[tile] = jnp.where(key_row <= posq, total * LOG2E, FLOOR)

    loop(0, 4, lambda i: index_tile(IK1[pl.ds(i * 2, 2)], i, col256 + (c * 1024 + i * 256)))
    loop(0, 4, lambda i: index_tile(IK2[i], i + 4, far_row + i * 128))
    lm = LM[...]
    im = jnp.maximum(jnp.max(jnp.max(lm, axis=0), axis=1, keepdims=True), LOW)
    il = jnp.sum(jnp.sum(jnp.exp2(lm - im[None]), axis=0), axis=1, keepdims=True)
    lane16 = lax.broadcasted_iota(jnp.int32, (16, 128), 1)
    diag = lane16 == lax.broadcasted_iota(jnp.int32, (16, 128), 0)
    il = im + log2(jnp.maximum(il, 1e-37))
    SI[...] = jnp.broadcast_to(jnp.sum(jnp.where(diag, il, 0.0), axis=0, keepdims=True), (8, 128))
    others(16, g, lambda gg: si_copy(gg, g).start())
    SIG[g] = SI[...]

    others(16, g, lambda gg: st_copy(gg, gg).wait_recv())
    stats = STG[...]
    top = jnp.max(stats, axis=0)
    lse = top + log2(jnp.sum(jnp.exp2(stats - top[None]), axis=0))
    weights = [jnp.exp2(MS[16 * p:16 * (p + 1)] * C2 - lse) * (1.0 / HM) for p in range(5)]
    MA[...] = jnp.concatenate(weights + [jnp.zeros((48, 128), F32)], axis=0).T

    def target(slot):
        for p in range(5):
            w = jnp.sum(jnp.where(lane == p * 16 + slot, MA[...], 0.0), axis=1, keepdims=True)
            lo, hi = (0, 1024) if p == 0 else (768 + 256 * p, 1024 + 256 * p)
            row = jnp.sum(E[slot, :, lo:hi] * w, axis=0, keepdims=True)
            for t in range(lo // 256, hi // 256):
                T[t, pl.ds(slot, 1), :] = row[:, t * 256 - lo:t * 256 - lo + 256]

    loop(0, 16, target)
    others(16, g, lambda gg: si_copy(gg, gg).wait_recv())
    istats = SIG[...]
    itop = jnp.max(istats, axis=0)
    li = (itop + log2(jnp.sum(jnp.exp2(istats - itop[None]), axis=0)))[0:1]
    li = jnp.sum(jnp.where(diag, li, 0.0), axis=1, keepdims=True)
    loss = jnp.zeros((16, 1), F32)
    for t in range(8):
        shifted = LM[t] - li
        tt = T[t]
        loss = loss - jnp.sum(tt * shifted, axis=1, keepdims=True) * LN2
        T[t] = jnp.exp2(shifted) - tt

    WGP[...] = jnp.where(lane16 == 64, loss, 0.0)

    def back(i):
        for h in range(2):
            zz = zm(z + 4 - 2 * i - h)
            rows = pl.ds(pl.multiple_of(zz * 64, 64), 64)
            accs = []
            for cs in range(2):
                hb = HB[pl.ds(cs * 32 + zz * 4, 4)]
                hb = jnp.concatenate([hb, hb], axis=2)
                acc = jnp.zeros((4, 16, 128), F32)
                for t in range(8):
                    aff = AFF[t, cs, rows, :].reshape(4, 16, 256)
                    delta = T[t][None]
                    sg = jnp.where(aff > 0.0, delta * hb, 0.0)
                    top_row = h * 128 + cs * 64
                    SG[t, top_row:top_row + 64, :] = sg.reshape(64, 256).astype(BF)
                    prod = delta * jnp.maximum(aff, 0.0)
                    acc = acc + prod[:, :, 0:128] + prod[:, :, 128:256]
                accs.append(acc)
            acc = jnp.concatenate(accs, axis=0)
            got = jnp.sum(acc, axis=2, keepdims=True) * ISCALE
            wg = WGP[...]
            for n in range(8):
                cs, ys = n // 4, n % 4
                j = (ys // 2) * 32 + zz * 4 + (ys % 2) * 2 + cs
                wg = jnp.where(lane16 == j, got[n], wg)
            WGP[...] = wg
        total = jnp.zeros((256, 128), F32)
        for t in range(8):
            kt = IK1[2 * t:2 * t + 2] if t < 4 else IK2[t - 4]
            total = total + dot(SG[t], kt.reshape(256, 128))
        for h in range(2):
            zz = zm(z + 4 - 2 * i - h)
            part = total[h * 128:(h + 1) * 128].reshape(2, 4, 16, 128)
            RSB[pl.ds(zz * 2, 2)] = part.astype(BF)
            for cs in range(2):
                gg = zz * 2 + cs

                @pl.when(gg != g)
                def _():
                    rs_copy(gg, g).start()

    loop(0, 4, back)
    others(16, g, lambda gg: wg_copy(gg, g).start())
    WGR[g] = WGP[...]
    RSR[g] = RSB[g]

    mp_copy.wait_send()
    for h in range(2):
        ik_copy(h).wait_send()

    def k_sent(i):
        k_copy(0, i).wait_send()
        k_copy(1, i).wait_send()

    loop(0, 4, k_sent)
    for n in range(7):
        hop("a", n).wait_send()
        hop("b", n).wait_send()
    iqt_copy.wait_send()
    hwt_copy.wait_send()

    def twins(zz):
        to_twin(zz, "a").wait_send()
        to_twin(zz, "b").wait_send()

    loop(0, 8, twins)

    def w_sent(i):
        t, uu = i // 4, i % 4

        @pl.when(not_self(t, uu))
        def _():
            w_copy(t, uu, u).wait_send()

    loop(0, 8, w_sent)

    def x_sent(bb):
        hx_copy(bb, b).wait_send()
        for t in range(2):
            lx_copy(bb, t, b).wait_send()

    others(4, b, x_sent)
    others(4, y, lambda yy: hwy_copy(yy, y).wait_send())

    def g_sent(gg):
        st_copy(gg, g).wait_send()
        si_copy(gg, g).wait_send()

    others(16, g, g_sent)

    def z_sent(zz):
        iqz_copy(zz, z).wait_send()
        hwz_copy(zz, z).wait_send()

    others(8, z, z_sent)
    others(16, by, lambda n: pj_copy(n, by).wait_send())

    others(16, g, lambda gg: rs_copy(gg, gg).wait_recv())
    qg = RSR[0].astype(F32)
    for gg in range(1, 16):
        qg = qg + RSR[gg].astype(F32)
    DISP[...] = qg.astype(BF)
    others(16, by, lambda n: dq_copy(n, by).start())
    QGA[by] = DISP[y]

    others(16, by, lambda n: dq_copy(n, n).wait_recv())
    for t in range(2):
        o = dot(LTF[t].reshape(256, 192), QGA[...].reshape(256, 128), TN)
        OUTP[t] = o.astype(BF).reshape(4, 48, 128)
        for uu in range(4):

            @pl.when(not_self(t, uu))
            def _():
                o_copy(t, uu).start()

    @pl.when(b == 0)
    def _():
        out_q[:, out_cols(z, u, 1)] = OUTP[0, u]

    others(16, g, lambda gg: wg_copy(gg, gg).wait_recv())
    wg = WGR[0]
    for gg in range(1, 16):
        wg = wg + WGR[gg]
    WGS[...] = wg
    others(16, by, lambda n: dw_copy(n, by).start())
    WGA[by] = WGS[...]
    for t in range(2):
        for uu in range(4):

            @pl.when(not_self(t, uu))
            def _():
                o_arrival(t, uu).wait_recv()

        others(4, b, lambda bb: ox_copy(bb, t).start())

    others(4, b, lambda bb: hx_copy(bb, bb).wait_recv())
    others(16, by, lambda n: dw_copy(n, n).wait_recv())
    wg_all = WGA[...].reshape(256, 128)
    GWT[...] = dot(wg_all.astype(BF), HTX[...].reshape(256, hid_rows), TN)
    out_w[...] = GWT[pl.ds(pl.multiple_of(yh * 32, 32), 32), :]
    own = WGA[pl.ds(b * 4, 4)].reshape(64, 128)
    row = lax.broadcasted_iota(jnp.int32, (64, 128), 0)
    col = lax.broadcasted_iota(jnp.int32, (64, 128), 1)
    losses = jnp.where(natural(row) == col, own[:, 64:65], 0.0)
    out_l[...] = jnp.sum(losses, axis=0, keepdims=True)[:, 0:64]

    def g_left(gg):
        rs_copy(gg, g).wait_send()
        wg_copy(gg, g).wait_send()

    others(16, g, g_left)

    def by_left(n):
        dq_copy(n, by).wait_send()
        dw_copy(n, by).wait_send()

    others(16, by, by_left)
    for t in range(2):
        for uu in range(4):

            @pl.when(not_self(t, uu))
            def _():
                o_copy(t, uu).wait_send()

    for t in range(2):
        others(4, b, lambda bb: ox_arrival(bb, t).wait_recv())
    for t in range(2):
        others(4, b, lambda bb: ox_copy(bb, t).wait_send())


def per_device(
    q_latent, hidden, main_queries, main_keys, index_keys, positions, w_query, w_weights
):
    hid_rows = w_weights.shape[0]
    vm = pl.BlockSpec(memory_space=pltpu.VMEM)
    hbm = pl.BlockSpec(memory_space=pl.ANY)
    dma = pltpu.SemaphoreType.DMA
    sems = [dma((7,))]
    for n in (8, 16, 8, 4, 8, 1, 1, 1, 8, 8, 8, 8, 2, 8, 16, 16, 16, 16, 16, 16, 8, 4, 8, 8):
        sems += [dma((n,)), dma((n,))]
    out_q, out_w, out_l = pl.pallas_call(
        kernel,
        out_shape=(
            jax.ShapeDtypeStruct((48, 4096), BF),
            jax.ShapeDtypeStruct((32, hid_rows), F32),
            jax.ShapeDtypeStruct((1, 64), F32),
        ),
        in_specs=[pl.BlockSpec(memory_space=pltpu.SMEM)] + [hbm] * 7,
        out_specs=(vm, vm, vm),
        scratch_shapes=[
            pltpu.VMEM((64, 1536), BF),
            pltpu.VMEM((64, 384), BF),
            pltpu.VMEM((2, 64, DL), BF),
            pltpu.VMEM((DL, 1024), BF),
            pltpu.VMEM((8, 128, DI), BF),
            pltpu.VMEM((48, 4096), BF),
            pltpu.VMEM((32, hid_rows), BF),
            pltpu.VMEM((128, hid_rows), BF),
            pltpu.VMEM((8, 64, 192), BF),
            pltpu.VMEM((64, hid_rows), BF),
            pltpu.VMEM((2, 4, 64, 192), BF),
            pltpu.VMEM((4, 64, hid_rows), BF),
            pltpu.VMEM((2, 4, 48, 128), BF),
            pltpu.VMEM((16, 16, 128), F32),
            pltpu.VMEM((16, 16, 128), F32),
            pltpu.VMEM((4, 16, 128), BF),
            pltpu.VMEM((2, 8, 4, 16, 128), BF),
            pltpu.VMEM((4, 16, 128), F32),
            pltpu.VMEM((4, 16, 128), F32),
            pltpu.VMEM((8, 128), F32),
            pltpu.VMEM((8, 8, 128), F32),
            pltpu.VMEM((8, 128), F32),
            pltpu.VMEM((8, 128), F32),
            pltpu.VMEM((64, 16, 128), F32),
            pltpu.VMEM((8, 2, 2, 64, DL), BF),
            pltpu.VMEM((4, DL, 256), BF),
            pltpu.VMEM((4, 2, 128, DI), BF),
            pltpu.VMEM((16, 128, 2048), F32),
            pltpu.VMEM((128, 128), F32),
            pltpu.VMEM((128, 128), F32),
            pltpu.VMEM((128, 128), F32),
            pltpu.VMEM((16, 128), F32),
            pltpu.VMEM((16, 16, 128), F32),
            pltpu.VMEM((8, 128), F32),
            pltpu.VMEM((16, 8, 128), F32),
            pltpu.VMEM((8, 2, 512, 256), F32),
            pltpu.VMEM((8, 16, 256), F32),
            pltpu.VMEM((8, 16, 256), F32),
            pltpu.VMEM((8, 256, 256), BF),
            pltpu.VMEM((16, 4, 16, 128), BF),
            pltpu.VMEM((16, 4, 16, 128), BF),
            pltpu.VMEM((16, 128), F32),
            pltpu.VMEM((16, 16, 128), F32),
            pltpu.VMEM((4, 16, 128), BF),
            pltpu.VMEM((16, 16, 128), BF),
            pltpu.VMEM((16, 128), F32),
            pltpu.VMEM((16, 16, 128), F32),
            pltpu.VMEM((2, 4, 48, 128), BF),
            pltpu.VMEM((128, hid_rows), F32),
        ]
        + sems,
        compiler_params=pltpu.CompilerParams(
            collective_id=0, has_side_effects=True, vmem_limit_bytes=56 * 1024 * 1024
        ),
        name="indexer_step",
    )(
        positions, q_latent[0], hidden[0], main_queries[0], main_keys[0].T,
        index_keys[0].reshape(8, 128, DI), w_query, w_weights.T,
    )
    return out_q.astype(F32), out_w.T, out_l


def solution(mesh):
    return jax.shard_map(
        per_device,
        mesh=mesh,
        in_specs=(
            P("dp", None, None),
            P("dp", None, None),
            P("dp", "ctx", "head", None),
            P("dp", "ctx", None),
            P("dp", "ctx", None),
            P("dp", None),
            P("ctx", "head"),
            P("ctx", "head"),
        ),
        out_specs=(P("ctx", "head"), P("ctx", "head"), P("dp", None)),
        check_vma=False,
    )
```

```python
import jax
import jax.numpy as jnp
from jax import lax
from jax.experimental import pallas as pl
from jax.experimental.pallas import tpu as pltpu
from jax.sharding import PartitionSpec as P

HI = 64
DI = 128
HM = 128
DL = 576
MESH = pl.DeviceIdType.MESH
BF = jnp.bfloat16
F32 = jnp.float32

LOG2E = 1.4426950408889634
LN2 = 0.6931471805599453
C2 = 192.0 ** (-0.5) * LOG2E
ISCALE = (HI * DI) ** (-0.5)
FLOOR = -1e30
LOW = -1e29

NT = (((1,), (1,)), ((), ()))
NN = (((1,), (0,)), ((), ()))
TN = (((0,), (0,)), ((), ()))


def dot(a, b, dims=NN):
    return lax.dot_general(a, b, dims, preferred_element_type=F32)


def log2(x):
    return jnp.log(x) * LOG2E


def remote(src, dst, ss, rs, dev):
    return pltpu.make_async_remote_copy(
        src_ref=src, dst_ref=dst, send_sem=ss, recv_sem=rs, device_id=dev, device_id_type=MESH
    )


def loop(lo, hi, body):
    def turn(i, carry):
        body(i)
        return carry

    lax.fori_loop(lo, hi, turn, 0)


def kernel(
    pos_s, lat_h, hid_h, mq_h, mk_h, ik_h, wq_h, ww_h,
    out_q, out_w, out_l,
    LATN, HIDW, MQL, PK, QS, K1, IK1, WQ, WWT, WWF, LAT8, HID, LTF, HTX, WB, PJ, IQP, IQY, IQG,
    HWL, HWY, HWS, HWG, HWC, HWT, HB, MQ, K2, IK2, E, MA, LA, MS, ST, STG, SI, SIG, AFF, LM, T, SG,
    RSB, RSR, WGP, WGR, DISP, QGA, WGS, WGA, OUTP, GWT,
    s_in,
    s_w, r_w, s_pj, r_pj, s_iqg, r_iqg, s_hwy, r_hwy, s_hwg, r_hwg,
    s_iqt, r_iqt, s_hwt, r_hwt, s_mp, r_mp, s_qa, r_qa, s_qb, r_qb, s_ca, r_ca, s_cb, r_cb,
    s_ik, r_ik, s_k, r_k, s_st, r_st, s_si, r_si, s_rs, r_rs, s_wg, r_wg, s_dq, r_dq, s_dw, r_dw,
    s_lx, r_lx, s_hx, r_hx, s_o, r_o, s_ox, r_ox,
):
    b = lax.axis_index("dp")
    yh = lax.axis_index("head")
    c = lax.axis_index("ctx")
    z = c // 4
    yl = (c // 2) % 2
    core = c % 2
    y = yh * 2 + yl
    u = yl * 2 + core
    g = z * 2 + core
    by = b * 4 + y
    hid_rows = ww_h.shape[1]

    hid_tile = jnp.minimum((c * hid_rows) // 128, 53)
    hid_rest = c * hid_rows - hid_tile * 128
    loads = [
        pltpu.make_async_copy(lat_h, LATN, s_in.at[0]),
        pltpu.make_async_copy(
            hid_h.at[:, pl.ds(pl.multiple_of(hid_tile * 128, 128), 384)], HIDW, s_in.at[1]
        ),
        pltpu.make_async_copy(ww_h, WWT, s_in.at[2]),
        pltpu.make_async_copy(wq_h, WQ, s_in.at[3]),
        pltpu.make_async_copy(mq_h, MQL, s_in.at[4]),
        pltpu.make_async_copy(mk_h, K1, s_in.at[5]),
        pltpu.make_async_copy(ik_h, IK1, s_in.at[6]),
    ]
    def g_dev(gg):
        return {"dp": b, "head": yh, "ctx": (gg // 2) * 4 + yl * 2 + gg % 2}

    def y_dev(yy):
        return {"dp": b, "head": yy // 2, "ctx": z * 4 + (yy % 2) * 2 + core}

    def x_dev(bb):
        return {"dp": bb, "head": yh, "ctx": c}

    def by_dev(n):
        yy = n % 4
        return {"dp": n // 4, "head": yy // 2, "ctx": z * 4 + (yy % 2) * 2 + core}

    def a_dev(zz, uu):
        return {"dp": b, "head": yh, "ctx": zz * 4 + uu}

    def zm(v):
        return lax.rem(v + 16, 8)

    def others(n, me, start):
        def turn(i):
            d = n // 2 + jnp.where(lax.rem(i, 2) == 1, (i + 1) // 2, -(i // 2))
            start(lax.rem(me + d, n))

        loop(0, n - 1, turn)

    bar = pltpu.get_barrier_semaphore()

    def hello(dev):
        pl.semaphore_signal(bar, inc=1, device_id=dev, device_id_type=MESH)

    others(16, g, lambda gg: hello(g_dev(gg)))
    others(16, by, lambda n: hello(by_dev(n)))

    def not_self(t, uu):
        return jnp.logical_or(b > 0, jnp.logical_or(t > 0, uu != u))

    def hello_a(i):
        t, uu = i // 4, i % 4

        @pl.when(not_self(t, uu))
        def _():
            hello(a_dev(zm(z - b - 4 * t), uu))
            hello(a_dev(zm(z + b + 4 * t), uu))

    loop(0, 8, hello_a)
    for one in loads:
        one.start()

    row64 = lax.broadcasted_iota(jnp.int32, (64, 64), 0)
    col64 = lax.broadcasted_iota(jnp.int32, (64, 64), 1)

    def natural(r):
        return ((r >> 1) & 7) * 8 + ((r >> 4) & 1) * 4 + (r & 1) * 2 + (r >> 5)

    perm = jnp.where(natural(row64) == col64, 1.0, 0.0).astype(BF)
    WWF[...] = jnp.zeros_like(WWF)
    loads[0].wait()
    lat = dot(perm, LATN[...]).astype(BF)
    for p in range(8):
        LAT8[p] = lat[:, p * 192:(p + 1) * 192]
    loads[1].wait()
    loads[2].wait()
    WWF[pl.ds(pl.multiple_of(yh * 32, 32), 32), :] = WWT[...]
    sel_row = lax.broadcasted_iota(jnp.int32, (384, hid_rows), 0)
    sel_col = lax.broadcasted_iota(jnp.int32, (384, hid_rows), 1)
    sel = jnp.where(sel_row == sel_col + hid_rest, 1.0, 0.0).astype(BF)
    HID[...] = dot(perm, dot(HIDW[...], sel).astype(BF)).astype(BF)
    HWL[...] = dot(HID[...], WWF[...], NT).reshape(4, 16, 128)
    for one in loads[3:]:
        one.wait()
    for n in range(2):
        x = MQL[n]
        for p in range(4):
            PK[n, p * 64:(p + 1) * 64] = x[:, p * 128:(p + 1) * 128]
        PK[n, 256:288] = jnp.concatenate([x[0:32, 512:576], x[32:64, 512:576]], axis=1)
    pl.semaphore_wait(bar, jnp.where(b == 0, 44, 46))

    def w_copy(t, uu, slot):
        zd = zm(z - b - 4 * t)
        cols = pl.ds(pl.multiple_of((zd * 4 + uu) * 128, 128), 128)
        return remote(
            WQ.at[:, cols], WB.at[t, u], s_w.at[t * 4 + uu], r_w.at[t * 4 + slot], a_dev(zd, uu)
        )

    def pj_copy(n, slot):
        return remote(PJ.at[n], IQP.at[slot], s_pj.at[n], r_pj.at[slot], by_dev(n))

    def iqz_copy(zz, slot):
        return remote(IQY, IQG.at[core, slot], s_iqg.at[zz], r_iqg.at[slot], a_dev(zz, u))

    def hwz_copy(zz, slot):
        return remote(HWS, HWG.at[slot], s_hwg.at[zz], r_hwg.at[slot], a_dev(zz, u))

    def hwy_copy(yy, slot):
        return remote(HWL.at[yy], HWY.at[slot], s_hwy.at[yy], r_hwy.at[slot], y_dev(yy))

    def st_copy(gg, slot):
        return remote(ST, STG.at[slot], s_st.at[gg], r_st.at[slot], g_dev(gg))

    def si_copy(gg, slot):
        return remote(SI, SIG.at[slot], s_si.at[gg], r_si.at[slot], g_dev(gg))

    def rs_copy(gg, slot):
        return remote(RSB.at[gg], RSR.at[slot], s_rs.at[gg], r_rs.at[slot], g_dev(gg))

    def wg_copy(gg, slot):
        return remote(WGP, WGR.at[slot], s_wg.at[gg], r_wg.at[slot], g_dev(gg))

    def dq_copy(n, slot):
        return remote(DISP.at[n % 4], QGA.at[slot], s_dq.at[n], r_dq.at[slot], by_dev(n))

    def dw_copy(n, slot):
        return remote(WGS, WGA.at[slot], s_dw.at[n], r_dw.at[slot], by_dev(n))

    def lx_copy(bb, t, slot):
        return remote(
            LAT8.at[zm(z + bb + 4 * t)], LTF.at[t, slot],
            s_lx.at[bb * 2 + t], r_lx.at[slot * 2 + t], x_dev(bb),
        )

    def hx_copy(bb, slot):
        return remote(HID, HTX.at[slot], s_hx.at[bb], r_hx.at[slot], x_dev(bb))

    def out_cols(zz, uu, n):
        return pl.ds(pl.multiple_of((zz * 4 + uu) * 128, 128), n * 128)

    def o_copy(t, uu):
        return remote(
            OUTP.at[t, uu], out_q.at[:, out_cols(z, u, 1)], s_o.at[t * 4 + uu], r_o.at[t * 4 + u],
            a_dev(zm(z + b + 4 * t), uu),
        )

    def o_arrival(t, uu):
        zz = zm(z - b - 4 * t)
        return remote(
            OUTP.at[t, uu], out_q.at[:, out_cols(zz, uu, 1)], s_o.at[t * 4 + uu],
            r_o.at[t * 4 + uu], a_dev(zz, uu),
        )

    def ox_copy(bb, t):
        cols = out_cols(zm(z - b - 4 * t), 0, 4)
        return remote(
            out_q.at[:, cols], out_q.at[:, cols], s_ox.at[bb * 2 + t], r_ox.at[b * 2 + t], x_dev(bb)
        )

    def ox_arrival(bb, t):
        cols = out_cols(zm(z - bb - 4 * t), 0, 4)
        return remote(
            out_q.at[:, cols], out_q.at[:, cols], s_ox.at[bb * 2 + t], r_ox.at[bb * 2 + t], x_dev(bb)
        )

    twin = {"dp": b, "head": yh, "ctx": z * 4 + yl * 2 + (1 - core)}
    iqt_copy = remote(IQG.at[core], IQG.at[core], s_iqt.at[0], r_iqt.at[0], twin)
    hwt_copy = remote(HWC, HWT, s_hwt.at[0], r_hwt.at[0], twin)
    hops = {
        "a": ((0, 2), (0, -2), (0, 1), (0, -1), (-2, 1), (2, -1), (-3, 1)),
        "b": ((0, 2), (0, -2), (0, 1), (0, -1), (-2, 1), (2, -1), (2, -2)),
    }

    places = {0: 0, 1: 1, -1: 2, 2: 3, -2: 4, 3: 5, -3: 6, 4: 7, -4: 7}

    def piece(of, kind):
        return MQ.at[places[of], core, yh if kind == "a" else 1 - yh]

    def hop(kind, n):
        of, far_by = hops[kind][n]
        ss, rs = (s_qa, r_qa) if kind == "a" else (s_qb, r_qb)
        there = of - far_by
        return remote(
            piece(of, kind), piece(there, kind), ss.at[n], rs.at[places[there]],
            a_dev(zm(z + far_by), u),
        )

    def arrival(kind, of):
        ss, rs = (s_qa, r_qa) if kind == "a" else (s_qb, r_qb)
        here = piece(of, kind)
        remote(here, here, ss.at[0], rs.at[places[of]], a_dev(zm(z + of), u)).wait_recv()
        to_twin(places[of], kind).start()

    def to_twin(k, kind):
        ss, rs = (s_ca, r_ca) if kind == "a" else (s_cb, r_cb)
        here = MQ.at[k, core, yh if kind == "a" else 1 - yh]
        return remote(here, here, ss.at[k], rs.at[k], twin)

    partner = {"dp": b, "head": 1 - yh, "ctx": c}
    mp_copy = remote(PK.at[1 - yh], MQ.at[0, core, yh], s_mp.at[0], r_mp.at[0], partner)
    up = y_dev(lax.rem(y + 1, 4))
    down = y_dev(lax.rem(y + 3, 4))

    def ik_copy(h):
        return remote(
            IK1.at[h * 4:(h + 1) * 4], IK2.at[:, h], s_ik.at[h], r_ik.at[h], down if h else up
        )

    def k_copy(h, i):
        return remote(
            K1.at[:, pl.ds(pl.multiple_of(h * 512 + i * 128, 128), 128)],
            K2.at[i, :, h * 128:(h + 1) * 128],
            s_k.at[h * 4 + i], r_k.at[h * 4 + i], down if h else up,
        )

    def w_start(i):
        t, uu = i // 4, i % 4

        @pl.when(not_self(t, uu))
        def _():
            w_copy(t, uu, u).start()

    loop(0, 8, w_start)
    mp_copy.start()
    others(4, b, lambda bb: [lx_copy(bb, t, b).start() for t in range(2)])
    MQ[0, core, yh] = PK[yh]
    for n in range(4):
        hop("a", n).start()
    to_twin(0, "a").start()
    others(4, y, lambda yy: hwy_copy(yy, y).start())

    def k_start(i):
        k_copy(0, i).start()
        k_copy(1, i).start()

    k_start(0)
    k_start(1)
    HWY[y] = HWL[y]

    @pl.when(b == 0)
    def _():
        WB[0, u] = WQ[:, pl.ds(pl.multiple_of(c * 128, 128), 128)]

    for t in range(2):
        LTF[t, b] = LAT8[zm(z + b + 4 * t)]
    HTX[b] = HID[...]
    MA[...] = jnp.zeros_like(MA)
    LA[...] = jnp.zeros_like(LA)

    mp_copy.wait_recv()
    for n in range(4):
        hop("b", n).start()
    to_twin(0, "b").start()

    lane = lax.broadcasted_iota(jnp.int32, (128, 128), 1)
    near_row = lax.broadcasted_iota(jnp.int32, (1, 1024), 1) + c * 1024
    col256 = lax.broadcasted_iota(jnp.int32, (1, 256), 1)
    far_row = (z * 4 + (1 - yl) * 2 + core) * 1024 + (col256 >> 7) * 512 + (col256 & 127)

    def position(slot):
        return pos_s[0, (slot // 2) * 8 + (slot % 2) * 2 + 4 * yl + yh]

    def plane(k):
        return zm(z + jnp.where(lax.rem(k, 2) == 1, (k + 1) // 2, -(k // 2)))

    def scores(k, count, keys, key_row, part, cols):
        q = QS[pl.ds(k, count)].reshape(count * 256, DL)
        s = dot(q, keys)
        ma, la = MA[...], LA[...]
        for i in range(count * 2):
            slot = plane(k + i // 2) * 2 + i % 2
            vis = key_row <= position(slot)
            si = jnp.where(vis, s[i * 128:(i + 1) * 128], FLOOR)
            m = jnp.maximum(jnp.max(si, axis=1, keepdims=True), LOW)
            e = jnp.exp2((si - m) * C2)
            E[slot, :, cols] = e
            here = lane == part * 16 + slot
            ma = jnp.where(here, m, ma)
            la = jnp.where(here, jnp.sum(e, axis=1, keepdims=True), la)
        MA[...] = ma
        LA[...] = la

    def near(k, count):
        for i in range(k, k + count):
            to_twin(i, "a").wait_recv()
            to_twin(i, "b").wait_recv()
            for n in range(4):
                x = MQ[i, n // 2, n % 2]
                rows = slice(n * 64, (n + 1) * 64)
                for p in range(4):
                    QS[i, rows, p * 128:(p + 1) * 128] = x[p * 64:(p + 1) * 64]
                rest = jnp.concatenate([x[256:288, 0:64], x[256:288, 64:128]], axis=0)
                QS[i, rows, 512:576] = rest
        scores(k, count, K1[...], near_row, 0, pl.ds(0, 1024))

    def w_wait(i):
        t, uu = i // 4, i % 4

        @pl.when(not_self(t, uu))
        def _():
            w_copy(t, uu, uu).wait_recv()

    loop(0, 8, w_wait)
    others(4, b, lambda bb: [lx_copy(bb, t, bb).wait_recv() for t in range(2)])
    PJ[...] = (
        dot(LTF[0].reshape(256, 192), WB[0].reshape(192, 128))
        + dot(LTF[1].reshape(256, 192), WB[1].reshape(192, 128))
    ).reshape(16, 16, 128)
    others(16, by, lambda n: pj_copy(n, by).start())
    k_start(2)
    k_start(3)
    for h in range(2):
        ik_copy(h).start()
    IQP[by] = PJ[by]

    for of, n in ((-2, 4), (2, 5)):
        arrival("a", of)
        hop("a", n).start()
    arrival("a", -1)
    arrival("a", 1)
    others(4, y, lambda yy: hwy_copy(yy, yy).wait_recv())
    hw = HWY[0] + HWY[1] + HWY[2] + HWY[3]
    HWS[...] = jnp.concatenate([hw[0:8, 0:64], hw[8:16, 0:64]], axis=1)
    others(8, z, lambda zz: hwz_copy(zz, z).start())
    HWG[z] = HWS[...]
    others(4, b, lambda bb: hx_copy(bb, b).start())
    near(0, 1)
    for of, n in ((-2, 4), (2, 5)):
        arrival("b", of)
        hop("b", n).start()
        if of == 2:
            hop("b", 6).start()
    arrival("b", -1)
    arrival("b", 1)
    others(16, by, lambda n: pj_copy(n, n).wait_recv())
    for ys in range(4):
        IQY[ys] = (IQP[ys] + IQP[4 + ys] + IQP[8 + ys] + IQP[12 + ys]).astype(BF)
    others(8, z, lambda zz: iqz_copy(zz, z).start())
    IQG[core, z] = IQY[...]
    arrival("a", -3)
    hop("a", 6).start()

    near(1, 4)

    def far(i, k, count):
        cols = pl.ds(pl.multiple_of(1024 + i * 256, 256), 256)
        scores(k, count, K2[i], far_row + i * 128, 1 + i, cols)

    def far_early(i):
        k_copy(0, i).wait_recv()
        k_copy(1, i).wait_recv()
        far(i, 0, 5)

    loop(0, 4, far_early)
    for kind, of in (("a", 3), ("a", 4), ("b", -3), ("b", 3), ("b", 4)):
        arrival(kind, of)
    others(8, z, lambda zz: hwz_copy(zz, zz).wait_recv())
    hw = HWG[0]
    for zz in range(1, 8):
        hw = hw + HWG[zz]
    HWC[...] = hw
    hwt_copy.start()
    others(8, z, lambda zz: iqz_copy(zz, zz).wait_recv())
    iqt_copy.start()
    near(5, 3)
    loop(0, 4, lambda i: far(i, 5, 3))
    MS[...] = MA[...].T
    sums = LA[...].T
    tops = [MS[16 * p:16 * (p + 1)] for p in range(5)]
    mx = tops[0]
    for p in range(1, 5):
        mx = jnp.maximum(mx, tops[p])
    total = jnp.zeros((16, 128), F32)
    for p in range(5):
        total = total + sums[16 * p:16 * (p + 1)] * jnp.exp2((tops[p] - mx) * C2)
    ST[...] = mx * C2 + log2(jnp.maximum(total, 1e-37))
    others(16, g, lambda gg: st_copy(gg, g).start())
    STG[g] = ST[...]

    hwt_copy.wait_recv()
    hw = (HWC[...] + HWT[...]) * ISCALE
    hw = jnp.concatenate([hw[:, 0:64], hw[:, 64:128]], axis=0)
    for p in range(64):
        cs, zs, ys = p // 32, (p // 4) % 8, p % 4
        j = (ys // 2) * 32 + zs * 4 + (ys % 2) * 2 + cs
        HB[p] = jnp.broadcast_to(hw[:, j:j + 1], (16, 128))
    sub256 = lax.broadcasted_iota(jnp.int32, (16, 256), 0)
    posq = jnp.zeros((16, 256), jnp.int32)
    for slot in range(16):
        posq = jnp.where(sub256 == slot, position(slot), posq)
    iqt_copy.wait_recv()
    for h in range(2):
        ik_copy(h).wait_recv()

    def index_tile(kt, tile, key_row):
        aff = dot(IQG[...].reshape(1024, 128), kt.reshape(256, 128), NT)
        AFF[tile] = aff.reshape(2, 512, 256)
        total = jnp.zeros((16, 256), F32)
        for p in range(64):
            hb = HB[p]
            total = total + jnp.maximum(aff[p * 16:(p + 1) * 16], 0.0) * jnp.concatenate([hb, hb], axis=1)
        LM[tile] = jnp.where(key_row <= posq, total * LOG2E, FLOOR)

    loop(0, 4, lambda i: index_tile(IK1[pl.ds(i * 2, 2)], i, col256 + (c * 1024 + i * 256)))
    loop(0, 4, lambda i: index_tile(IK2[i], i + 4, far_row + i * 128))
    lm = LM[...]
    im = jnp.maximum(jnp.max(jnp.max(lm, axis=0), axis=1, keepdims=True), LOW)
    il = jnp.sum(jnp.sum(jnp.exp2(lm - im[None]), axis=0), axis=1, keepdims=True)
    lane16 = lax.broadcasted_iota(jnp.int32, (16, 128), 1)
    diag = lane16 == lax.broadcasted_iota(jnp.int32, (16, 128), 0)
    il = im + log2(jnp.maximum(il, 1e-37))
    SI[...] = jnp.broadcast_to(jnp.sum(jnp.where(diag, il, 0.0), axis=0, keepdims=True), (8, 128))
    others(16, g, lambda gg: si_copy(gg, g).start())
    SIG[g] = SI[...]

    others(16, g, lambda gg: st_copy(gg, gg).wait_recv())
    stats = STG[...]
    top = jnp.max(stats, axis=0)
    lse = top + log2(jnp.sum(jnp.exp2(stats - top[None]), axis=0))
    weights = [jnp.exp2(MS[16 * p:16 * (p + 1)] * C2 - lse) * (1.0 / HM) for p in range(5)]
    MA[...] = jnp.concatenate(weights + [jnp.zeros((48, 128), F32)], axis=0).T

    def target(slot):
        for p in range(5):
            w = jnp.sum(jnp.where(lane == p * 16 + slot, MA[...], 0.0), axis=1, keepdims=True)
            lo, hi = (0, 1024) if p == 0 else (768 + 256 * p, 1024 + 256 * p)
            row = jnp.sum(E[slot, :, lo:hi] * w, axis=0, keepdims=True)
            for t in range(lo // 256, hi // 256):
                T[t, pl.ds(slot, 1), :] = row[:, t * 256 - lo:t * 256 - lo + 256]

    loop(0, 16, target)
    others(16, g, lambda gg: si_copy(gg, gg).wait_recv())
    istats = SIG[...]
    itop = jnp.max(istats, axis=0)
    li = (itop + log2(jnp.sum(jnp.exp2(istats - itop[None]), axis=0)))[0:1]
    li = jnp.sum(jnp.where(diag, li, 0.0), axis=1, keepdims=True)
    loss = jnp.zeros((16, 1), F32)
    for t in range(8):
        shifted = LM[t] - li
        tt = T[t]
        loss = loss - jnp.sum(tt * shifted, axis=1, keepdims=True) * LN2
        T[t] = jnp.exp2(shifted) - tt

    WGP[...] = jnp.where(lane16 == 64, loss, 0.0)

    def back(i):
        for h in range(2):
            zz = zm(z + 4 - 2 * i - h)
            rows = pl.ds(pl.multiple_of(zz * 64, 64), 64)
            accs = []
            for cs in range(2):
                hb = HB[pl.ds(cs * 32 + zz * 4, 4)]
                hb = jnp.concatenate([hb, hb], axis=2)
                acc = jnp.zeros((4, 16, 128), F32)
                for t in range(8):
                    aff = AFF[t, cs, rows, :].reshape(4, 16, 256)
                    delta = T[t][None]
                    sg = jnp.where(aff > 0.0, delta * hb, 0.0)
                    top_row = h * 128 + cs * 64
                    SG[t, top_row:top_row + 64, :] = sg.reshape(64, 256).astype(BF)
                    prod = delta * jnp.maximum(aff, 0.0)
                    acc = acc + prod[:, :, 0:128] + prod[:, :, 128:256]
                accs.append(acc)
            acc = jnp.concatenate(accs, axis=0)
            got = jnp.sum(acc, axis=2, keepdims=True) * ISCALE
            wg = WGP[...]
            for n in range(8):
                cs, ys = n // 4, n % 4
                j = (ys // 2) * 32 + zz * 4 + (ys % 2) * 2 + cs
                wg = jnp.where(lane16 == j, got[n], wg)
            WGP[...] = wg
        total = jnp.zeros((256, 128), F32)
        for t in range(8):
            kt = IK1[2 * t:2 * t + 2] if t < 4 else IK2[t - 4]
            total = total + dot(SG[t], kt.reshape(256, 128))
        for h in range(2):
            zz = zm(z + 4 - 2 * i - h)
            part = total[h * 128:(h + 1) * 128].reshape(2, 4, 16, 128)
            RSB[pl.ds(zz * 2, 2)] = part.astype(BF)
            for cs in range(2):
                gg = zz * 2 + cs

                @pl.when(gg != g)
                def _():
                    rs_copy(gg, g).start()

    loop(0, 4, back)
    others(16, g, lambda gg: wg_copy(gg, g).start())
    WGR[g] = WGP[...]
    RSR[g] = RSB[g]

    mp_copy.wait_send()
    for h in range(2):
        ik_copy(h).wait_send()

    def k_sent(i):
        k_copy(0, i).wait_send()
        k_copy(1, i).wait_send()

    loop(0, 4, k_sent)
    for n in range(7):
        hop("a", n).wait_send()
        hop("b", n).wait_send()
    iqt_copy.wait_send()
    hwt_copy.wait_send()

    def twins(zz):
        to_twin(zz, "a").wait_send()
        to_twin(zz, "b").wait_send()

    loop(0, 8, twins)

    def w_sent(i):
        t, uu = i // 4, i % 4

        @pl.when(not_self(t, uu))
        def _():
            w_copy(t, uu, u).wait_send()

    loop(0, 8, w_sent)

    def x_sent(bb):
        hx_copy(bb, b).wait_send()
        for t in range(2):
            lx_copy(bb, t, b).wait_send()

    others(4, b, x_sent)
    others(4, y, lambda yy: hwy_copy(yy, y).wait_send())

    def g_sent(gg):
        st_copy(gg, g).wait_send()
        si_copy(gg, g).wait_send()

    others(16, g, g_sent)

    def z_sent(zz):
        iqz_copy(zz, z).wait_send()
        hwz_copy(zz, z).wait_send()

    others(8, z, z_sent)
    others(16, by, lambda n: pj_copy(n, by).wait_send())

    others(16, g, lambda gg: rs_copy(gg, gg).wait_recv())
    qg = RSR[0].astype(F32)
    for gg in range(1, 16):
        qg = qg + RSR[gg].astype(F32)
    DISP[...] = qg.astype(BF)
    others(16, by, lambda n: dq_copy(n, by).start())
    QGA[by] = DISP[y]

    others(16, by, lambda n: dq_copy(n, n).wait_recv())
    for t in range(2):
        o = dot(LTF[t].reshape(256, 192), QGA[...].reshape(256, 128), TN)
        OUTP[t] = o.astype(BF).reshape(4, 48, 128)
        for uu in range(4):

            @pl.when(not_self(t, uu))
            def _():
                o_copy(t, uu).start()

    @pl.when(b == 0)
    def _():
        out_q[:, out_cols(z, u, 1)] = OUTP[0, u]

    others(16, g, lambda gg: wg_copy(gg, gg).wait_recv())
    wg = WGR[0]
    for gg in range(1, 16):
        wg = wg + WGR[gg]
    WGS[...] = wg
    others(16, by, lambda n: dw_copy(n, by).start())
    WGA[by] = WGS[...]
    for t in range(2):
        for uu in range(4):

            @pl.when(not_self(t, uu))
            def _():
                o_arrival(t, uu).wait_recv()

        others(4, b, lambda bb: ox_copy(bb, t).start())

    others(4, b, lambda bb: hx_copy(bb, bb).wait_recv())
    others(16, by, lambda n: dw_copy(n, n).wait_recv())
    wg_all = WGA[...].reshape(256, 128)
    GWT[...] = dot(wg_all.astype(BF), HTX[...].reshape(256, hid_rows), TN)
    out_w[...] = GWT[pl.ds(pl.multiple_of(yh * 32, 32), 32), :]
    own = WGA[pl.ds(b * 4, 4)].reshape(64, 128)
    row = lax.broadcasted_iota(jnp.int32, (64, 128), 0)
    col = lax.broadcasted_iota(jnp.int32, (64, 128), 1)
    losses = jnp.where(natural(row) == col, own[:, 64:65], 0.0)
    out_l[...] = jnp.sum(losses, axis=0, keepdims=True)[:, 0:64]

    def g_left(gg):
        rs_copy(gg, g).wait_send()
        wg_copy(gg, g).wait_send()

    others(16, g, g_left)

    def by_left(n):
        dq_copy(n, by).wait_send()
        dw_copy(n, by).wait_send()

    others(16, by, by_left)
    for t in range(2):
        for uu in range(4):

            @pl.when(not_self(t, uu))
            def _():
                o_copy(t, uu).wait_send()

    for t in range(2):
        others(4, b, lambda bb: ox_arrival(bb, t).wait_recv())
    for t in range(2):
        others(4, b, lambda bb: ox_copy(bb, t).wait_send())


def widen(q_ref, w_ref, l_ref, out_q, out_w, out_l):
    out_q[...] = q_ref[...].astype(F32)
    out_w[...] = w_ref[...]
    out_l[...] = l_ref[...]


def per_device(
    q_latent, hidden, main_queries, main_keys, index_keys, positions, w_query, w_weights
):
    hid_rows = w_weights.shape[0]
    vm = pl.BlockSpec(memory_space=pltpu.VMEM)
    hbm = pl.BlockSpec(memory_space=pl.ANY)
    dma = pltpu.SemaphoreType.DMA
    sems = [dma((7,))]
    for n in (8, 16, 8, 4, 8, 1, 1, 1, 8, 8, 8, 8, 2, 8, 16, 16, 16, 16, 16, 16, 8, 4, 8, 8):
        sems += [dma((n,)), dma((n,))]
    out_q, out_w, out_l = pl.pallas_call(
        kernel,
        out_shape=(
            jax.ShapeDtypeStruct((48, 4096), BF),
            jax.ShapeDtypeStruct((32, hid_rows), F32),
            jax.ShapeDtypeStruct((1, 64), F32),
        ),
        in_specs=[pl.BlockSpec(memory_space=pltpu.SMEM)] + [hbm] * 7,
        out_specs=(vm, vm, vm),
        scratch_shapes=[
            pltpu.VMEM((64, 1536), BF),
            pltpu.VMEM((64, 384), BF),
            pltpu.VMEM((2, 64, DL), BF),
            pltpu.VMEM((2, 288, 128), BF),
            pltpu.VMEM((8, 256, DL), BF),
            pltpu.VMEM((DL, 1024), BF),
            pltpu.VMEM((8, 128, DI), BF),
            pltpu.VMEM((48, 4096), BF),
            pltpu.VMEM((32, hid_rows), BF),
            pltpu.VMEM((128, hid_rows), BF),
            pltpu.VMEM((8, 64, 192), BF),
            pltpu.VMEM((64, hid_rows), BF),
            pltpu.VMEM((2, 4, 64, 192), BF),
            pltpu.VMEM((4, 64, hid_rows), BF),
            pltpu.VMEM((2, 4, 48, 128), BF),
            pltpu.VMEM((16, 16, 128), F32),
            pltpu.VMEM((16, 16, 128), F32),
            pltpu.VMEM((4, 16, 128), BF),
            pltpu.VMEM((2, 8, 4, 16, 128), BF),
            pltpu.VMEM((4, 16, 128), F32),
            pltpu.VMEM((4, 16, 128), F32),
            pltpu.VMEM((8, 128), F32),
            pltpu.VMEM((8, 8, 128), F32),
            pltpu.VMEM((8, 128), F32),
            pltpu.VMEM((8, 128), F32),
            pltpu.VMEM((64, 16, 128), F32),
            pltpu.VMEM((8, 2, 2, 288, 128), BF),
            pltpu.VMEM((4, DL, 256), BF),
            pltpu.VMEM((4, 2, 128, DI), BF),
            pltpu.VMEM((16, 128, 2048), F32),
            pltpu.VMEM((128, 128), F32),
            pltpu.VMEM((128, 128), F32),
            pltpu.VMEM((128, 128), F32),
            pltpu.VMEM((16, 128), F32),
            pltpu.VMEM((16, 16, 128), F32),
            pltpu.VMEM((8, 128), F32),
            pltpu.VMEM((16, 8, 128), F32),
            pltpu.VMEM((8, 2, 512, 256), F32),
            pltpu.VMEM((8, 16, 256), F32),
            pltpu.VMEM((8, 16, 256), F32),
            pltpu.VMEM((8, 256, 256), BF),
            pltpu.VMEM((16, 4, 16, 128), BF),
            pltpu.VMEM((16, 4, 16, 128), BF),
            pltpu.VMEM((16, 128), F32),
            pltpu.VMEM((16, 16, 128), F32),
            pltpu.VMEM((4, 16, 128), BF),
            pltpu.VMEM((16, 16, 128), BF),
            pltpu.VMEM((16, 128), F32),
            pltpu.VMEM((16, 16, 128), F32),
            pltpu.VMEM((2, 4, 48, 128), BF),
            pltpu.VMEM((128, hid_rows), F32),
        ]
        + sems,
        compiler_params=pltpu.CompilerParams(
            collective_id=0, has_side_effects=True, vmem_limit_bytes=56 * 1024 * 1024
        ),
        name="indexer_step",
    )(
        positions, q_latent[0], hidden[0], main_queries[0], main_keys[0].T,
        index_keys[0].reshape(8, 128, DI), w_query, w_weights.T,
    )
    out_q, out_w, out_l = pl.pallas_call(
        widen,
        out_shape=(
            jax.ShapeDtypeStruct((48, 4096), F32),
            jax.ShapeDtypeStruct((32, hid_rows), F32),
            jax.ShapeDtypeStruct((1, 64), F32),
        ),
        in_specs=[vm] * 3,
        out_specs=(vm, vm, vm),
        name="widen",
    )(out_q, out_w, out_l)
    return out_q, out_w.T, out_l


def solution(mesh):
    return jax.shard_map(
        per_device,
        mesh=mesh,
        in_specs=(
            P("dp", None, None),
            P("dp", None, None),
            P("dp", "ctx", "head", None),
            P("dp", "ctx", None),
            P("dp", "ctx", None),
            P("dp", None),
            P("ctx", "head"),
            P("ctx", "head"),
        ),
        out_specs=(P("ctx", "head"), P("ctx", "head"), P("dp", None)),
        check_vma=False,
    )
```

```python
import jax
import jax.numpy as jnp
from jax import lax
from jax.experimental import pallas as pl
from jax.experimental.pallas import tpu as pltpu
from jax.sharding import PartitionSpec as P

HI = 64
DI = 128
HM = 128
DL = 576
MESH = pl.DeviceIdType.MESH
BF = jnp.bfloat16
F32 = jnp.float32

LOG2E = 1.4426950408889634
LN2 = 0.6931471805599453
C2 = 192.0 ** (-0.5) * LOG2E
ISCALE = (HI * DI) ** (-0.5)
FLOOR = -1e30
LOW = -1e29

NT = (((1,), (1,)), ((), ()))
NN = (((1,), (0,)), ((), ()))
TN = (((0,), (0,)), ((), ()))


def dot(a, b, dims=NN):
    return lax.dot_general(a, b, dims, preferred_element_type=F32)


def log2(x):
    return jnp.log(x) * LOG2E


def remote(src, dst, ss, rs, dev):
    return pltpu.make_async_remote_copy(
        src_ref=src, dst_ref=dst, send_sem=ss, recv_sem=rs, device_id=dev, device_id_type=MESH
    )


def loop(lo, hi, body):
    def turn(i, carry):
        body(i)
        return carry

    lax.fori_loop(lo, hi, turn, 0)


def kernel(
    pos_s, lat_h, hid_h, mq_h, mk_h, ik_h, wq_h, ww_h,
    out_q, out_w, out_l,
    LATN, HIDW, MQL, PK, QS, K1, IK1, WQ, WWT, WWF, LAT8, HID, LTF, HTX, WB, PJ, IQP, IQY, IQG,
    HWL, HWY, HWS, HWG, HWC, HWT, HB, MQ, K2, IK2, E, MA, LA, MS, ST, STG, SI, SIG, AFF, LM, T, SG,
    RSB, RSR, WGP, WGR, DISP, QGA, WGS, WGA, OUTP, GWT,
    s_in,
    s_w, r_w, s_pj, r_pj, s_iqg, r_iqg, s_hwy, r_hwy, s_hwg, r_hwg,
    s_iqt, r_iqt, s_hwt, r_hwt, s_mp, r_mp, s_qa, r_qa, s_qb, r_qb, s_ca, r_ca, s_cb, r_cb,
    s_ik, r_ik, s_k, r_k, s_st, r_st, s_si, r_si, s_rs, r_rs, s_wg, r_wg, s_dq, r_dq, s_dw, r_dw,
    s_lx, r_lx, s_hx, r_hx, s_o, r_o, s_ox, r_ox,
):
    b = lax.axis_index("dp")
    yh = lax.axis_index("head")
    c = lax.axis_index("ctx")
    z = c // 4
    yl = (c // 2) % 2
    core = c % 2
    y = yh * 2 + yl
    u = yl * 2 + core
    g = z * 2 + core
    by = b * 4 + y
    hid_rows = ww_h.shape[1]

    hid_tile = jnp.minimum((c * hid_rows) // 128, 53)
    hid_rest = c * hid_rows - hid_tile * 128
    loads = [
        pltpu.make_async_copy(lat_h, LATN, s_in.at[0]),
        pltpu.make_async_copy(
            hid_h.at[:, pl.ds(pl.multiple_of(hid_tile * 128, 128), 384)], HIDW, s_in.at[1]
        ),
        pltpu.make_async_copy(ww_h, WWT, s_in.at[2]),
        pltpu.make_async_copy(wq_h, WQ, s_in.at[3]),
        pltpu.make_async_copy(mq_h, MQL, s_in.at[4]),
        pltpu.make_async_copy(mk_h, K1, s_in.at[5]),
        pltpu.make_async_copy(ik_h, IK1, s_in.at[6]),
    ]
    def g_dev(gg):
        return {"dp": b, "head": yh, "ctx": (gg // 2) * 4 + yl * 2 + gg % 2}

    def y_dev(yy):
        return {"dp": b, "head": yy // 2, "ctx": z * 4 + (yy % 2) * 2 + core}

    def x_dev(bb):
        return {"dp": bb, "head": yh, "ctx": c}

    def by_dev(n):
        yy = n % 4
        return {"dp": n // 4, "head": yy // 2, "ctx": z * 4 + (yy % 2) * 2 + core}

    def a_dev(zz, uu):
        return {"dp": b, "head": yh, "ctx": zz * 4 + uu}

    def zm(v):
        return lax.rem(v + 16, 8)

    def others(n, me, start):
        def turn(i):
            d = n // 2 + jnp.where(lax.rem(i, 2) == 1, (i + 1) // 2, -(i // 2))
            start(lax.rem(me + d, n))

        loop(0, n - 1, turn)

    bar = pltpu.get_barrier_semaphore()

    def hello(dev):
        pl.semaphore_signal(bar, inc=1, device_id=dev, device_id_type=MESH)

    others(16, g, lambda gg: hello(g_dev(gg)))
    others(16, by, lambda n: hello(by_dev(n)))

    def not_self(t, uu):
        return jnp.logical_or(b > 0, jnp.logical_or(t > 0, uu != u))

    def hello_a(i):
        t, uu = i // 4, i % 4

        @pl.when(not_self(t, uu))
        def _():
            hello(a_dev(zm(z - b - 4 * t), uu))
            hello(a_dev(zm(z + b + 4 * t), uu))

    loop(0, 8, hello_a)
    for one in loads:
        one.start()

    row64 = lax.broadcasted_iota(jnp.int32, (64, 64), 0)
    col64 = lax.broadcasted_iota(jnp.int32, (64, 64), 1)

    def natural(r):
        return ((r >> 1) & 7) * 8 + ((r >> 4) & 1) * 4 + (r & 1) * 2 + (r >> 5)

    perm = jnp.where(natural(row64) == col64, 1.0, 0.0).astype(BF)
    WWF[...] = jnp.zeros_like(WWF)
    loads[0].wait()
    lat = dot(perm, LATN[...]).astype(BF)
    for p in range(8):
        LAT8[p] = lat[:, p * 192:(p + 1) * 192]
    loads[1].wait()
    loads[2].wait()
    WWF[pl.ds(pl.multiple_of(yh * 32, 32), 32), :] = WWT[...]
    sel_row = lax.broadcasted_iota(jnp.int32, (384, hid_rows), 0)
    sel_col = lax.broadcasted_iota(jnp.int32, (384, hid_rows), 1)
    sel = jnp.where(sel_row == sel_col + hid_rest, 1.0, 0.0).astype(BF)
    HID[...] = dot(perm, dot(HIDW[...], sel).astype(BF)).astype(BF)
    HWL[...] = dot(HID[...], WWF[...], NT).reshape(4, 16, 128)
    for one in loads[3:]:
        one.wait()
    for n in range(2):
        x = MQL[n]
        for p in range(4):
            PK[n, p * 64:(p + 1) * 64] = x[:, p * 128:(p + 1) * 128]
        PK[n, 256:288] = jnp.concatenate([x[0:32, 512:576], x[32:64, 512:576]], axis=1)
    pl.semaphore_wait(bar, jnp.where(b == 0, 44, 46))

    def w_copy(t, uu, slot):
        zd = zm(z - b - 4 * t)
        cols = pl.ds(pl.multiple_of((zd * 4 + uu) * 128, 128), 128)
        return remote(
            WQ.at[:, cols], WB.at[t, u], s_w.at[t * 4 + uu], r_w.at[t * 4 + slot], a_dev(zd, uu)
        )

    def pj_copy(n, slot):
        return remote(PJ.at[n], IQP.at[slot], s_pj.at[n], r_pj.at[slot], by_dev(n))

    def iqz_copy(zz, slot):
        return remote(IQY, IQG.at[core, slot], s_iqg.at[zz], r_iqg.at[slot], a_dev(zz, u))

    def hwz_copy(zz, slot):
        return remote(HWS, HWG.at[slot], s_hwg.at[zz], r_hwg.at[slot], a_dev(zz, u))

    def hwy_copy(yy, slot):
        return remote(HWL.at[yy], HWY.at[slot], s_hwy.at[yy], r_hwy.at[slot], y_dev(yy))

    def st_copy(gg, slot):
        return remote(ST, STG.at[slot], s_st.at[gg], r_st.at[slot], g_dev(gg))

    def si_copy(gg, slot):
        return remote(SI, SIG.at[slot], s_si.at[gg], r_si.at[slot], g_dev(gg))

    def rs_copy(gg, slot):
        return remote(RSB.at[gg], RSR.at[slot], s_rs.at[gg], r_rs.at[slot], g_dev(gg))

    def wg_copy(gg, slot):
        return remote(WGP, WGR.at[slot], s_wg.at[gg], r_wg.at[slot], g_dev(gg))

    def dq_copy(n, slot):
        return remote(DISP.at[n % 4], QGA.at[slot], s_dq.at[n], r_dq.at[slot], by_dev(n))

    def dw_copy(n, slot):
        return remote(WGS, WGA.at[slot], s_dw.at[n], r_dw.at[slot], by_dev(n))

    def lx_copy(bb, t, slot):
        return remote(
            LAT8.at[zm(z + bb + 4 * t)], LTF.at[t, slot],
            s_lx.at[bb * 2 + t], r_lx.at[slot * 2 + t], x_dev(bb),
        )

    def hx_copy(bb, slot):
        return remote(HID, HTX.at[slot], s_hx.at[bb], r_hx.at[slot], x_dev(bb))

    def out_cols(zz, uu, n):
        return pl.ds(pl.multiple_of((zz * 4 + uu) * 128, 128), n * 128)

    def o_copy(t, uu):
        return remote(
            OUTP.at[t, uu], out_q.at[:, out_cols(z, u, 1)], s_o.at[t * 4 + uu], r_o.at[t * 4 + u],
            a_dev(zm(z + b + 4 * t), uu),
        )

    def o_arrival(t, uu):
        zz = zm(z - b - 4 * t)
        return remote(
            OUTP.at[t, uu], out_q.at[:, out_cols(zz, uu, 1)], s_o.at[t * 4 + uu],
            r_o.at[t * 4 + uu], a_dev(zz, uu),
        )

    def ox_copy(bb, t):
        cols = out_cols(zm(z - b - 4 * t), 0, 4)
        return remote(
            out_q.at[:, cols], out_q.at[:, cols], s_ox.at[bb * 2 + t], r_ox.at[b * 2 + t], x_dev(bb)
        )

    def ox_arrival(bb, t):
        cols = out_cols(zm(z - bb - 4 * t), 0, 4)
        return remote(
            out_q.at[:, cols], out_q.at[:, cols], s_ox.at[bb * 2 + t], r_ox.at[bb * 2 + t], x_dev(bb)
        )

    twin = {"dp": b, "head": yh, "ctx": z * 4 + yl * 2 + (1 - core)}
    iqt_copy = remote(IQG.at[core], IQG.at[core], s_iqt.at[0], r_iqt.at[0], twin)
    hwt_copy = remote(HWC, HWT, s_hwt.at[0], r_hwt.at[0], twin)
    hops = {
        "a": ((0, 2), (0, -2), (0, 1), (0, -1), (-2, 1), (2, -1), (-3, 1)),
        "b": ((0, 2), (0, -2), (0, 1), (0, -1), (-2, 1), (2, -1), (2, -2)),
    }

    places = {0: 0, 1: 1, -1: 2, 2: 3, -2: 4, 3: 5, -3: 6, 4: 7, -4: 7}

    def piece(of, kind):
        return MQ.at[places[of], core, yh if kind == "a" else 1 - yh]

    def hop(kind, n):
        of, far_by = hops[kind][n]
        ss, rs = (s_qa, r_qa) if kind == "a" else (s_qb, r_qb)
        there = of - far_by
        return remote(
            piece(of, kind), piece(there, kind), ss.at[n], rs.at[places[there]],
            a_dev(zm(z + far_by), u),
        )

    def arrival(kind, of):
        ss, rs = (s_qa, r_qa) if kind == "a" else (s_qb, r_qb)
        here = piece(of, kind)
        remote(here, here, ss.at[0], rs.at[places[of]], a_dev(zm(z + of), u)).wait_recv()
        to_twin(places[of], kind).start()

    def to_twin(k, kind):
        ss, rs = (s_ca, r_ca) if kind == "a" else (s_cb, r_cb)
        here = MQ.at[k, core, yh if kind == "a" else 1 - yh]
        return remote(here, here, ss.at[k], rs.at[k], twin)

    partner = {"dp": b, "head": 1 - yh, "ctx": c}
    mp_copy = remote(PK.at[1 - yh], MQ.at[0, core, yh], s_mp.at[0], r_mp.at[0], partner)
    up = y_dev(lax.rem(y + 1, 4))
    down = y_dev(lax.rem(y + 3, 4))

    def ik_copy(h):
        return remote(
            IK1.at[h * 4:(h + 1) * 4], IK2.at[:, h], s_ik.at[h], r_ik.at[h], down if h else up
        )

    def k_copy(h, i):
        return remote(
            K1.at[:, pl.ds(pl.multiple_of(h * 512 + i * 128, 128), 128)],
            K2.at[i, :, h * 128:(h + 1) * 128],
            s_k.at[h * 4 + i], r_k.at[h * 4 + i], down if h else up,
        )

    def w_start(i):
        t, uu = i // 4, i % 4

        @pl.when(not_self(t, uu))
        def _():
            w_copy(t, uu, u).start()

    mp_copy.start()
    loop(0, 8, w_start)
    others(4, b, lambda bb: [lx_copy(bb, t, b).start() for t in range(2)])
    MQ[0, core, yh] = PK[yh]
    for n in range(4):
        hop("a", n).start()
    to_twin(0, "a").start()
    others(4, y, lambda yy: hwy_copy(yy, y).start())

    def k_start(i):
        k_copy(0, i).start()
        k_copy(1, i).start()

    k_start(0)
    k_start(1)
    HWY[y] = HWL[y]

    @pl.when(b == 0)
    def _():
        WB[0, u] = WQ[:, pl.ds(pl.multiple_of(c * 128, 128), 128)]

    for t in range(2):
        LTF[t, b] = LAT8[zm(z + b + 4 * t)]
    HTX[b] = HID[...]
    MA[...] = jnp.zeros_like(MA)
    LA[...] = jnp.zeros_like(LA)

    mp_copy.wait_recv()
    for n in range(4):
        hop("b", n).start()
    to_twin(0, "b").start()

    lane = lax.broadcasted_iota(jnp.int32, (128, 128), 1)
    near_row = lax.broadcasted_iota(jnp.int32, (1, 1024), 1) + c * 1024
    col256 = lax.broadcasted_iota(jnp.int32, (1, 256), 1)
    far_row = (z * 4 + (1 - yl) * 2 + core) * 1024 + (col256 >> 7) * 512 + (col256 & 127)

    def position(slot):
        return pos_s[0, (slot // 2) * 8 + (slot % 2) * 2 + 4 * yl + yh]

    def plane(k):
        return zm(z + jnp.where(lax.rem(k, 2) == 1, (k + 1) // 2, -(k // 2)))

    def scores(k, count, keys, key_row, part, cols):
        q = QS[pl.ds(k, count)].reshape(count * 256, DL)
        s = dot(q, keys)
        ma, la = MA[...], LA[...]
        for i in range(count * 2):
            slot = plane(k + i // 2) * 2 + i % 2
            vis = key_row <= position(slot)
            si = jnp.where(vis, s[i * 128:(i + 1) * 128], FLOOR)
            m = jnp.maximum(jnp.max(si, axis=1, keepdims=True), LOW)
            e = jnp.exp2((si - m) * C2)
            E[slot, :, cols] = e
            here = lane == part * 16 + slot
            ma = jnp.where(here, m, ma)
            la = jnp.where(here, jnp.sum(e, axis=1, keepdims=True), la)
        MA[...] = ma
        LA[...] = la

    def near(k, count):
        for i in range(k, k + count):
            to_twin(i, "a").wait_recv()
            to_twin(i, "b").wait_recv()
            for n in range(4):
                x = MQ[i, n // 2, n % 2]
                rows = slice(n * 64, (n + 1) * 64)
                for p in range(4):
                    QS[i, rows, p * 128:(p + 1) * 128] = x[p * 64:(p + 1) * 64]
                rest = jnp.concatenate([x[256:288, 0:64], x[256:288, 64:128]], axis=0)
                QS[i, rows, 512:576] = rest
        scores(k, count, K1[...], near_row, 0, pl.ds(0, 1024))

    def w_wait(i):
        t, uu = i // 4, i % 4

        @pl.when(not_self(t, uu))
        def _():
            w_copy(t, uu, uu).wait_recv()

    loop(0, 8, w_wait)
    others(4, b, lambda bb: [lx_copy(bb, t, bb).wait_recv() for t in range(2)])
    PJ[...] = (
        dot(LTF[0].reshape(256, 192), WB[0].reshape(192, 128))
        + dot(LTF[1].reshape(256, 192), WB[1].reshape(192, 128))
    ).reshape(16, 16, 128)
    others(16, by, lambda n: pj_copy(n, by).start())
    k_start(2)
    k_start(3)
    for h in range(2):
        ik_copy(h).start()
    IQP[by] = PJ[by]

    for of, n in ((-2, 4), (2, 5)):
        arrival("a", of)
        hop("a", n).start()
    arrival("a", -1)
    arrival("a", 1)
    others(4, y, lambda yy: hwy_copy(yy, yy).wait_recv())
    hw = HWY[0] + HWY[1] + HWY[2] + HWY[3]
    HWS[...] = jnp.concatenate([hw[0:8, 0:64], hw[8:16, 0:64]], axis=1)
    others(8, z, lambda zz: hwz_copy(zz, z).start())
    HWG[z] = HWS[...]
    others(4, b, lambda bb: hx_copy(bb, b).start())
    near(0, 1)
    for of, n in ((-2, 4), (2, 5)):
        arrival("b", of)
        hop("b", n).start()
        if of == 2:
            hop("b", 6).start()
    arrival("b", -1)
    arrival("b", 1)
    others(16, by, lambda n: pj_copy(n, n).wait_recv())
    for ys in range(4):
        IQY[ys] = (IQP[ys] + IQP[4 + ys] + IQP[8 + ys] + IQP[12 + ys]).astype(BF)
    others(8, z, lambda zz: iqz_copy(zz, z).start())
    IQG[core, z] = IQY[...]
    arrival("a", -3)
    hop("a", 6).start()

    near(1, 4)

    def far(i, k, count):
        cols = pl.ds(pl.multiple_of(1024 + i * 256, 256), 256)
        scores(k, count, K2[i], far_row + i * 128, 1 + i, cols)

    def far_early(i):
        k_copy(0, i).wait_recv()
        k_copy(1, i).wait_recv()
        far(i, 0, 5)

    loop(0, 4, far_early)
    for kind, of in (("a", 3), ("a", 4), ("b", -3), ("b", 3), ("b", 4)):
        arrival(kind, of)
    others(8, z, lambda zz: hwz_copy(zz, zz).wait_recv())
    hw = HWG[0]
    for zz in range(1, 8):
        hw = hw + HWG[zz]
    HWC[...] = hw
    hwt_copy.start()
    others(8, z, lambda zz: iqz_copy(zz, zz).wait_recv())
    iqt_copy.start()
    near(5, 3)
    loop(0, 4, lambda i: far(i, 5, 3))
    MS[...] = MA[...].T
    sums = LA[...].T
    tops = [MS[16 * p:16 * (p + 1)] for p in range(5)]
    mx = tops[0]
    for p in range(1, 5):
        mx = jnp.maximum(mx, tops[p])
    total = jnp.zeros((16, 128), F32)
    for p in range(5):
        total = total + sums[16 * p:16 * (p + 1)] * jnp.exp2((tops[p] - mx) * C2)
    ST[...] = mx * C2 + log2(jnp.maximum(total, 1e-37))
    others(16, g, lambda gg: st_copy(gg, g).start())
    STG[g] = ST[...]

    hwt_copy.wait_recv()
    hw = (HWC[...] + HWT[...]) * ISCALE
    hw = jnp.concatenate([hw[:, 0:64], hw[:, 64:128]], axis=0)
    for p in range(64):
        cs, zs, ys = p // 32, (p // 4) % 8, p % 4
        j = (ys // 2) * 32 + zs * 4 + (ys % 2) * 2 + cs
        HB[p] = jnp.broadcast_to(hw[:, j:j + 1], (16, 128))
    sub256 = lax.broadcasted_iota(jnp.int32, (16, 256), 0)
    posq = jnp.zeros((16, 256), jnp.int32)
    for slot in range(16):
        posq = jnp.where(sub256 == slot, position(slot), posq)
    iqt_copy.wait_recv()
    for h in range(2):
        ik_copy(h).wait_recv()

    def index_tile(kt, tile, key_row):
        aff = dot(IQG[...].reshape(1024, 128), kt.reshape(256, 128), NT)
        AFF[tile] = aff.reshape(2, 512, 256)
        total = jnp.zeros((16, 256), F32)
        for p in range(64):
            hb = HB[p]
            total = total + jnp.maximum(aff[p * 16:(p + 1) * 16], 0.0) * jnp.concatenate([hb, hb], axis=1)
        LM[tile] = jnp.where(key_row <= posq, total * LOG2E, FLOOR)

    loop(0, 4, lambda i: index_tile(IK1[pl.ds(i * 2, 2)], i, col256 + (c * 1024 + i * 256)))
    loop(0, 4, lambda i: index_tile(IK2[i], i + 4, far_row + i * 128))
    lm = LM[...]
    im = jnp.maximum(jnp.max(jnp.max(lm, axis=0), axis=1, keepdims=True), LOW)
    il = jnp.sum(jnp.sum(jnp.exp2(lm - im[None]), axis=0), axis=1, keepdims=True)
    lane16 = lax.broadcasted_iota(jnp.int32, (16, 128), 1)
    diag = lane16 == lax.broadcasted_iota(jnp.int32, (16, 128), 0)
    il = im + log2(jnp.maximum(il, 1e-37))
    SI[...] = jnp.broadcast_to(jnp.sum(jnp.where(diag, il, 0.0), axis=0, keepdims=True), (8, 128))
    others(16, g, lambda gg: si_copy(gg, g).start())
    SIG[g] = SI[...]

    others(16, g, lambda gg: st_copy(gg, gg).wait_recv())
    stats = STG[...]
    top = jnp.max(stats, axis=0)
    lse = top + log2(jnp.sum(jnp.exp2(stats - top[None]), axis=0))
    weights = [jnp.exp2(MS[16 * p:16 * (p + 1)] * C2 - lse) * (1.0 / HM) for p in range(5)]
    MA[...] = jnp.concatenate(weights + [jnp.zeros((48, 128), F32)], axis=0).T

    def target(slot):
        for p in range(5):
            w = jnp.sum(jnp.where(lane == p * 16 + slot, MA[...], 0.0), axis=1, keepdims=True)
            lo, hi = (0, 1024) if p == 0 else (768 + 256 * p, 1024 + 256 * p)
            row = jnp.sum(E[slot, :, lo:hi] * w, axis=0, keepdims=True)
            for t in range(lo // 256, hi // 256):
                T[t, pl.ds(slot, 1), :] = row[:, t * 256 - lo:t * 256 - lo + 256]

    loop(0, 4, lambda i: [target(4 * i + j) for j in range(4)])
    others(16, g, lambda gg: si_copy(gg, gg).wait_recv())
    istats = SIG[...]
    itop = jnp.max(istats, axis=0)
    li = (itop + log2(jnp.sum(jnp.exp2(istats - itop[None]), axis=0)))[0:1]
    li = jnp.sum(jnp.where(diag, li, 0.0), axis=1, keepdims=True)
    loss = jnp.zeros((16, 1), F32)
    for t in range(8):
        shifted = LM[t] - li
        tt = T[t]
        loss = loss - jnp.sum(tt * shifted, axis=1, keepdims=True) * LN2
        T[t] = jnp.exp2(shifted) - tt

    WGP[...] = jnp.where(lane16 == 64, loss, 0.0)

    def back(i):
        for h in range(2):
            zz = zm(z + 4 - 2 * i - h)
            rows = pl.ds(pl.multiple_of(zz * 64, 64), 64)
            accs = []
            for cs in range(2):
                hb = HB[pl.ds(cs * 32 + zz * 4, 4)]
                hb = jnp.concatenate([hb, hb], axis=2)
                acc = jnp.zeros((4, 16, 128), F32)
                for t in range(8):
                    aff = AFF[t, cs, rows, :].reshape(4, 16, 256)
                    delta = T[t][None]
                    sg = jnp.where(aff > 0.0, delta * hb, 0.0)
                    top_row = h * 128 + cs * 64
                    SG[t, top_row:top_row + 64, :] = sg.reshape(64, 256).astype(BF)
                    prod = delta * jnp.maximum(aff, 0.0)
                    acc = acc + prod[:, :, 0:128] + prod[:, :, 128:256]
                accs.append(acc)
            acc = jnp.concatenate(accs, axis=0)
            got = jnp.sum(acc, axis=2, keepdims=True) * ISCALE
            wg = WGP[...]
            for n in range(8):
                cs, ys = n // 4, n % 4
                j = (ys // 2) * 32 + zz * 4 + (ys % 2) * 2 + cs
                wg = jnp.where(lane16 == j, got[n], wg)
            WGP[...] = wg
        total = jnp.zeros((256, 128), F32)
        for t in range(8):
            kt = IK1[2 * t:2 * t + 2] if t < 4 else IK2[t - 4]
            total = total + dot(SG[t], kt.reshape(256, 128))
        for h in range(2):
            zz = zm(z + 4 - 2 * i - h)
            part = total[h * 128:(h + 1) * 128].reshape(2, 4, 16, 128)
            RSB[pl.ds(zz * 2, 2)] = part.astype(BF)
            for cs in range(2):
                gg = zz * 2 + cs

                @pl.when(gg != g)
                def _():
                    rs_copy(gg, g).start()

    loop(0, 4, back)
    others(16, g, lambda gg: wg_copy(gg, g).start())
    WGR[g] = WGP[...]
    RSR[g] = RSB[g]

    mp_copy.wait_send()
    for h in range(2):
        ik_copy(h).wait_send()

    def k_sent(i):
        k_copy(0, i).wait_send()
        k_copy(1, i).wait_send()

    loop(0, 4, k_sent)
    for n in range(7):
        hop("a", n).wait_send()
        hop("b", n).wait_send()
    iqt_copy.wait_send()
    hwt_copy.wait_send()

    def twins(zz):
        to_twin(zz, "a").wait_send()
        to_twin(zz, "b").wait_send()

    loop(0, 8, twins)

    def w_sent(i):
        t, uu = i // 4, i % 4

        @pl.when(not_self(t, uu))
        def _():
            w_copy(t, uu, u).wait_send()

    loop(0, 8, w_sent)

    def x_sent(bb):
        hx_copy(bb, b).wait_send()
        for t in range(2):
            lx_copy(bb, t, b).wait_send()

    others(4, b, x_sent)
    others(4, y, lambda yy: hwy_copy(yy, y).wait_send())

    def g_sent(gg):
        st_copy(gg, g).wait_send()
        si_copy(gg, g).wait_send()

    others(16, g, g_sent)

    def z_sent(zz):
        iqz_copy(zz, z).wait_send()
        hwz_copy(zz, z).wait_send()

    others(8, z, z_sent)
    others(16, by, lambda n: pj_copy(n, by).wait_send())

    others(16, g, lambda gg: rs_copy(gg, gg).wait_recv())
    qg = RSR[0].astype(F32)
    for gg in range(1, 16):
        qg = qg + RSR[gg].astype(F32)
    DISP[...] = qg.astype(BF)
    others(16, by, lambda n: dq_copy(n, by).start())
    QGA[by] = DISP[y]

    others(16, by, lambda n: dq_copy(n, n).wait_recv())
    for t in range(2):
        o = dot(LTF[t].reshape(256, 192), QGA[...].reshape(256, 128), TN)
        OUTP[t] = o.astype(BF).reshape(4, 48, 128)
        for uu in range(4):

            @pl.when(not_self(t, uu))
            def _():
                o_copy(t, uu).start()

    @pl.when(b == 0)
    def _():
        out_q[:, out_cols(z, u, 1)] = OUTP[0, u]

    others(16, g, lambda gg: wg_copy(gg, gg).wait_recv())
    wg = WGR[0]
    for gg in range(1, 16):
        wg = wg + WGR[gg]
    WGS[...] = wg
    others(16, by, lambda n: dw_copy(n, by).start())
    WGA[by] = WGS[...]
    for t in range(2):
        for uu in range(4):

            @pl.when(not_self(t, uu))
            def _():
                o_arrival(t, uu).wait_recv()

        others(4, b, lambda bb: ox_copy(bb, t).start())

    others(4, b, lambda bb: hx_copy(bb, bb).wait_recv())
    others(16, by, lambda n: dw_copy(n, n).wait_recv())
    wg_all = WGA[...].reshape(256, 128)
    GWT[...] = dot(wg_all.astype(BF), HTX[...].reshape(256, hid_rows), TN)
    out_w[...] = GWT[pl.ds(pl.multiple_of(yh * 32, 32), 32), :]
    own = WGA[pl.ds(b * 4, 4)].reshape(64, 128)
    row = lax.broadcasted_iota(jnp.int32, (64, 128), 0)
    col = lax.broadcasted_iota(jnp.int32, (64, 128), 1)
    losses = jnp.where(natural(row) == col, own[:, 64:65], 0.0)
    out_l[...] = jnp.sum(losses, axis=0, keepdims=True)[:, 0:64]

    def g_left(gg):
        rs_copy(gg, g).wait_send()
        wg_copy(gg, g).wait_send()

    others(16, g, g_left)

    def by_left(n):
        dq_copy(n, by).wait_send()
        dw_copy(n, by).wait_send()

    others(16, by, by_left)
    for t in range(2):
        for uu in range(4):

            @pl.when(not_self(t, uu))
            def _():
                o_copy(t, uu).wait_send()

    for t in range(2):
        others(4, b, lambda bb: ox_arrival(bb, t).wait_recv())
    for t in range(2):
        others(4, b, lambda bb: ox_copy(bb, t).wait_send())


def widen(q_ref, w_ref, l_ref, out_q, out_w, out_l):
    out_q[...] = q_ref[...].astype(F32)
    out_w[...] = w_ref[...]
    out_l[...] = l_ref[...]


def per_device(
    q_latent, hidden, main_queries, main_keys, index_keys, positions, w_query, w_weights
):
    hid_rows = w_weights.shape[0]
    vm = pl.BlockSpec(memory_space=pltpu.VMEM)
    hbm = pl.BlockSpec(memory_space=pl.ANY)
    dma = pltpu.SemaphoreType.DMA
    sems = [dma((7,))]
    for n in (8, 16, 8, 4, 8, 1, 1, 1, 8, 8, 8, 8, 2, 8, 16, 16, 16, 16, 16, 16, 8, 4, 8, 8):
        sems += [dma((n,)), dma((n,))]
    out_q, out_w, out_l = pl.pallas_call(
        kernel,
        out_shape=(
            jax.ShapeDtypeStruct((48, 4096), BF),
            jax.ShapeDtypeStruct((32, hid_rows), F32),
            jax.ShapeDtypeStruct((1, 64), F32),
        ),
        in_specs=[pl.BlockSpec(memory_space=pltpu.SMEM)] + [hbm] * 7,
        out_specs=(vm, vm, vm),
        scratch_shapes=[
            pltpu.VMEM((64, 1536), BF),
            pltpu.VMEM((64, 384), BF),
            pltpu.VMEM((2, 64, DL), BF),
            pltpu.VMEM((2, 288, 128), BF),
            pltpu.VMEM((8, 256, DL), BF),
            pltpu.VMEM((DL, 1024), BF),
            pltpu.VMEM((8, 128, DI), BF),
            pltpu.VMEM((48, 4096), BF),
            pltpu.VMEM((32, hid_rows), BF),
            pltpu.VMEM((128, hid_rows), BF),
            pltpu.VMEM((8, 64, 192), BF),
            pltpu.VMEM((64, hid_rows), BF),
            pltpu.VMEM((2, 4, 64, 192), BF),
            pltpu.VMEM((4, 64, hid_rows), BF),
            pltpu.VMEM((2, 4, 48, 128), BF),
            pltpu.VMEM((16, 16, 128), F32),
            pltpu.VMEM((16, 16, 128), F32),
            pltpu.VMEM((4, 16, 128), BF),
            pltpu.VMEM((2, 8, 4, 16, 128), BF),
            pltpu.VMEM((4, 16, 128), F32),
            pltpu.VMEM((4, 16, 128), F32),
            pltpu.VMEM((8, 128), F32),
            pltpu.VMEM((8, 8, 128), F32),
            pltpu.VMEM((8, 128), F32),
            pltpu.VMEM((8, 128), F32),
            pltpu.VMEM((64, 16, 128), F32),
            pltpu.VMEM((8, 2, 2, 288, 128), BF),
            pltpu.VMEM((4, DL, 256), BF),
            pltpu.VMEM((4, 2, 128, DI), BF),
            pltpu.VMEM((16, 128, 2048), F32),
            pltpu.VMEM((128, 128), F32),
            pltpu.VMEM((128, 128), F32),
            pltpu.VMEM((128, 128), F32),
            pltpu.VMEM((16, 128), F32),
            pltpu.VMEM((16, 16, 128), F32),
            pltpu.VMEM((8, 128), F32),
            pltpu.VMEM((16, 8, 128), F32),
            pltpu.VMEM((8, 2, 512, 256), F32),
            pltpu.VMEM((8, 16, 256), F32),
            pltpu.VMEM((8, 16, 256), F32),
            pltpu.VMEM((8, 256, 256), BF),
            pltpu.VMEM((16, 4, 16, 128), BF),
            pltpu.VMEM((16, 4, 16, 128), BF),
            pltpu.VMEM((16, 128), F32),
            pltpu.VMEM((16, 16, 128), F32),
            pltpu.VMEM((4, 16, 128), BF),
            pltpu.VMEM((16, 16, 128), BF),
            pltpu.VMEM((16, 128), F32),
            pltpu.VMEM((16, 16, 128), F32),
            pltpu.VMEM((2, 4, 48, 128), BF),
            pltpu.VMEM((128, hid_rows), F32),
        ]
        + sems,
        compiler_params=pltpu.CompilerParams(
            collective_id=0, has_side_effects=True, vmem_limit_bytes=56 * 1024 * 1024
        ),
        name="indexer_step",
    )(
        positions, q_latent[0], hidden[0], main_queries[0], main_keys[0].T,
        index_keys[0].reshape(8, 128, DI), w_query, w_weights.T,
    )
    out_q, out_w, out_l = pl.pallas_call(
        widen,
        out_shape=(
            jax.ShapeDtypeStruct((48, 4096), F32),
            jax.ShapeDtypeStruct((32, hid_rows), F32),
            jax.ShapeDtypeStruct((1, 64), F32),
        ),
        in_specs=[vm] * 3,
        out_specs=(vm, vm, vm),
        name="widen",
    )(out_q, out_w, out_l)
    return out_q, out_w.T, out_l


def solution(mesh):
    return jax.shard_map(
        per_device,
        mesh=mesh,
        in_specs=(
            P("dp", None, None),
            P("dp", None, None),
            P("dp", "ctx", "head", None),
            P("dp", "ctx", None),
            P("dp", "ctx", None),
            P("dp", None),
            P("ctx", "head"),
            P("ctx", "head"),
        ),
        out_specs=(P("ctx", "head"), P("ctx", "head"), P("dp", None)),
        check_vma=False,
    )
```
